32 devices in a mesh: gx: 8 (over z, core), gy: 4 (over y, x).
Axes of the slice: x: 2, y: 2, z: 4, core: 2. Of those that a mesh axis runs over, the one named last changes fastest.
Arguments:
- offset: float32 [3, 768, 128], P(None, ('gx', 'gy')), may hold values from 0.5 to 1.5
- particle_mass: float32 [768, 128], P(('gx', 'gy')), may hold values from 0.5 to 2
- velocity: float32 [3, 768, 128], P(None, ('gx', 'gy')), may hold values from -6 to 6
- affine: float32 [9, 768, 128], P(None, ('gx', 'gy')), may hold values from -3 to 3
- deform: float32 [9, 768, 128], P(None, ('gx', 'gy')), may hold values from -0.3 to 1.3, as said below
- particle_cell: int32 [768, 128], P(('gx', 'gy')), may hold values from 0 to 127
- body_id: int32 [768, 128], P(('gx', 'gy')), may hold values from 0 to 63
- slot_tile_number: int32 [768], P(('gx', 'gy')), may hold values from 0 to 127, as said below
- block_count: int32 [8, 4], P('gx', 'gy'), may hold values from 12 to 24, as said below
- normal_code: int32 [64, 32, 256], P('gx', 'gy'), may hold values from 0 to 25
Outputs:
- new_velocity: float32 [3, 768, 128], P(None, ('gx', 'gy'))
- new_affine: float32 [9, 768, 128], P(None, ('gx', 'gy'))
- new_deform: float32 [9, 768, 128], P(None, ('gx', 'gy'))
- new_stress: float32 [6, 768, 128], P(None, ('gx', 'gy'))
The draws below stay inside these ranges and needn't reach their ends.
Inputs may be any that keep to these rules, and one draw needn't show every extreme that they name: `deform`: A 3 x 3 identity plus entries between -0.3 and 0.3. `slot_tile_number`: on every device the first four slots lie in tiles on the low x, high x, low y and high y faces of its part of the grid, in that order. `block_count`: slots below the count are live; some device has exactly 24.
All inputs are finite; a program needn't handle non-finite values.
Results may differ from the reference program's by a relative error of at most 0.000073.
Values sent between devices are 32-bit elements; how exact they have to be, the bound alone decides.
A program may use at most 128 MiB of HBM per device.

```python
import math
import jax
import jax.numpy as jnp
from jax import lax

TX = 8
TY = 8
NZ = 256
BLK_CAP = 24
PB = 128
BODIES = 64
NX = 64
NY = 32
NBLK = 768
N_GX = 8
N_GY = 4


def draw_deform(key, part):
    noise = jnp.clip(0.1 * jax.random.normal(key, (9, NBLK, PB), jnp.float32), -0.3, 0.3)
    diagonal = (jnp.arange(9) % 4 == 0).astype(jnp.float32)
    return diagonal[:, None, None] + noise


def draw_slot_tile_number(key, part):
    tiles_x = TX // 4
    vertical_tiles = TY // 4
    tiles_z = NZ // 8
    devices = NBLK // BLK_CAP
    subkeys = jax.random.split(key, 3)
    coord_x = jax.random.randint(subkeys[0], (devices, BLK_CAP), 0, tiles_x)
    coord_y = jax.random.randint(subkeys[1], (devices, BLK_CAP), 0, vertical_tiles)
    coord_z = jax.random.randint(subkeys[2], (devices, BLK_CAP), 0, tiles_z)
    slot_position = jnp.arange(BLK_CAP)[None, :]
    coord_x = jnp.where(slot_position == 0, 0, jnp.where(slot_position == 1, tiles_x - 1, coord_x))
    coord_y = jnp.where(slot_position == 2, 0, jnp.where(slot_position == 3, vertical_tiles - 1, coord_y))
    return ((coord_x * vertical_tiles + coord_y) * tiles_z + coord_z).reshape(-1).astype(jnp.int32)


def draw_block_count(key, part):
    subkeys = jax.random.split(key, 2)
    lowest = BLK_CAP // 2
    counts = lowest + jax.random.randint(subkeys[0], (N_GX * N_GY,), 0, BLK_CAP - lowest + 1)
    busiest = jax.random.randint(subkeys[1], (), 0, N_GX * N_GY)
    counts = counts.at[busiest].set(BLK_CAP)
    return counts.reshape(N_GX, N_GY).astype(jnp.int32)


def touch_ends(values, stream_key, smallest, high):
    extent = values.shape
    index_at = [jax.random.randint(jax.random.fold_in(stream_key, axis), (), 0, extent[axis]) for axis in range(len(extent))]
    values = values.at[tuple(index_at)].set(smallest)
    longest = extent.index(max(extent))
    index_at[longest] = (index_at[longest] + 1) % extent[longest]
    return values.at[tuple(index_at)].set(high)


def levels(own_key, dims, shards, low, largest):
    level = 1.0
    for position, blocks in shards:
        draws = jax.random.uniform(jax.random.fold_in(jax.random.fold_in(own_key, 6), position), (blocks,), jnp.float32, low / len(shards), largest / len(shards))
        level = level * jnp.repeat(jnp.exp(draws), dims[position] // blocks).reshape((-1,) + (1,) * (len(dims) - 1 - position))
    return level


def gaussian(stream_key, shape, scale, bound, cuts=(), kind=jnp.bfloat16):
    values = jax.random.normal(stream_key, shape, jnp.float32) * scale
    if len(cuts) > 0:
        values = levels(stream_key, shape, cuts, -0.22, 0.18) * values
    return jnp.clip(values, min=-bound, max=bound).astype(kind)


def setup_inputs(seed: int = 0) -> dict:
    arg_keys = jax.random.split(jax.random.key(seed), 11)
    return {
        "offset": jnp.clip(0.5 + 1.0 * jax.random.uniform(arg_keys[0], (3, NBLK, PB), jnp.float32) ** levels(arg_keys[0], (3, NBLK, PB), ((1, 32),), -0.2, 0.2), 0.5, 1.5),
        "particle_mass": jnp.clip(jnp.exp(math.log(2.0) - 1.3862944 * jax.random.uniform(arg_keys[1], (NBLK, PB), jnp.float32) ** levels(arg_keys[1], (NBLK, PB), ((0, 32),), -0.2, 0.2)), 0.5, 2.0),
        "velocity": gaussian(arg_keys[2], (3, NBLK, PB), 1.0, 6.0, ((1, 32),), jnp.float32),
        "affine": gaussian(arg_keys[3], (9, NBLK, PB), 0.5, 3.0, ((1, 32),), jnp.float32),
        "deform": draw_deform(jax.random.fold_in(arg_keys[10], 71), 0),
        "particle_cell": touch_ends(jax.random.randint(arg_keys[5], (NBLK, PB), 0, 128), jax.random.fold_in(arg_keys[5], 1), 0, 127).astype(jnp.int32),
        "body_id": touch_ends(jax.random.randint(arg_keys[6], (NBLK, PB), 0, BODIES), jax.random.fold_in(arg_keys[6], 1), 0, BODIES - 1).astype(jnp.int32),
        "slot_tile_number": draw_slot_tile_number(jax.random.fold_in(arg_keys[10], 71), 0),
        "block_count": draw_block_count(jax.random.fold_in(arg_keys[10], 71), 0),
        "normal_code": touch_ends(jax.random.randint(arg_keys[9], (NX, NY, NZ), 0, 26), jax.random.fold_in(arg_keys[9], 1), 0, 25).astype(jnp.int32),
    }


DT = 0.1
MU = 2.0
LAM = 3.0
GRAVITY = -2.0
FLOOR = 0.25

def spline_weights(fraction):
    return [0.5 * (1.5 - fraction) * (1.5 - fraction), 0.75 - (fraction - 1.0) * (fraction - 1.0), 0.5 * (fraction - 0.5) * (fraction - 0.5)]

def determinant(matrix):
    return matrix[0] * (matrix[4] * matrix[8] - matrix[5] * matrix[7]) - matrix[1] * (matrix[3] * matrix[8] - matrix[5] * matrix[6]) + matrix[2] * (matrix[3] * matrix[7] - matrix[4] * matrix[6])

def kirchhoff(matrix):
    volume_ratio = determinant(matrix)
    pressure = 0.5 * LAM * (volume_ratio * volume_ratio - 1.0)
    entries = []
    for row_index in range(3):
        for column_position in range(3):
            element = matrix[3 * row_index] * matrix[3 * column_position] + matrix[3 * row_index + 1] * matrix[3 * column_position + 1] + matrix[3 * row_index + 2] * matrix[3 * column_position + 2]
            if row_index == column_position:
                element = MU * (element - 1.0) + pressure
            else:
                element = MU * element
            entries.append(element)
    return jnp.stack(entries)

def advance_deform(affine_new, deform):
    entries = []
    for row_index in range(3):
        for column_position in range(3):
            element = deform[3 * row_index + column_position]
            for inner_index in range(3):
                element = element + DT * affine_new[3 * row_index + inner_index] * deform[3 * inner_index + column_position]
            entries.append(element)
    return jnp.stack(entries)

def unit_normals(direction):
    shifted = direction + (direction >= 13).astype(jnp.int32)
    components = [shifted // 9 - 1, shifted // 3 % 3 - 1, shifted % 3 - 1]
    components = [part_value.astype(jnp.float32) for part_value in components]
    length = jnp.sqrt(components[0] * components[0] + components[1] * components[1] + components[2] * components[2])
    return jnp.stack([part_value / length for part_value in components])

def node_update(node_grid, normal):
    first_body_mass = node_grid[0]
    momentum_zero = node_grid[1:4]
    mass_one = node_grid[4]
    momentum_one = node_grid[5:8]
    gravity_step = jnp.array([0.0, 0.0, DT * GRAVITY], dtype=node_grid.dtype).reshape((3,) + (1,) * (node_grid.ndim - 1))
    speed_zero = momentum_zero / jnp.maximum(first_body_mass, FLOOR) + gravity_step
    speed_one = momentum_one / jnp.maximum(mass_one, FLOOR) + gravity_step
    center_speed = (momentum_zero + momentum_one) / jnp.maximum(first_body_mass + mass_one, FLOOR) + gravity_step
    contact_share = jnp.minimum(1.0, jnp.minimum(first_body_mass, mass_one) / FLOOR)
    approach_zero = jnp.maximum(lax.optimization_barrier(jnp.sum((speed_zero - center_speed) * normal, 0)), 0.0)
    approach_one = jnp.maximum(lax.optimization_barrier(jnp.sum((center_speed - speed_one) * normal, 0)), 0.0)
    speed_zero = speed_zero - (contact_share * approach_zero)[None] * normal
    speed_one = speed_one + (contact_share * approach_one)[None] * normal
    return jnp.concatenate([speed_zero, speed_one], 0)

def reference(offset, particle_mass, velocity, affine, deform, particle_cell, body_id, slot_tile_number, block_count, normal_code):
    slot_total = slot_tile_number.shape[0]
    slot_position = jnp.arange(slot_total, dtype=jnp.int32)
    device = slot_position // BLK_CAP
    index_x = device // N_GY
    index_y = device % N_GY
    live_mask = (slot_position % BLK_CAP < block_count.reshape(-1)[device]).astype(jnp.float32)[:, None]
    vertical_tiles = TY // 4
    tiles_z = NZ // 8
    tile_x = slot_tile_number // (vertical_tiles * tiles_z)
    tile_y = slot_tile_number // tiles_z % vertical_tiles
    tile_z = slot_tile_number % tiles_z
    cell_x = particle_cell // 32
    cell_y = particle_cell // 8 % 4
    cell_z = particle_cell % 8
    base_x = (index_x * TX + tile_x * 4)[:, None] + cell_x
    base_y = (index_y * TY + tile_y * 4)[:, None] + cell_y
    base_z = (tile_z * 8)[:, None] + cell_z
    size_x = TX * N_GX + 2
    vertical_size = TY * N_GY + 2
    size_z = NZ + 2
    weight_x = spline_weights(offset[0])
    weight_y = spline_weights(offset[1])
    weight_z = spline_weights(offset[2])
    field_zero = (body_id % 2 == 0).astype(jnp.float32)
    field_one = 1.0 - field_zero
    weighted = particle_mass * live_mask
    stress_old = kirchhoff(deform)
    affine_force = weighted[None] * (affine - 4.0 * DT * stress_old)
    node_grid = jnp.zeros((8, size_x * vertical_size * size_z), jnp.float32)
    for shift_x in range(3):
        for shift_y in range(3):
            for shift_z in range(3):
                weight = weight_x[shift_x] * weight_y[shift_y] * weight_z[shift_z]
                distance = [shift_x - offset[0], shift_y - offset[1], shift_z - offset[2]]
                momentum = []
                for row_index in range(3):
                    element = weighted * velocity[row_index]
                    for column_position in range(3):
                        element = element + affine_force[3 * row_index + column_position] * distance[column_position]
                    momentum.append(weight * element)
                values = [weight * weighted * field_zero] + [part_value * field_zero for part_value in momentum] + [weight * weighted * field_one] + [part_value * field_one for part_value in momentum]
                flat_index = ((base_x + shift_x) * vertical_size + base_y + shift_y) * size_z + base_z + shift_z
                node_grid = node_grid.at[:, flat_index.reshape(-1)].add(jnp.stack(values).reshape(8, -1))
    node_grid = node_grid.reshape(8, size_x, vertical_size, size_z)
    normal = jnp.pad(unit_normals(normal_code), ((0, 0), (1, 1), (1, 1), (1, 1)))
    inside = jnp.pad(jnp.ones((size_x - 2, vertical_size - 2, size_z - 2), jnp.float32), 1)
    node_speeds = node_update(node_grid, normal) * inside[None]
    flat_speeds = node_speeds.reshape(6, -1)
    speed_sum = jnp.zeros((3,) + particle_mass.shape, jnp.float32)
    moment_sums = jnp.zeros((9,) + particle_mass.shape, jnp.float32)
    for shift_x in range(3):
        for shift_y in range(3):
            for shift_z in range(3):
                weight = weight_x[shift_x] * weight_y[shift_y] * weight_z[shift_z]
                distance = [shift_x - offset[0], shift_y - offset[1], shift_z - offset[2]]
                flat_index = ((base_x + shift_x) * vertical_size + base_y + shift_y) * size_z + base_z + shift_z
                gathered = flat_speeds[:, flat_index.reshape(-1)].reshape((6,) + particle_mass.shape)
                chosen = gathered[0:3] * field_zero + gathered[3:6] * field_one
                speed_sum = speed_sum + weight * chosen
                moment_sums = moment_sums + jnp.stack([weight * distance[column_position] * chosen[row_index] for row_index in range(3) for column_position in range(3)])
    new_velocity = speed_sum * live_mask
    new_affine = 4.0 * moment_sums * live_mask
    new_deform = advance_deform(new_affine, deform) * live_mask
    stress_new = kirchhoff(new_deform)
    new_stress = jnp.stack([stress_new[0], stress_new[4], stress_new[8], stress_new[1], stress_new[2], stress_new[5]]) * live_mask
    return (new_velocity, new_affine, new_deform, new_stress)
```

```python
import functools

import jax
import jax.numpy as jnp
from jax import lax
from jax.experimental import pallas as pl
from jax.experimental.pallas import tpu as pltpu
from jax.sharding import PartitionSpec as P

DT = 0.1
MU = 2.0
LAM = 3.0
GRAVITY = -2.0
FLOOR = 0.25
LANES = 128
SUB = 8
TILE_X, TILE_Y, TILE_Z = 4, 4, 8
SPAN_Z = TILE_Z + 2
MESH = pl.DeviceIdType.MESH
F32 = jnp.float32
BF16 = jnp.bfloat16
DIRECTIONS = [(-1, 0), (1, 0), (0, -1), (0, 1), (-1, -1), (-1, 1), (1, -1), (1, 1)]


def spline_weights(fraction):
    return [
        0.5 * (1.5 - fraction) * (1.5 - fraction),
        0.75 - (fraction - 1.0) * (fraction - 1.0),
        0.5 * (fraction - 0.5) * (fraction - 0.5),
    ]


def determinant(m):
    return (
        m[0] * (m[4] * m[8] - m[5] * m[7])
        - m[1] * (m[3] * m[8] - m[5] * m[6])
        + m[2] * (m[3] * m[7] - m[4] * m[6])
    )


def kirchhoff(m):
    ratio = determinant(m)
    pressure = 0.5 * LAM * (ratio * ratio - 1.0)

    def dot(r, c):
        return m[3 * r] * m[3 * c] + m[3 * r + 1] * m[3 * c + 1] + m[3 * r + 2] * m[3 * c + 2]

    return [MU * (dot(r, r) - 1.0) + pressure for r in range(3)] + [
        MU * dot(0, 1),
        MU * dot(0, 2),
        MU * dot(1, 2),
    ]


SYMMETRIC = [0, 3, 4, 3, 1, 5, 4, 5, 2]


def split(value):
    high = value.astype(BF16)
    return high, (value - high.astype(F32)).astype(BF16)


def store_rows(rows_ref, blocks, offset_ref, cell_ref):
    cell = cell_ref[...]
    cells = [cell // (TILE_Y * TILE_Z), cell // TILE_Z % TILE_Y, cell % TILE_Z]
    rows = []
    for axis in range(2):
        fraction = offset_ref[axis]
        weights = spline_weights(fraction)
        rows.append(cells[axis].astype(F32))
        rows.extend(weights)
        rows.extend(weights[step] * (step - fraction) for step in range(3))
    fraction = offset_ref[2]
    weights = spline_weights(fraction)
    moments = [weights[step] * (step - fraction) for step in range(3)]
    for values in (weights, moments):
        for k in range(SPAN_Z):
            total = jnp.zeros_like(fraction)
            for step in range(3):
                total = jnp.where(cells[2] == k - step, values[step], total)
            rows.append(total)
    for index, row in enumerate(rows):
        rows_ref[pl.ds(index * blocks, blocks), :] = row


N_ROWS = 14 + 2 * SPAN_Z


def node_coordinates(n_y, padded_nodes):
    node = lax.broadcasted_iota(jnp.int32, (padded_nodes, LANES), 0)
    return (node // n_y).astype(F32), (node % n_y).astype(F32)


def plane_weights(rows_ref, blocks, block, tile, tiles, coordinates):
    tiles_y, tiles_z = tiles
    tile_x = (tile // (tiles_y * tiles_z) * TILE_X).astype(F32)
    tile_y = (tile // tiles_z % tiles_y * TILE_Y).astype(F32)

    def row(index):
        return rows_ref[pl.ds(index * blocks + block, 1), :]

    parts = []
    for axis, corner in enumerate((tile_x, tile_y)):
        first = 7 * axis
        step = coordinates[axis] - (row(first) + corner)
        hits = [step == float(s) for s in range(3)]
        for shift in (1, 4):
            total = jnp.zeros_like(step)
            for s in range(3):
                total = jnp.where(hits[s], row(first + shift + s), total)
            parts.append(total)
    weight_x, moment_x, weight_y, moment_y = parts
    out = [weight_x * weight_y, moment_x * weight_y, weight_x * moment_y]
    pad = jnp.zeros((LANES - coordinates[0].shape[0], LANES), F32)
    return [jnp.concatenate([p, pad], 0) for p in out]


def scatter_kernel(
    shape,
    tile_ref,
    count_ref,
    offset_ref,
    mass_ref,
    velocity_ref,
    affine_ref,
    deform_ref,
    cell_ref,
    body_ref,
    grid_ref,
    source_ref,
    rows_ref,
):
    n_y, padded_nodes, tiles, unroll = shape
    blocks = mass_ref.shape[0]
    slot = lax.broadcasted_iota(jnp.int32, mass_ref.shape, 0)
    mass = jnp.where(slot < count_ref[0, 0], mass_ref[...], 0.0)
    even = body_ref[...] % 2 == 0
    masses = [jnp.where(even, mass, 0.0), jnp.where(even, 0.0, mass)]
    tau = kirchhoff([deform_ref[i] for i in range(9)])
    force = [affine_ref[i] - 4.0 * DT * tau[SYMMETRIC[i]] for i in range(9)]
    zero = jnp.zeros_like(mass)

    def put(group, channel, value):
        source_ref[pl.ds(group * blocks * SUB + channel, blocks, stride=SUB), :] = value

    for field in range(2):
        put(0, 4 * field, masses[field])
        for r in range(3):
            put(0, 4 * field + 1 + r, masses[field] * velocity_ref[r])
        for c in range(3):
            put(1 + c, 4 * field, zero)
            for r in range(3):
                put(1 + c, 4 * field + 1 + r, masses[field] * force[3 * r + c])
    store_rows(rows_ref, blocks, offset_ref, cell_ref)
    grid_ref[...] = jnp.zeros_like(grid_ref)
    coordinates = node_coordinates(n_y, padded_nodes)

    def block_sums(block):
        tile = tile_ref[block]
        planes = plane_weights(rows_ref, blocks, block, tile, tiles, coordinates)
        groups = [
            source_ref[
                pl.ds(pl.multiple_of(g * blocks * SUB + block * SUB, SUB), SUB), :
            ]
            for g in range(4)
        ]
        left = [[], [], []]
        for k in range(SPAN_Z):
            weight = rows_ref[pl.ds((14 + k) * blocks + block, 1), :]
            moment = rows_ref[pl.ds((14 + SPAN_Z + k) * blocks + block, 1), :]
            left[0].append(groups[0] * weight + groups[3] * moment)
            left[1].append(groups[1] * weight)
            left[2].append(groups[2] * weight)
        left = jnp.concatenate([jnp.concatenate(part, 0) for part in left], 1)
        right = jnp.concatenate(planes, 1)
        left_high, left_low = split(left)
        right_high, right_low = split(right)
        product = lax.dot_general(
            jnp.concatenate([left_high, left_low], 0),
            jnp.concatenate([right_high, right_low], 0),
            (((1,), (1,)), ((), ())),
            preferred_element_type=F32,
        )
        n = SPAN_Z * SUB
        return product[:n, :LANES] + (product[:n, LANES:] + product[n:, :LANES])

    def step(index, carry):
        members = [index * unroll + u for u in range(unroll)]
        sums = [block_sums(block) for block in members]
        for block, patch in zip(members, sums):
            start = pl.multiple_of(tile_ref[block] % tiles[1] * (TILE_Z * SUB), SUB)
            window = pl.ds(start, SPAN_Z * SUB)
            grid_ref[window, :] = grid_ref[window, :] + patch
        return carry

    lax.fori_loop(0, blocks // unroll, step, 0)


def face_runs(direction, n_x, n_y):
    dx, dy = direction
    xs = {-1: (0, 2), 0: (0, n_x), 1: (n_x - 2, 2)}[dx]
    ys = {-1: (0, 2), 0: (0, n_y), 1: (n_y - 2, 2)}[dy]
    if dy == 0:
        return [(xs[0] * n_y, xs[1] * n_y)]
    return [((xs[0] + i) * n_y + ys[0], ys[1]) for i in range(xs[1])]


def face_nodes(direction, n_x, n_y):
    return sum(count for _, count in face_runs(direction, n_x, n_y))


def exchange_kernel(shape, grid_ref, code_ref, speed_ref, *scratch):
    n_x, n_y, padded_nodes, halves = shape
    node_ref, codes_ref, planes_ref, send_code, recv_code = scratch[:5]
    sends = scratch[5:13]
    recvs = scratch[13:21]
    send_sem, recv_sem, code_send_sem, code_recv_sem = scratch[21:]
    size_x, size_y = lax.axis_size("gx"), lax.axis_size("gy")
    me_x, me_y = lax.axis_index("gx"), lax.axis_index("gy")
    own_x, own_y = n_x - 2, n_y - 2
    valid = []
    for dx, dy in DIRECTIONS:
        ok = None
        for d, me, size in ((dx, me_x, size_x), (dy, me_y, size_y)):
            if d == 0:
                continue
            one = me > 0 if d < 0 else me < size - 1
            ok = one if ok is None else jnp.logical_and(ok, one)
        valid.append(ok)
    barrier = pltpu.get_barrier_semaphore()

    def target(index):
        dx, dy = DIRECTIONS[index]
        return {"gx": me_x + dx, "gy": me_y + dy}

    for index in range(8):

        @pl.when(valid[index])
        def _(index=index):
            pl.semaphore_signal(
                barrier, inc=1, device_id=target(index), device_id_type=MESH
            )

    opposite = [DIRECTIONS.index((-dx, -dy)) for dx, dy in DIRECTIONS]
    plane = padded_nodes * SUB

    for half in range(halves):
        lanes = pl.ds(half * LANES, LANES)
        rows = pl.ds(half * own_y, own_y)
        for index, (dx, dy) in enumerate(DIRECTIONS):
            x = 0 if dx < 0 else own_x - 1
            y = 0 if dy < 0 else own_y - 1
            if dy == 0:
                send_code[index, rows, :] = code_ref[x, :, lanes]
            elif dx == 0:
                for i in range(own_x):
                    send_code[index, pl.ds(half * own_y + i, 1), :] = code_ref[
                        i, pl.ds(y, 1), lanes
                    ]
            else:
                send_code[index, rows, :] = jnp.broadcast_to(
                    code_ref[x, pl.ds(y, 1), lanes], (own_y, LANES)
                )

    def code_copy(index):
        return pltpu.make_async_remote_copy(
            src_ref=send_code.at[index],
            dst_ref=recv_code.at[opposite[index]],
            send_sem=code_send_sem.at[index],
            recv_sem=code_recv_sem.at[opposite[index]],
            device_id=target(index),
            device_id_type=MESH,
        )

    def face_copy(index):
        return pltpu.make_async_remote_copy(
            src_ref=sends[index],
            dst_ref=recvs[opposite[index]],
            send_sem=send_sem.at[index],
            recv_sem=recv_sem.at[opposite[index]],
            device_id=target(index),
            device_id_type=MESH,
        )

    for half in range(halves):
        for c in range(SUB):
            part = grid_ref[pl.ds((1 + half * LANES) * SUB + c, LANES, stride=SUB), :]
            node_ref[pl.ds(half * plane + c, padded_nodes, stride=SUB), :] = part.T[
                :padded_nodes
            ]

    def each_run(index):
        offset = 0
        for half in range(halves):
            for first, count in face_runs(DIRECTIONS[index], n_x, n_y):
                yield (
                    pl.ds(half * plane + first * SUB, count * SUB),
                    pl.ds(offset, count * SUB),
                )
                offset += count * SUB

    for index in range(8):
        for nodes, run in each_run(index):
            sends[index][run, :] = node_ref[nodes, :]

    arrivals = sum(ok.astype(jnp.int32) for ok in valid)
    pl.semaphore_wait(barrier, arrivals)
    for index in [2, 3, 4, 5, 6, 7, 0, 1]:

        @pl.when(valid[index])
        def _(index=index):
            code_copy(index).start()
            face_copy(index).start()

        @pl.when(jnp.logical_not(valid[index]))
        def _(index=index):
            recv_code[index] = jnp.zeros(recv_code.shape[1:], jnp.int32)
            recvs[index][...] = jnp.zeros_like(recvs[index])

    codes_ref[...] = jnp.zeros_like(codes_ref)
    for half in range(halves):
        lanes = pl.ds(half * LANES, LANES)
        for x in range(own_x):
            codes_ref[pl.ds(half * padded_nodes + (x + 1) * n_y + 1, own_y), :] = code_ref[
                x, :, lanes
            ]
    planes_ref[:, pl.ds(padded_nodes, LANES - padded_nodes), :] = jnp.zeros(
        (planes_ref.shape[0], LANES - padded_nodes, LANES), F32
    )

    for index in [0, 1, 4, 5, 6, 7, 2, 3]:

        @pl.when(valid[index])
        def _(index=index):
            code_copy(opposite[index]).wait_recv()
            face_copy(opposite[index]).wait_recv()

    for index, (dx, dy) in enumerate(DIRECTIONS):
        x = 0 if dx < 0 else n_x - 1
        y = 0 if dy < 0 else n_y - 1
        for half in range(halves):
            base = half * padded_nodes
            if dy == 0:
                codes_ref[pl.ds(base + x * n_y + 1, own_y), :] = recv_code[
                    index, pl.ds(half * own_y, own_y), :
                ]
            elif dx == 0:
                for i in range(own_x):
                    codes_ref[pl.ds(base + (i + 1) * n_y + y, 1), :] = recv_code[
                        index, pl.ds(half * own_y + i, 1), :
                    ]
            else:
                codes_ref[pl.ds(base + x * n_y + y, 1), :] = recv_code[
                    index, pl.ds(half * own_y, 1), :
                ]
        for nodes, run in each_run(index):
            node_ref[nodes, :] = node_ref[nodes, :] + recvs[index][run, :]

    groups = padded_nodes // SUB

    def update(step, carry):
        half = step // groups
        group = step % groups
        base = half * plane + group * (SUB * SUB)
        channels = [
            node_ref[pl.ds(base + c, SUB, stride=SUB), :] for c in range(SUB)
        ]
        code = codes_ref[pl.ds(pl.multiple_of(step * SUB, SUB), SUB), :]
        shifted = code + (code >= 13).astype(jnp.int32)
        normal = [shifted // 9 - 1, shifted // 3 % 3 - 1, shifted % 3 - 1]
        normal = [n.astype(F32) for n in normal]
        length = jnp.sqrt(
            normal[0] * normal[0] + normal[1] * normal[1] + normal[2] * normal[2]
        )
        length = jnp.maximum(length, 1.0)
        normal = [n / length for n in normal]
        masses = [channels[0], channels[4]]
        momenta = [channels[1:4], channels[5:8]]
        gravity = [0.0, 0.0, DT * GRAVITY]
        speeds = [
            [p / jnp.maximum(masses[f], FLOOR) + gravity[r] for r, p in enumerate(momenta[f])]
            for f in range(2)
        ]
        both = jnp.maximum(masses[0] + masses[1], FLOOR)
        center = [
            (momenta[0][r] + momenta[1][r]) / both + gravity[r] for r in range(3)
        ]
        share = jnp.minimum(1.0, jnp.minimum(masses[0], masses[1]) / FLOOR)
        closing = [
            share
            * jnp.maximum(
                sum((speeds[0][r] - center[r]) * normal[r] for r in range(3)), 0.0
            ),
            share
            * jnp.maximum(
                sum((center[r] - speeds[1][r]) * normal[r] for r in range(3)), 0.0
            ),
        ]
        node = group * SUB + lax.broadcasted_iota(jnp.int32, (SUB, LANES), 0)
        x = me_x * own_x + node // n_y
        y = me_y * own_y + node % n_y
        inside = (x >= 1) & (x <= size_x * own_x) & (y >= 1) & (y <= size_y * own_y)
        rows = pl.ds(pl.multiple_of(group * SUB, SUB), SUB)
        for f, sign in ((0, -1.0), (1, 1.0)):
            for r in range(3):
                speed = speeds[f][r] + sign * closing[f] * normal[r]
                planes_ref[half * 6 + 3 * f + r, rows, :] = jnp.where(inside, speed, 0.0)
        return carry

    lax.fori_loop(0, halves * groups, update, 0)
    edge = jnp.zeros((SUB, LANES), F32)
    depth = halves * LANES
    speed_ref[pl.ds(0, SUB), :] = edge
    speed_ref[pl.ds((depth + 1) * SUB, SUB), :] = edge
    for half in range(halves):
        for c in range(6):
            channel = c // 3 * 4 + c % 3
            speed_ref[
                pl.ds((1 + half * LANES) * SUB + channel, LANES, stride=SUB), :
            ] = planes_ref[half * 6 + c].T
        for channel in (3, 7):
            speed_ref[
                pl.ds((1 + half * LANES) * SUB + channel, LANES, stride=SUB), :
            ] = jnp.zeros((LANES, LANES), F32)

    for index in range(8):

        @pl.when(valid[index])
        def _(index=index):
            code_copy(index).wait_send()
            face_copy(index).wait_send()


def gather_kernel(
    shape,
    tile_ref,
    count_ref,
    speed_ref,
    offset_ref,
    deform_ref,
    cell_ref,
    body_ref,
    new_velocity_ref,
    new_affine_ref,
    new_deform_ref,
    new_stress_ref,
    result_ref,
    rows_ref,
):
    n_y, padded_nodes, tiles, unroll = shape
    blocks = cell_ref.shape[0]
    store_rows(rows_ref, blocks, offset_ref, cell_ref)
    coordinates = node_coordinates(n_y, padded_nodes)

    def block_speeds(block):
        tile = tile_ref[block]
        planes = plane_weights(rows_ref, blocks, block, tile, tiles, coordinates)
        start = pl.multiple_of(tile % tiles[1] * (TILE_Z * SUB), SUB)
        speeds = speed_ref[pl.ds(start, SPAN_Z * SUB), :]
        left_high, left_low = split(speeds)
        right_high, right_low = split(jnp.concatenate(planes, 1))
        product = jnp.dot(
            jnp.concatenate([left_high, left_low, left_high], 1),
            jnp.concatenate([right_high, right_high, right_low], 0),
            preferred_element_type=F32,
        )
        sums = [jnp.zeros((SUB, LANES), F32) for _ in range(4)]
        for k in range(SPAN_Z):
            weight = rows_ref[pl.ds((14 + k) * blocks + block, 1), :]
            moment = rows_ref[pl.ds((14 + SPAN_Z + k) * blocks + block, 1), :]
            rows = [product[k * SUB : (k + 1) * SUB, v * LANES : (v + 1) * LANES] for v in range(3)]
            sums[0] = sums[0] + rows[0] * weight
            sums[1] = sums[1] + rows[1] * weight
            sums[2] = sums[2] + rows[2] * weight
            sums[3] = sums[3] + rows[0] * moment
        return sums

    def step(index, carry):
        members = [index * unroll + u for u in range(unroll)]
        results = [block_speeds(block) for block in members]
        for block, sums in zip(members, results):
            for v in range(4):
                start = pl.multiple_of(v * blocks * SUB + block * SUB, SUB)
                result_ref[pl.ds(start, SUB), :] = sums[v]
        return carry

    lax.fori_loop(0, blocks // unroll, step, 0)
    slot = lax.broadcasted_iota(jnp.int32, cell_ref.shape, 0)
    live = slot < count_ref[0, 0]
    even = body_ref[...] % 2 == 0

    def take(v, r):
        fields = [
            result_ref[pl.ds(v * blocks * SUB + 4 * f + r, blocks, stride=SUB), :]
            for f in range(2)
        ]
        return jnp.where(live, jnp.where(even, fields[0], fields[1]), 0.0)

    for r in range(3):
        new_velocity_ref[r] = take(0, r)
    affine = [4.0 * take(1 + c, r) for r in range(3) for c in range(3)]
    deform = [deform_ref[i] for i in range(9)]
    moved = []
    for r in range(3):
        for c in range(3):
            entry = deform[3 * r + c]
            for i in range(3):
                entry = entry + DT * affine[3 * r + i] * deform[3 * i + c]
            moved.append(jnp.where(live, entry, 0.0))
    for i in range(9):
        new_affine_ref[i] = affine[i]
        new_deform_ref[i] = moved[i]
    for i, entry in enumerate(kirchhoff(moved)):
        new_stress_ref[i] = jnp.where(live, entry, 0.0)


def per_device(
    offset,
    particle_mass,
    velocity,
    affine,
    deform,
    particle_cell,
    body_id,
    slot_tile_number,
    block_count,
    normal_code,
):
    blocks, particles = particle_mass.shape
    own_x, own_y, depth = normal_code.shape
    tiles = (own_y // TILE_Y, depth // TILE_Z)
    n_x, n_y = own_x + 2, own_y + 2
    padded_nodes = -(-n_x * n_y // SUB) * SUB
    halves = depth // LANES
    assert particles == LANES and padded_nodes <= LANES and depth % LANES == 0
    unroll = 2 if blocks % 2 == 0 else 1
    vmem = pl.BlockSpec(memory_space=pltpu.VMEM)
    smem = pl.BlockSpec(memory_space=pltpu.SMEM)
    limit = 40 * 1024 * 1024
    grid_shape = jax.ShapeDtypeStruct(((depth + 2) * SUB, LANES), F32)
    work = (n_y, padded_nodes, tiles, unroll)
    node_sums = pl.pallas_call(
        functools.partial(scatter_kernel, work),
        out_shape=grid_shape,
        in_specs=[smem, smem] + [vmem] * 7,
        out_specs=vmem,
        scratch_shapes=[
            pltpu.VMEM((4 * blocks * SUB, LANES), F32),
            pltpu.VMEM((N_ROWS * blocks, LANES), F32),
        ],
        compiler_params=pltpu.CompilerParams(vmem_limit_bytes=limit),
        name="particles_to_nodes",
    )(
        slot_tile_number,
        block_count,
        offset,
        particle_mass,
        velocity,
        affine,
        deform,
        particle_cell,
        body_id,
    )
    faces = [
        pltpu.VMEM((halves * face_nodes(d, n_x, n_y) * SUB, LANES), F32) for d in DIRECTIONS
    ]
    speeds = pl.pallas_call(
        functools.partial(exchange_kernel, (n_x, n_y, padded_nodes, halves)),
        out_shape=grid_shape,
        in_specs=[vmem, vmem],
        out_specs=vmem,
        scratch_shapes=[
            pltpu.VMEM((halves * padded_nodes * SUB, LANES), F32),
            pltpu.VMEM((halves * padded_nodes, LANES), jnp.int32),
            pltpu.VMEM((halves * 6, LANES, LANES), F32),
            pltpu.VMEM((8, halves * own_y, LANES), jnp.int32),
            pltpu.VMEM((8, halves * own_y, LANES), jnp.int32),
        ]
        + faces
        + faces
        + [pltpu.SemaphoreType.DMA((8,))] * 4,
        compiler_params=pltpu.CompilerParams(
            collective_id=0, has_side_effects=True, vmem_limit_bytes=limit
        ),
        name="node_exchange",
    )(node_sums, normal_code)
    shaped = lambda n: jax.ShapeDtypeStruct((n, blocks, LANES), F32)
    return pl.pallas_call(
        functools.partial(gather_kernel, work),
        out_shape=(shaped(3), shaped(9), shaped(9), shaped(6)),
        in_specs=[smem, smem] + [vmem] * 5,
        out_specs=(vmem,) * 4,
        scratch_shapes=[
            pltpu.VMEM((4 * blocks * SUB, LANES), F32),
            pltpu.VMEM((N_ROWS * blocks, LANES), F32),
        ],
        compiler_params=pltpu.CompilerParams(vmem_limit_bytes=limit),
        name="nodes_to_particles",
    )(slot_tile_number, block_count, speeds, offset, deform, particle_cell, body_id)


def solution(mesh):
    particle = P(None, ("gx", "gy"), None)
    flat = P(("gx", "gy"), None)
    placed = (
        particle,
        flat,
        particle,
        particle,
        particle,
        flat,
        flat,
        P(("gx", "gy")),
        P("gx", "gy"),
        P("gx", "gy", None),
    )
    return jax.shard_map(
        per_device,
        mesh=mesh,
        in_specs=placed,
        out_specs=(particle,) * 4,
        check_vma=False,
    )
```

```python
import functools

import jax
import jax.numpy as jnp
from jax import lax
from jax.experimental import pallas as pl
from jax.experimental.pallas import tpu as pltpu
from jax.sharding import PartitionSpec as P

DT = 0.1
MU = 2.0
LAM = 3.0
GRAVITY = -2.0
FLOOR = 0.25
LANES = 128
SUB = 8
TILE_X, TILE_Y, TILE_Z = 4, 4, 8
SPAN_Z = TILE_Z + 2
MESH = pl.DeviceIdType.MESH
F32 = jnp.float32
BF16 = jnp.bfloat16
SIDES = [(-1, 0), (1, 0), (0, -1), (0, 1)]
DIRECTIONS = [(-1, 0), (1, 0), (0, -1), (0, 1), (-1, -1), (-1, 1), (1, -1), (1, 1)]


def spline_weights(fraction):
    return [
        0.5 * (1.5 - fraction) * (1.5 - fraction),
        0.75 - (fraction - 1.0) * (fraction - 1.0),
        0.5 * (fraction - 0.5) * (fraction - 0.5),
    ]


def determinant(m):
    return (
        m[0] * (m[4] * m[8] - m[5] * m[7])
        - m[1] * (m[3] * m[8] - m[5] * m[6])
        + m[2] * (m[3] * m[7] - m[4] * m[6])
    )


def kirchhoff(m):
    ratio = determinant(m)
    pressure = 0.5 * LAM * (ratio * ratio - 1.0)

    def dot(r, c):
        return m[3 * r] * m[3 * c] + m[3 * r + 1] * m[3 * c + 1] + m[3 * r + 2] * m[3 * c + 2]

    return [MU * (dot(r, r) - 1.0) + pressure for r in range(3)] + [
        MU * dot(0, 1),
        MU * dot(0, 2),
        MU * dot(1, 2),
    ]


SYMMETRIC = [0, 3, 4, 3, 1, 5, 4, 5, 2]


def split(value):
    high = value.astype(BF16)
    return high, (value - high.astype(F32)).astype(BF16)


def store_rows(rows_ref, blocks, offset_ref, cell_ref):
    cell = cell_ref[...]
    cells = [cell // (TILE_Y * TILE_Z), cell // TILE_Z % TILE_Y, cell % TILE_Z]
    rows = []
    for axis in range(2):
        fraction = offset_ref[axis]
        weights = spline_weights(fraction)
        rows.append(cells[axis].astype(F32))
        rows.extend(weights)
        rows.extend(weights[step] * (step - fraction) for step in range(3))
    fraction = offset_ref[2]
    weights = spline_weights(fraction)
    moments = [weights[step] * (step - fraction) for step in range(3)]
    for values in (weights, moments):
        for k in range(SPAN_Z):
            total = jnp.zeros_like(fraction)
            for step in range(3):
                total = jnp.where(cells[2] == k - step, values[step], total)
            rows.append(total)
    for index, row in enumerate(rows):
        rows_ref[pl.ds(index * blocks, blocks), :] = row


N_ROWS = 14 + 2 * SPAN_Z


def node_coordinates(n_x, padded_nodes):
    node = lax.broadcasted_iota(jnp.int32, (padded_nodes, LANES), 0)
    return (node % n_x).astype(F32), (node // n_x).astype(F32)


def plane_weights(rows_ref, blocks, block, tile, tiles, coordinates):
    tiles_y, tiles_z = tiles
    tile_x = (tile // (tiles_y * tiles_z) * TILE_X).astype(F32)
    tile_y = (tile // tiles_z % tiles_y * TILE_Y).astype(F32)

    def row(index):
        return rows_ref[pl.ds(index * blocks + block, 1), :]

    parts = []
    for axis, corner in enumerate((tile_x, tile_y)):
        first = 7 * axis
        step = coordinates[axis] - (row(first) + corner)
        hits = [step == float(s) for s in range(3)]
        for shift in (1, 4):
            total = jnp.zeros_like(step)
            for s in range(3):
                total = jnp.where(hits[s], row(first + shift + s), total)
            parts.append(total)
    weight_x, moment_x, weight_y, moment_y = parts
    out = [weight_x * weight_y, moment_x * weight_y, weight_x * moment_y]
    pad = jnp.zeros((LANES - coordinates[0].shape[0], LANES), F32)
    return [jnp.concatenate([p, pad], 0) for p in out]


def face_runs(kind, side, n_x, n_y):
    if kind == "x":
        first = 0 if side < 0 else n_x - 2
        return [(y * n_x + first, 2) for y in range(n_y)]
    layers = (0, 1) if side < 0 else (n_y - 2, n_y - 1)
    if kind == "inner":
        return [(y * n_x + 2, n_x - 4) for y in layers]
    return [(y * n_x + first, 2) for y in layers for first in (0, n_x - 2)]


FACES = [("x", -1), ("x", 1), ("inner", -1), ("inner", 1), ("outer", -1), ("outer", 1)]


def nodes_kernel(
    shape,
    tile_ref,
    count_ref,
    offset_hbm,
    mass_hbm,
    velocity_hbm,
    affine_hbm,
    deform_hbm,
    cell_hbm,
    body_hbm,
    code_hbm,
    speed_ref,
    *scratch,
):
    n_x, n_y, padded_nodes, halves, tiles, unroll = shape
    inputs = scratch[:8]
    offset_ref, mass_ref, velocity_ref, affine_ref, deform_ref = inputs[:5]
    cell_ref, body_ref, code_ref = inputs[5:]
    (
        source_ref,
        rows_ref,
        chain_ref,
        grid_ref,
        table_ref,
        links,
        node_ref,
        codes_ref,
        planes_ref,
        send_code,
        recv_code,
    ) = scratch[8:19]
    sends = scratch[19:25]
    recvs = scratch[25:31]
    send_sem, recv_sem, code_send_sem, code_recv_sem, in_sem, table_sem = scratch[31:]
    blocks = mass_ref.shape[0]
    size_x, size_y = lax.axis_size("gx"), lax.axis_size("gy")
    me_x, me_y = lax.axis_index("gx"), lax.axis_index("gy")
    own_x, own_y = n_x - 2, n_y - 2

    hbm = (
        offset_hbm,
        mass_hbm,
        velocity_hbm,
        affine_hbm,
        deform_hbm,
        cell_hbm,
        body_hbm,
        code_hbm,
    )
    loads = [
        pltpu.make_async_copy(source, target, in_sem.at[i])
        for i, (source, target) in enumerate(zip(hbm, inputs))
    ]
    for load in loads:
        load.start()

    valid = []
    for dx, dy in DIRECTIONS:
        ok = None
        for d, me, size in ((dx, me_x, size_x), (dy, me_y, size_y)):
            if d == 0:
                continue
            one = me > 0 if d < 0 else me < size - 1
            ok = one if ok is None else jnp.logical_and(ok, one)
        valid.append(ok)
    barrier = pltpu.get_barrier_semaphore()

    def target(index):
        dx, dy = DIRECTIONS[index]
        return {"gx": me_x + dx, "gy": me_y + dy}

    for index in range(8):

        @pl.when(valid[index])
        def _(index=index):
            pl.semaphore_signal(
                barrier, inc=1, device_id=target(index), device_id_type=MESH
            )

    opposite = [DIRECTIONS.index((-dx, -dy)) for dx, dy in DIRECTIONS]
    plane = padded_nodes * SUB

    lane = lax.broadcasted_iota(jnp.int32, (SUB, LANES), 1)
    heights = [tile_ref[s] % tiles[1] for s in range(blocks)]
    height = jnp.full((SUB, LANES), -1, jnp.int32)
    for s in range(blocks):
        height = jnp.where(lane == s, heights[s], height)
    before = jnp.zeros((SUB, LANES), jnp.int32)
    last = jnp.zeros((SUB, LANES), jnp.int32)
    for s in range(blocks):
        before = jnp.where((height == heights[s]) & (lane > s), s + 1, before)
        last = jnp.where(lane == heights[s], s + 1, last)
    sublane = lax.broadcasted_iota(jnp.int32, (SUB, LANES), 0)
    table_ref[...] = jnp.where(sublane == 0, before, last)
    table_copy = pltpu.make_async_copy(table_ref, links, table_sem)
    table_copy.start()

    for load in loads[:7]:
        load.wait()
    slot = lax.broadcasted_iota(jnp.int32, mass_ref.shape, 0)
    mass = jnp.where(slot < count_ref[0, 0], mass_ref[...], 0.0)
    even = body_ref[...] % 2 == 0
    masses = [jnp.where(even, mass, 0.0), jnp.where(even, 0.0, mass)]
    tau = kirchhoff([deform_ref[i] for i in range(9)])
    force = [affine_ref[i] - 4.0 * DT * tau[SYMMETRIC[i]] for i in range(9)]
    zero = jnp.zeros_like(mass)

    def put(group, channel, value):
        source_ref[pl.ds(group * blocks * SUB + channel, blocks, stride=SUB), :] = value

    for field in range(2):
        put(0, 4 * field, masses[field])
        for r in range(3):
            put(0, 4 * field + 1 + r, masses[field] * velocity_ref[r])
        for c in range(3):
            put(1 + c, 4 * field, zero)
            for r in range(3):
                put(1 + c, 4 * field + 1 + r, masses[field] * force[3 * r + c])
    store_rows(rows_ref, blocks, offset_ref, cell_ref)
    coordinates = node_coordinates(n_x, padded_nodes)
    span = SPAN_Z * SUB
    chain_ref[0] = jnp.zeros((span, LANES), F32)
    table_copy.wait()

    def block_sums(block):
        tile = tile_ref[block]
        planes = plane_weights(rows_ref, blocks, block, tile, tiles, coordinates)
        groups = [
            source_ref[
                pl.ds(pl.multiple_of(g * blocks * SUB + block * SUB, SUB), SUB), :
            ]
            for g in range(4)
        ]
        left = [[], [], []]
        for k in range(SPAN_Z):
            weight = rows_ref[pl.ds((14 + k) * blocks + block, 1), :]
            moment = rows_ref[pl.ds((14 + SPAN_Z + k) * blocks + block, 1), :]
            left[0].append(groups[0] * weight + groups[3] * moment)
            left[1].append(groups[1] * weight)
            left[2].append(groups[2] * weight)
        left = jnp.concatenate([jnp.concatenate(part, 0) for part in left], 1)
        right = jnp.concatenate(planes, 1)
        left_high, left_low = split(left)
        right_high, right_low = split(right)
        product = lax.dot_general(
            jnp.concatenate([left_high, left_low], 0),
            jnp.concatenate([right_high, right_low], 0),
            (((1,), (1,)), ((), ())),
            preferred_element_type=F32,
        )
        return product[:span, :LANES] + (product[:span, LANES:] + product[span:, :LANES])

    def step(index, carry):
        members = [index * unroll + u for u in range(unroll)]
        sums = [block_sums(block) for block in members]
        for block, patch in zip(members, sums):
            chain_ref[block + 1] = chain_ref[links[0, block]] + patch
        return carry

    lax.fori_loop(0, blocks // unroll, step, 0)

    loads[7].wait()
    for half in range(halves):
        lanes = pl.ds(half * LANES, LANES)
        rows = pl.ds(half * own_y, own_y)
        for index, (dx, dy) in enumerate(DIRECTIONS):
            x = 0 if dx < 0 else own_x - 1
            y = 0 if dy < 0 else own_y - 1
            if dy == 0:
                send_code[index, rows, :] = code_ref[x, :, lanes]
            elif dx == 0:
                for i in range(own_x):
                    send_code[index, pl.ds(half * own_y + i, 1), :] = code_ref[
                        i, pl.ds(y, 1), lanes
                    ]
            else:
                send_code[index, rows, :] = jnp.broadcast_to(
                    code_ref[x, pl.ds(y, 1), lanes], (own_y, LANES)
                )

    def code_copy(index):
        return pltpu.make_async_remote_copy(
            src_ref=send_code.at[index],
            dst_ref=recv_code.at[opposite[index]],
            send_sem=code_send_sem.at[index],
            recv_sem=code_recv_sem.at[opposite[index]],
            device_id=target(index),
            device_id_type=MESH,
        )

    def face_copy(face):
        return pltpu.make_async_remote_copy(
            src_ref=sends[face],
            dst_ref=recvs[face ^ 1],
            send_sem=send_sem.at[face],
            recv_sem=recv_sem.at[face ^ 1],
            device_id=target(min(face, 2 + face % 2)),
            device_id_type=MESH,
        )

    def face_valid(face):
        return valid[min(face, 2 + face % 2)]

    arrivals = sum(ok.astype(jnp.int32) for ok in valid)
    pl.semaphore_wait(barrier, arrivals)
    for index in range(8):

        @pl.when(valid[index])
        def _(index=index):
            code_copy(index).start()

        @pl.when(jnp.logical_not(valid[index]))
        def _(index=index):
            recv_code[index] = jnp.zeros(recv_code.shape[1:], jnp.int32)

    body_rows = TILE_Z * SUB
    over = span - body_rows

    def assemble(j, carry):
        patch = chain_ref[links[1, j]]
        rows = pl.multiple_of(j * body_rows, SUB)
        grid_ref[pl.ds(rows, over), :] = patch[:over] + carry
        grid_ref[pl.ds(rows + over, body_rows - over), :] = patch[over:body_rows]
        return patch[body_rows:]

    tail = lax.fori_loop(0, tiles[1], assemble, jnp.zeros((over, LANES), F32), unroll=4)
    grid_ref[pl.ds(tiles[1] * body_rows, over), :] = tail

    for half in range(halves):
        for c in range(SUB):
            part = grid_ref[pl.ds((1 + half * LANES) * SUB + c, LANES, stride=SUB), :]
            node_ref[pl.ds(half * plane + c, padded_nodes, stride=SUB), :] = part.T[
                :padded_nodes
            ]

    def each_run(face):
        offset = 0
        for half in range(halves):
            for first, count in face_runs(*FACES[face], n_x, n_y):
                yield (
                    pl.ds(half * plane + first * SUB, count * SUB),
                    pl.ds(offset, count * SUB),
                )
                offset += count * SUB

    def send_face(face):
        for nodes, run in each_run(face):
            sends[face][run, :] = node_ref[nodes, :]

        @pl.when(face_valid(face))
        def _():
            face_copy(face).start()

        @pl.when(jnp.logical_not(face_valid(face)))
        def _():
            recvs[face][...] = jnp.zeros_like(recvs[face])

    def take_face(face):
        @pl.when(face_valid(face))
        def _():
            face_copy(face ^ 1).wait_recv()

        for nodes, run in each_run(face):
            node_ref[nodes, :] = node_ref[nodes, :] + recvs[face][run, :]

    for face in (0, 1, 2, 3):
        send_face(face)

    codes_ref[...] = jnp.zeros_like(codes_ref)
    for half in range(halves):
        lanes = pl.ds(half * LANES, LANES)
        for x in range(own_x):
            codes_ref[
                pl.ds(half * padded_nodes + n_x + x + 1, own_y, stride=n_x), :
            ] = code_ref[x, :, lanes]
    planes_ref[:, pl.ds(padded_nodes, LANES - padded_nodes), :] = jnp.zeros(
        (planes_ref.shape[0], LANES - padded_nodes, LANES), F32
    )
    for index, (dx, dy) in enumerate(DIRECTIONS):

        @pl.when(valid[index])
        def _(index=index):
            code_copy(opposite[index]).wait_recv()

        x = 0 if dx < 0 else n_x - 1
        y = 0 if dy < 0 else n_y - 1
        for half in range(halves):
            base = half * padded_nodes
            rows = pl.ds(half * own_y, own_y)
            if dy == 0:
                codes_ref[pl.ds(base + n_x + x, own_y, stride=n_x), :] = recv_code[
                    index, rows, :
                ]
            elif dx == 0:
                codes_ref[pl.ds(base + y * n_x + 1, own_x), :] = recv_code[
                    index, pl.ds(half * own_y, own_x), :
                ]
            else:
                codes_ref[pl.ds(base + y * n_x + x, 1), :] = recv_code[
                    index, pl.ds(half * own_y, 1), :
                ]

    take_face(0)
    take_face(1)
    send_face(4)
    send_face(5)

    groups = padded_nodes // SUB

    def update(half, group):
        base = half * plane + group * (SUB * SUB)
        channels = [
            node_ref[pl.ds(base + c, SUB, stride=SUB), :] for c in range(SUB)
        ]
        row = half * padded_nodes + group * SUB
        code = codes_ref[pl.ds(pl.multiple_of(row, SUB), SUB), :]
        shifted = code + (code >= 13).astype(jnp.int32)
        normal = [shifted // 9 - 1, shifted // 3 % 3 - 1, shifted % 3 - 1]
        normal = [n.astype(F32) for n in normal]
        length = jnp.sqrt(
            normal[0] * normal[0] + normal[1] * normal[1] + normal[2] * normal[2]
        )
        normal = [n / length for n in normal]
        masses = [channels[0], channels[4]]
        momenta = [channels[1:4], channels[5:8]]
        gravity = [0.0, 0.0, DT * GRAVITY]
        speeds = [
            [p / jnp.maximum(masses[f], FLOOR) + gravity[r] for r, p in enumerate(momenta[f])]
            for f in range(2)
        ]
        both = jnp.maximum(masses[0] + masses[1], FLOOR)
        center = [
            (momenta[0][r] + momenta[1][r]) / both + gravity[r] for r in range(3)
        ]
        share = jnp.minimum(1.0, jnp.minimum(masses[0], masses[1]) / FLOOR)
        closing = [
            share
            * jnp.maximum(
                sum((speeds[0][r] - center[r]) * normal[r] for r in range(3)), 0.0
            ),
            share
            * jnp.maximum(
                sum((center[r] - speeds[1][r]) * normal[r] for r in range(3)), 0.0
            ),
        ]
        node = group * SUB + lax.broadcasted_iota(jnp.int32, (SUB, LANES), 0)
        x = me_x * own_x + node % n_x
        y = me_y * own_y + node // n_x
        inside = (x >= 1) & (x <= size_x * own_x) & (y >= 1) & (y <= size_y * own_y)
        rows = pl.ds(pl.multiple_of(group * SUB, SUB), SUB)
        for f, sign in ((0, -1.0), (1, 1.0)):
            for r in range(3):
                speed = speeds[f][r] + sign * closing[f] * normal[r]
                planes_ref[half * 6 + 3 * f + r, rows, :] = jnp.where(inside, speed, 0.0)

    def update_groups(first, count):
        def body(step, carry):
            update(step // count, first + step % count)
            return carry

        lax.fori_loop(0, halves * count, body, 0)

    early = -(-2 * n_x // SUB)
    late = (n_y - 2) * n_x // SUB
    update_groups(early, late - early)
    for face in (2, 3, 4, 5):
        take_face(face)
    update_groups(0, early)
    update_groups(late, groups - late)
    edge = jnp.zeros((SUB, LANES), F32)
    depth = halves * LANES
    speed_ref[pl.ds(0, SUB), :] = edge
    speed_ref[pl.ds((depth + 1) * SUB, SUB), :] = edge
    for half in range(halves):
        for c in range(6):
            channel = c // 3 * 4 + c % 3
            speed_ref[
                pl.ds((1 + half * LANES) * SUB + channel, LANES, stride=SUB), :
            ] = planes_ref[half * 6 + c].T
        for channel in (3, 7):
            speed_ref[
                pl.ds((1 + half * LANES) * SUB + channel, LANES, stride=SUB), :
            ] = jnp.zeros((LANES, LANES), F32)

    for index in range(8):

        @pl.when(valid[index])
        def _(index=index):
            code_copy(index).wait_send()

    for face in range(6):

        @pl.when(face_valid(face))
        def _(face=face):
            face_copy(face).wait_send()


def gather_kernel(
    shape,
    tile_ref,
    count_ref,
    speed_ref,
    offset_ref,
    deform_ref,
    cell_ref,
    body_ref,
    new_velocity_ref,
    new_affine_ref,
    new_deform_ref,
    new_stress_ref,
    result_ref,
    rows_ref,
):
    n_x, padded_nodes, tiles, unroll = shape
    blocks = cell_ref.shape[0]
    store_rows(rows_ref, blocks, offset_ref, cell_ref)
    coordinates = node_coordinates(n_x, padded_nodes)

    def block_speeds(block):
        tile = tile_ref[block]
        planes = plane_weights(rows_ref, blocks, block, tile, tiles, coordinates)
        start = pl.multiple_of(tile % tiles[1] * (TILE_Z * SUB), SUB)
        speeds = speed_ref[pl.ds(start, SPAN_Z * SUB), :]
        left_high, left_low = split(speeds)
        right_high, right_low = split(jnp.concatenate(planes, 1))
        product = jnp.dot(
            jnp.concatenate([left_high, left_low, left_high], 1),
            jnp.concatenate([right_high, right_high, right_low], 0),
            preferred_element_type=F32,
        )
        sums = [jnp.zeros((SUB, LANES), F32) for _ in range(4)]
        for k in range(SPAN_Z):
            weight = rows_ref[pl.ds((14 + k) * blocks + block, 1), :]
            moment = rows_ref[pl.ds((14 + SPAN_Z + k) * blocks + block, 1), :]
            rows = [product[k * SUB : (k + 1) * SUB, v * LANES : (v + 1) * LANES] for v in range(3)]
            sums[0] = sums[0] + rows[0] * weight
            sums[1] = sums[1] + rows[1] * weight
            sums[2] = sums[2] + rows[2] * weight
            sums[3] = sums[3] + rows[0] * moment
        return sums

    def step(index, carry):
        members = [index * unroll + u for u in range(unroll)]
        results = [block_speeds(block) for block in members]
        for block, sums in zip(members, results):
            for v in range(4):
                start = pl.multiple_of(v * blocks * SUB + block * SUB, SUB)
                result_ref[pl.ds(start, SUB), :] = sums[v]
        return carry

    lax.fori_loop(0, blocks // unroll, step, 0)
    slot = lax.broadcasted_iota(jnp.int32, cell_ref.shape, 0)
    live = slot < count_ref[0, 0]
    even = body_ref[...] % 2 == 0

    def take(v, r):
        fields = [
            result_ref[pl.ds(v * blocks * SUB + 4 * f + r, blocks, stride=SUB), :]
            for f in range(2)
        ]
        return jnp.where(live, jnp.where(even, fields[0], fields[1]), 0.0)

    for r in range(3):
        new_velocity_ref[r] = take(0, r)
    affine = [4.0 * take(1 + c, r) for r in range(3) for c in range(3)]
    deform = [deform_ref[i] for i in range(9)]
    moved = []
    for r in range(3):
        for c in range(3):
            entry = deform[3 * r + c]
            for i in range(3):
                entry = entry + DT * affine[3 * r + i] * deform[3 * i + c]
            moved.append(jnp.where(live, entry, 0.0))
    for i in range(9):
        new_affine_ref[i] = affine[i]
        new_deform_ref[i] = moved[i]
    for i, entry in enumerate(kirchhoff(moved)):
        new_stress_ref[i] = jnp.where(live, entry, 0.0)


def per_device(
    offset,
    particle_mass,
    velocity,
    affine,
    deform,
    particle_cell,
    body_id,
    slot_tile_number,
    block_count,
    normal_code,
):
    blocks, particles = particle_mass.shape
    own_x, own_y, depth = normal_code.shape
    tiles = (own_y // TILE_Y, depth // TILE_Z)
    n_x, n_y = own_x + 2, own_y + 2
    padded_nodes = -(-n_x * n_y // SUB) * SUB
    halves = depth // LANES
    assert particles == LANES and padded_nodes <= LANES and depth % LANES == 0
    unroll = 2 if blocks % 2 == 0 else 1
    assert own_x == own_y and max(blocks, tiles[1]) <= LANES
    vmem = pl.BlockSpec(memory_space=pltpu.VMEM)
    smem = pl.BlockSpec(memory_space=pltpu.SMEM)
    limit = 40 * 1024 * 1024
    grid_shape = jax.ShapeDtypeStruct(((depth + 2) * SUB, LANES), F32)
    work = (n_x, padded_nodes, tiles, unroll)
    operands = (offset, particle_mass, velocity, affine, deform, particle_cell, body_id)
    operands = operands + (normal_code,)
    faces = [
        pltpu.VMEM(
            (halves * SUB * sum(count for _, count in face_runs(*face, n_x, n_y)), LANES), F32
        )
        for face in FACES
    ]
    dma = pltpu.SemaphoreType.DMA
    speeds = pl.pallas_call(
        functools.partial(
            nodes_kernel, (n_x, n_y, padded_nodes, halves, tiles, unroll)
        ),
        out_shape=grid_shape,
        in_specs=[smem, smem] + [pl.BlockSpec(memory_space=pltpu.HBM)] * 8,
        out_specs=vmem,
        scratch_shapes=[pltpu.VMEM(a.shape, a.dtype) for a in operands]
        + [
            pltpu.VMEM((4 * blocks * SUB, LANES), F32),
            pltpu.VMEM((N_ROWS * blocks, LANES), F32),
            pltpu.VMEM((blocks + 1, SPAN_Z * SUB, LANES), F32),
            pltpu.VMEM(grid_shape.shape, F32),
            pltpu.VMEM((SUB, LANES), jnp.int32),
            pltpu.SMEM((SUB, LANES), jnp.int32),
            pltpu.VMEM((halves * padded_nodes * SUB, LANES), F32),
            pltpu.VMEM((halves * padded_nodes, LANES), jnp.int32),
            pltpu.VMEM((halves * 6, LANES, LANES), F32),
            pltpu.VMEM((8, halves * own_y, LANES), jnp.int32),
            pltpu.VMEM((8, halves * own_y, LANES), jnp.int32),
        ]
        + faces
        + faces
        + [dma((6,)), dma((6,)), dma((8,)), dma((8,)), dma((8,)), dma(())],
        compiler_params=pltpu.CompilerParams(
            collective_id=0, has_side_effects=True, vmem_limit_bytes=limit
        ),
        name="particles_to_node_speeds",
    )(slot_tile_number, block_count, *operands)
    shaped = lambda n: jax.ShapeDtypeStruct((n, blocks, LANES), F32)
    return pl.pallas_call(
        functools.partial(gather_kernel, work),
        out_shape=(shaped(3), shaped(9), shaped(9), shaped(6)),
        in_specs=[smem, smem] + [vmem] * 5,
        out_specs=(vmem,) * 4,
        scratch_shapes=[
            pltpu.VMEM((4 * blocks * SUB, LANES), F32),
            pltpu.VMEM((N_ROWS * blocks, LANES), F32),
        ],
        compiler_params=pltpu.CompilerParams(vmem_limit_bytes=limit),
        name="nodes_to_particles",
    )(slot_tile_number, block_count, speeds, offset, deform, particle_cell, body_id)


def solution(mesh):
    particle = P(None, ("gx", "gy"), None)
    flat = P(("gx", "gy"), None)
    placed = (
        particle,
        flat,
        particle,
        particle,
        particle,
        flat,
        flat,
        P(("gx", "gy")),
        P("gx", "gy"),
        P("gx", "gy", None),
    )
    return jax.shard_map(
        per_device,
        mesh=mesh,
        in_specs=placed,
        out_specs=(particle,) * 4,
        check_vma=False,
    )
```

```python
import functools

import jax
import jax.numpy as jnp
from jax import lax
from jax.experimental import pallas as pl
from jax.experimental.pallas import tpu as pltpu
from jax.sharding import PartitionSpec as P

DT = 0.1
MU = 2.0
LAM = 3.0
GRAVITY = -2.0
FLOOR = 0.25
LANES = 128
SUB = 8
TILE_X, TILE_Y, TILE_Z = 4, 4, 8
SPAN_Z = TILE_Z + 2
MESH = pl.DeviceIdType.MESH
F32 = jnp.float32
BF16 = jnp.bfloat16
SIDES = [(-1, 0), (1, 0), (0, -1), (0, 1)]
DIRECTIONS = [(-1, 0), (1, 0), (0, -1), (0, 1), (-1, -1), (-1, 1), (1, -1), (1, 1)]


def spline_weights(fraction):
    return [
        0.5 * (1.5 - fraction) * (1.5 - fraction),
        0.75 - (fraction - 1.0) * (fraction - 1.0),
        0.5 * (fraction - 0.5) * (fraction - 0.5),
    ]


def determinant(m):
    return (
        m[0] * (m[4] * m[8] - m[5] * m[7])
        - m[1] * (m[3] * m[8] - m[5] * m[6])
        + m[2] * (m[3] * m[7] - m[4] * m[6])
    )


def kirchhoff(m):
    ratio = determinant(m)
    pressure = 0.5 * LAM * (ratio * ratio - 1.0)

    def dot(r, c):
        return m[3 * r] * m[3 * c] + m[3 * r + 1] * m[3 * c + 1] + m[3 * r + 2] * m[3 * c + 2]

    return [MU * (dot(r, r) - 1.0) + pressure for r in range(3)] + [
        MU * dot(0, 1),
        MU * dot(0, 2),
        MU * dot(1, 2),
    ]


SYMMETRIC = [0, 3, 4, 3, 1, 5, 4, 5, 2]


def split(value):
    high = value.astype(BF16)
    return high, (value - high.astype(F32)).astype(BF16)


def store_rows(rows_ref, blocks, offset_ref, cell_ref):
    cell = cell_ref[...]
    cells = [cell // (TILE_Y * TILE_Z), cell // TILE_Z % TILE_Y, cell % TILE_Z]
    rows = []
    for axis in range(2):
        fraction = offset_ref[axis]
        weights = spline_weights(fraction)
        rows.append(cells[axis].astype(F32))
        rows.extend(weights)
        rows.extend(weights[step] * (step - fraction) for step in range(3))
    fraction = offset_ref[2]
    weights = spline_weights(fraction)
    moments = [weights[step] * (step - fraction) for step in range(3)]
    for values in (weights, moments):
        for k in range(SPAN_Z):
            total = jnp.zeros_like(fraction)
            for step in range(3):
                total = jnp.where(cells[2] == k - step, values[step], total)
            rows.append(total)
    for index, row in enumerate(rows):
        rows_ref[pl.ds(index * blocks, blocks), :] = row


N_ROWS = 14 + 2 * SPAN_Z


def node_coordinates(n_x, padded_nodes):
    node = lax.broadcasted_iota(jnp.int32, (padded_nodes, LANES), 0)
    return (node % n_x).astype(F32), (node // n_x).astype(F32)


def plane_weights(rows_ref, blocks, block, tile, tiles, coordinates):
    tiles_y, tiles_z = tiles
    tile_x = (tile // (tiles_y * tiles_z) * TILE_X).astype(F32)
    tile_y = (tile // tiles_z % tiles_y * TILE_Y).astype(F32)

    def row(index):
        return rows_ref[pl.ds(index * blocks + block, 1), :]

    parts = []
    for axis, corner in enumerate((tile_x, tile_y)):
        first = 7 * axis
        step = coordinates[axis] - (row(first) + corner)
        hits = [step == float(s) for s in range(3)]
        for shift in (1, 4):
            total = jnp.zeros_like(step)
            for s in range(3):
                total = jnp.where(hits[s], row(first + shift + s), total)
            parts.append(total)
    weight_x, moment_x, weight_y, moment_y = parts
    out = [weight_x * weight_y, moment_x * weight_y, weight_x * moment_y]
    pad = jnp.zeros((LANES - coordinates[0].shape[0], LANES), F32)
    return [jnp.concatenate([p, pad], 0) for p in out]


def face_runs(kind, side, n_x, n_y):
    if kind == "x":
        first = 0 if side < 0 else n_x - 2
        return [(y * n_x + first, 2) for y in range(n_y)]
    layers = (0, 1) if side < 0 else (n_y - 2, n_y - 1)
    if kind == "inner":
        return [(y * n_x + 2, n_x - 4) for y in layers]
    return [(y * n_x + first, 2) for y in layers for first in (0, n_x - 2)]


FACES = [("x", -1), ("x", 1), ("inner", -1), ("inner", 1), ("outer", -1), ("outer", 1)]


def nodes_kernel(
    shape,
    tile_ref,
    count_ref,
    offset_hbm,
    mass_hbm,
    velocity_hbm,
    affine_hbm,
    deform_hbm,
    cell_hbm,
    body_hbm,
    code_hbm,
    result_ref,
    *scratch,
):
    n_x, n_y, padded_nodes, halves, tiles, unroll = shape
    inputs = scratch[:8]
    offset_ref, mass_ref, velocity_ref, affine_ref, deform_ref = inputs[:5]
    cell_ref, body_ref, code_ref = inputs[5:]
    (
        source_ref,
        rows_ref,
        chain_ref,
        grid_ref,
        table_ref,
        links,
        node_ref,
        codes_ref,
        planes_ref,
        send_code,
        recv_code,
        speed_ref,
        high_ref,
        low_ref,
    ) = scratch[8:22]
    sends = scratch[22:28]
    recvs = scratch[28:34]
    send_sem, recv_sem, code_send_sem, code_recv_sem, in_sem, table_sem = scratch[34:]
    blocks = mass_ref.shape[0]
    size_x, size_y = lax.axis_size("gx"), lax.axis_size("gy")
    me_x, me_y = lax.axis_index("gx"), lax.axis_index("gy")
    own_x, own_y = n_x - 2, n_y - 2

    hbm = (
        offset_hbm,
        mass_hbm,
        velocity_hbm,
        affine_hbm,
        deform_hbm,
        cell_hbm,
        body_hbm,
        code_hbm,
    )
    loads = [
        pltpu.make_async_copy(source, target, in_sem.at[i])
        for i, (source, target) in enumerate(zip(hbm, inputs))
    ]
    for load in loads:
        load.start()

    valid = []
    for dx, dy in DIRECTIONS:
        ok = None
        for d, me, size in ((dx, me_x, size_x), (dy, me_y, size_y)):
            if d == 0:
                continue
            one = me > 0 if d < 0 else me < size - 1
            ok = one if ok is None else jnp.logical_and(ok, one)
        valid.append(ok)
    barrier = pltpu.get_barrier_semaphore()

    def target(index):
        dx, dy = DIRECTIONS[index]
        return {"gx": me_x + dx, "gy": me_y + dy}

    for index in range(8):

        @pl.when(valid[index])
        def _(index=index):
            pl.semaphore_signal(
                barrier, inc=1, device_id=target(index), device_id_type=MESH
            )

    opposite = [DIRECTIONS.index((-dx, -dy)) for dx, dy in DIRECTIONS]
    plane = padded_nodes * SUB

    lane = lax.broadcasted_iota(jnp.int32, (SUB, LANES), 1)
    heights = [tile_ref[s] % tiles[1] for s in range(blocks)]
    height = jnp.full((SUB, LANES), -1, jnp.int32)
    for s in range(blocks):
        height = jnp.where(lane == s, heights[s], height)
    before = jnp.zeros((SUB, LANES), jnp.int32)
    last = jnp.zeros((SUB, LANES), jnp.int32)
    for s in range(blocks):
        before = jnp.where((height == heights[s]) & (lane > s), s + 1, before)
        last = jnp.where(lane == heights[s], s + 1, last)
    sublane = lax.broadcasted_iota(jnp.int32, (SUB, LANES), 0)
    table_ref[...] = jnp.where(sublane == 0, before, last)
    table_copy = pltpu.make_async_copy(table_ref, links, table_sem)
    table_copy.start()

    for load in loads[:7]:
        load.wait()
    slot = lax.broadcasted_iota(jnp.int32, mass_ref.shape, 0)
    mass = jnp.where(slot < count_ref[0, 0], mass_ref[...], 0.0)
    even = body_ref[...] % 2 == 0
    masses = [jnp.where(even, mass, 0.0), jnp.where(even, 0.0, mass)]
    tau = kirchhoff([deform_ref[i] for i in range(9)])
    force = [affine_ref[i] - 4.0 * DT * tau[SYMMETRIC[i]] for i in range(9)]
    zero = jnp.zeros_like(mass)

    def put(group, channel, value):
        source_ref[pl.ds(group * blocks * SUB + channel, blocks, stride=SUB), :] = value

    for field in range(2):
        put(0, 4 * field, masses[field])
        for r in range(3):
            put(0, 4 * field + 1 + r, masses[field] * velocity_ref[r])
        for c in range(3):
            put(1 + c, 4 * field, zero)
            for r in range(3):
                put(1 + c, 4 * field + 1 + r, masses[field] * force[3 * r + c])
    store_rows(rows_ref, blocks, offset_ref, cell_ref)
    coordinates = node_coordinates(n_x, padded_nodes)
    span = SPAN_Z * SUB
    chain_ref[0] = jnp.zeros((span, LANES), F32)
    table_copy.wait()

    def block_sums(block):
        tile = tile_ref[block]
        planes = plane_weights(rows_ref, blocks, block, tile, tiles, coordinates)
        groups = [
            source_ref[
                pl.ds(pl.multiple_of(g * blocks * SUB + block * SUB, SUB), SUB), :
            ]
            for g in range(4)
        ]
        left = [[], [], []]
        for k in range(SPAN_Z):
            weight = rows_ref[pl.ds((14 + k) * blocks + block, 1), :]
            moment = rows_ref[pl.ds((14 + SPAN_Z + k) * blocks + block, 1), :]
            left[0].append(groups[0] * weight + groups[3] * moment)
            left[1].append(groups[1] * weight)
            left[2].append(groups[2] * weight)
        left = jnp.concatenate([jnp.concatenate(part, 0) for part in left], 1)
        right = jnp.concatenate(planes, 1)
        left_high, left_low = split(left)
        right_high, right_low = split(right)
        high_ref[block] = right_high
        low_ref[block] = right_low
        product = lax.dot_general(
            jnp.concatenate([left_high, left_low], 0),
            jnp.concatenate([right_high, right_low], 0),
            (((1,), (1,)), ((), ())),
            preferred_element_type=F32,
        )
        return product[:span, :LANES] + (product[:span, LANES:] + product[span:, :LANES])

    def step(index, carry):
        members = [index * unroll + u for u in range(unroll)]
        sums = [block_sums(block) for block in members]
        for block, patch in zip(members, sums):
            chain_ref[block + 1] = chain_ref[links[0, block]] + patch
        return carry

    lax.fori_loop(0, blocks // unroll, step, 0)

    loads[7].wait()
    for half in range(halves):
        lanes = pl.ds(half * LANES, LANES)
        rows = pl.ds(half * own_y, own_y)
        for index, (dx, dy) in enumerate(DIRECTIONS):
            x = 0 if dx < 0 else own_x - 1
            y = 0 if dy < 0 else own_y - 1
            if dy == 0:
                send_code[index, rows, :] = code_ref[x, :, lanes]
            elif dx == 0:
                for i in range(own_x):
                    send_code[index, pl.ds(half * own_y + i, 1), :] = code_ref[
                        i, pl.ds(y, 1), lanes
                    ]
            else:
                send_code[index, rows, :] = jnp.broadcast_to(
                    code_ref[x, pl.ds(y, 1), lanes], (own_y, LANES)
                )

    def code_copy(index):
        return pltpu.make_async_remote_copy(
            src_ref=send_code.at[index],
            dst_ref=recv_code.at[opposite[index]],
            send_sem=code_send_sem.at[index],
            recv_sem=code_recv_sem.at[opposite[index]],
            device_id=target(index),
            device_id_type=MESH,
        )

    def face_copy(face):
        return pltpu.make_async_remote_copy(
            src_ref=sends[face],
            dst_ref=recvs[face ^ 1],
            send_sem=send_sem.at[face],
            recv_sem=recv_sem.at[face ^ 1],
            device_id=target(min(face, 2 + face % 2)),
            device_id_type=MESH,
        )

    def face_valid(face):
        return valid[min(face, 2 + face % 2)]

    arrivals = sum(ok.astype(jnp.int32) for ok in valid)
    pl.semaphore_wait(barrier, arrivals)
    for index in range(8):

        @pl.when(valid[index])
        def _(index=index):
            code_copy(index).start()

        @pl.when(jnp.logical_not(valid[index]))
        def _(index=index):
            recv_code[index] = jnp.zeros(recv_code.shape[1:], jnp.int32)

    body_rows = TILE_Z * SUB
    over = span - body_rows

    def assemble(j, carry):
        patch = chain_ref[links[1, j]]
        rows = pl.multiple_of(j * body_rows, SUB)
        grid_ref[pl.ds(rows, over), :] = patch[:over] + carry
        grid_ref[pl.ds(rows + over, body_rows - over), :] = patch[over:body_rows]
        return patch[body_rows:]

    tail = lax.fori_loop(0, tiles[1], assemble, jnp.zeros((over, LANES), F32), unroll=4)
    grid_ref[pl.ds(tiles[1] * body_rows, over), :] = tail

    for half in range(halves):
        for c in range(SUB):
            part = grid_ref[pl.ds((1 + half * LANES) * SUB + c, LANES, stride=SUB), :]
            node_ref[pl.ds(half * plane + c, padded_nodes, stride=SUB), :] = part.T[
                :padded_nodes
            ]

    def each_run(face):
        offset = 0
        for half in range(halves):
            for first, count in face_runs(*FACES[face], n_x, n_y):
                yield (
                    pl.ds(half * plane + first * SUB, count * SUB),
                    pl.ds(offset, count * SUB),
                )
                offset += count * SUB

    def send_face(face):
        for nodes, run in each_run(face):
            sends[face][run, :] = node_ref[nodes, :]

        @pl.when(face_valid(face))
        def _():
            face_copy(face).start()

        @pl.when(jnp.logical_not(face_valid(face)))
        def _():
            recvs[face][...] = jnp.zeros_like(recvs[face])

    def take_face(face):
        @pl.when(face_valid(face))
        def _():
            face_copy(face ^ 1).wait_recv()

        for nodes, run in each_run(face):
            node_ref[nodes, :] = node_ref[nodes, :] + recvs[face][run, :]

    for face in (0, 1, 2, 3):
        send_face(face)

    codes_ref[...] = jnp.zeros_like(codes_ref)
    for half in range(halves):
        lanes = pl.ds(half * LANES, LANES)
        for x in range(own_x):
            codes_ref[
                pl.ds(half * padded_nodes + n_x + x + 1, own_y, stride=n_x), :
            ] = code_ref[x, :, lanes]
    planes_ref[:, pl.ds(padded_nodes, LANES - padded_nodes), :] = jnp.zeros(
        (planes_ref.shape[0], LANES - padded_nodes, LANES), F32
    )
    for index, (dx, dy) in enumerate(DIRECTIONS):

        @pl.when(valid[index])
        def _(index=index):
            code_copy(opposite[index]).wait_recv()

        x = 0 if dx < 0 else n_x - 1
        y = 0 if dy < 0 else n_y - 1
        for half in range(halves):
            base = half * padded_nodes
            rows = pl.ds(half * own_y, own_y)
            if dy == 0:
                codes_ref[pl.ds(base + n_x + x, own_y, stride=n_x), :] = recv_code[
                    index, rows, :
                ]
            elif dx == 0:
                codes_ref[pl.ds(base + y * n_x + 1, own_x), :] = recv_code[
                    index, pl.ds(half * own_y, own_x), :
                ]
            else:
                codes_ref[pl.ds(base + y * n_x + x, 1), :] = recv_code[
                    index, pl.ds(half * own_y, 1), :
                ]

    take_face(0)
    take_face(1)
    send_face(4)
    send_face(5)

    groups = padded_nodes // SUB

    def update(half, group):
        base = half * plane + group * (SUB * SUB)
        channels = [
            node_ref[pl.ds(base + c, SUB, stride=SUB), :] for c in range(SUB)
        ]
        row = half * padded_nodes + group * SUB
        code = codes_ref[pl.ds(pl.multiple_of(row, SUB), SUB), :]
        shifted = code + (code >= 13).astype(jnp.int32)
        normal = [shifted // 9 - 1, shifted // 3 % 3 - 1, shifted % 3 - 1]
        normal = [n.astype(F32) for n in normal]
        length = jnp.sqrt(
            normal[0] * normal[0] + normal[1] * normal[1] + normal[2] * normal[2]
        )
        normal = [n / length for n in normal]
        masses = [channels[0], channels[4]]
        momenta = [channels[1:4], channels[5:8]]
        gravity = [0.0, 0.0, DT * GRAVITY]
        speeds = [
            [p / jnp.maximum(masses[f], FLOOR) + gravity[r] for r, p in enumerate(momenta[f])]
            for f in range(2)
        ]
        both = jnp.maximum(masses[0] + masses[1], FLOOR)
        center = [
            (momenta[0][r] + momenta[1][r]) / both + gravity[r] for r in range(3)
        ]
        share = jnp.minimum(1.0, jnp.minimum(masses[0], masses[1]) / FLOOR)
        closing = [
            share
            * jnp.maximum(
                sum((speeds[0][r] - center[r]) * normal[r] for r in range(3)), 0.0
            ),
            share
            * jnp.maximum(
                sum((center[r] - speeds[1][r]) * normal[r] for r in range(3)), 0.0
            ),
        ]
        node = group * SUB + lax.broadcasted_iota(jnp.int32, (SUB, LANES), 0)
        x = me_x * own_x + node % n_x
        y = me_y * own_y + node // n_x
        inside = (x >= 1) & (x <= size_x * own_x) & (y >= 1) & (y <= size_y * own_y)
        rows = pl.ds(pl.multiple_of(group * SUB, SUB), SUB)
        for f, sign in ((0, -1.0), (1, 1.0)):
            for r in range(3):
                speed = speeds[f][r] + sign * closing[f] * normal[r]
                planes_ref[half * 6 + 3 * f + r, rows, :] = jnp.where(inside, speed, 0.0)

    def update_groups(first, count):
        def body(step, carry):
            update(step // count, first + step % count)
            return carry

        lax.fori_loop(0, halves * count, body, 0)

    early = -(-2 * n_x // SUB)
    late = (n_y - 2) * n_x // SUB
    update_groups(early, late - early)
    for face in (2, 3, 4, 5):
        take_face(face)
    update_groups(0, early)
    update_groups(late, groups - late)
    edge = jnp.zeros((SUB, LANES), F32)
    depth = halves * LANES
    grid_ref[pl.ds(0, SUB), :] = edge
    grid_ref[pl.ds((depth + 1) * SUB, SUB), :] = edge
    for half in range(halves):
        for c in range(6):
            channel = c // 3 * 4 + c % 3
            grid_ref[
                pl.ds((1 + half * LANES) * SUB + channel, LANES, stride=SUB), :
            ] = planes_ref[half * 6 + c].T
    for j in range(tiles[1]):
        speed_ref[j] = grid_ref[pl.ds(j * body_rows, body_rows), :]
    speed_ref[tiles[1], pl.ds(0, over), :] = grid_ref[pl.ds(tiles[1] * body_rows, over), :]

    def block_speeds(block):
        at = tile_ref[block] % tiles[1]
        speeds = jnp.concatenate([speed_ref[at], speed_ref[at + 1][:over]], 0)
        left_high, left_low = split(speeds)
        right_high, right_low = high_ref[block], low_ref[block]
        product = jnp.dot(
            jnp.concatenate([left_high, left_low, left_high], 1),
            jnp.concatenate([right_high, right_high, right_low], 0),
            preferred_element_type=F32,
        )
        sums = [jnp.zeros((SUB, LANES), F32) for _ in range(4)]
        for k in range(SPAN_Z):
            weight = rows_ref[pl.ds((14 + k) * blocks + block, 1), :]
            moment = rows_ref[pl.ds((14 + SPAN_Z + k) * blocks + block, 1), :]
            rows = [product[k * SUB : (k + 1) * SUB, v * LANES : (v + 1) * LANES] for v in range(3)]
            sums[0] = sums[0] + rows[0] * weight
            sums[1] = sums[1] + rows[1] * weight
            sums[2] = sums[2] + rows[2] * weight
            sums[3] = sums[3] + rows[0] * moment
        return sums

    def gather_step(index, carry):
        members = [index * unroll + u for u in range(unroll)]
        results = [block_speeds(block) for block in members]
        for block, sums in zip(members, results):
            for v in range(4):
                start = pl.multiple_of(v * blocks * SUB + block * SUB, SUB)
                result_ref[pl.ds(start, SUB), :] = sums[v]
        return carry

    lax.fori_loop(0, blocks // unroll, gather_step, 0)

    for index in range(8):

        @pl.when(valid[index])
        def _(index=index):
            code_copy(index).wait_send()

    for face in range(6):

        @pl.when(face_valid(face))
        def _(face=face):
            face_copy(face).wait_send()


def particle_kernel(
    count_ref,
    result_hbm,
    deform_hbm,
    body_hbm,
    new_velocity_hbm,
    new_affine_hbm,
    new_deform_hbm,
    new_stress_hbm,
    result_ref,
    deform_ref,
    body_ref,
    new_velocity_ref,
    new_affine_ref,
    new_deform_ref,
    new_stress_ref,
    in_sem,
    out_sem,
):
    pairs = ((result_hbm, result_ref), (deform_hbm, deform_ref), (body_hbm, body_ref))
    loads = [
        pltpu.make_async_copy(source, target, in_sem.at[i])
        for i, (source, target) in enumerate(pairs)
    ]
    for load in loads:
        load.start()
    pairs = (
        (new_velocity_ref, new_velocity_hbm),
        (new_affine_ref, new_affine_hbm),
        (new_deform_ref, new_deform_hbm),
        (new_stress_ref, new_stress_hbm),
    )
    stores = [
        pltpu.make_async_copy(source, target, out_sem.at[i])
        for i, (source, target) in enumerate(pairs)
    ]
    for load in loads:
        load.wait()
    blocks = body_ref.shape[0]
    slot = lax.broadcasted_iota(jnp.int32, body_ref.shape, 0)
    live = slot < count_ref[0, 0]
    even = body_ref[...] % 2 == 0

    def take(v, r):
        fields = [
            result_ref[pl.ds(v * blocks * SUB + 4 * f + r, blocks, stride=SUB), :]
            for f in range(2)
        ]
        return jnp.where(live, jnp.where(even, fields[0], fields[1]), 0.0)

    for r in range(3):
        new_velocity_ref[r] = take(0, r)
    stores[0].start()
    affine = [4.0 * take(1 + c, r) for r in range(3) for c in range(3)]
    deform = [deform_ref[i] for i in range(9)]
    moved = []
    for r in range(3):
        for c in range(3):
            entry = deform[3 * r + c]
            for i in range(3):
                entry = entry + DT * affine[3 * r + i] * deform[3 * i + c]
            moved.append(jnp.where(live, entry, 0.0))
    for i in range(9):
        new_affine_ref[i] = affine[i]
    stores[1].start()
    for i in range(9):
        new_deform_ref[i] = moved[i]
    stores[2].start()
    for i, entry in enumerate(kirchhoff(moved)):
        new_stress_ref[i] = jnp.where(live, entry, 0.0)
    stores[3].start()
    for store in stores:
        store.wait()


def per_device(
    offset,
    particle_mass,
    velocity,
    affine,
    deform,
    particle_cell,
    body_id,
    slot_tile_number,
    block_count,
    normal_code,
):
    blocks, particles = particle_mass.shape
    own_x, own_y, depth = normal_code.shape
    tiles = (own_y // TILE_Y, depth // TILE_Z)
    n_x, n_y = own_x + 2, own_y + 2
    padded_nodes = -(-n_x * n_y // SUB) * SUB
    halves = depth // LANES
    assert particles == LANES and padded_nodes <= LANES and depth % LANES == 0
    unroll = 2 if blocks % 2 == 0 else 1
    assert own_x == own_y and max(blocks, tiles[1]) <= LANES
    vmem = pl.BlockSpec(memory_space=pltpu.VMEM)
    smem = pl.BlockSpec(memory_space=pltpu.SMEM)
    hbm = pl.BlockSpec(memory_space=pltpu.HBM)
    result_shape = jax.ShapeDtypeStruct((4 * blocks * SUB, LANES), F32)
    operands = (offset, particle_mass, velocity, affine, deform, particle_cell, body_id)
    operands = operands + (normal_code,)
    faces = [
        pltpu.VMEM(
            (halves * SUB * sum(count for _, count in face_runs(*face, n_x, n_y)), LANES), F32
        )
        for face in FACES
    ]
    dma = pltpu.SemaphoreType.DMA
    result = pl.pallas_call(
        functools.partial(
            nodes_kernel, (n_x, n_y, padded_nodes, halves, tiles, unroll)
        ),
        out_shape=result_shape,
        in_specs=[smem, smem] + [hbm] * 8,
        out_specs=vmem,
        scratch_shapes=[pltpu.VMEM(a.shape, a.dtype) for a in operands]
        + [
            pltpu.VMEM((4 * blocks * SUB, LANES), F32),
            pltpu.VMEM((N_ROWS * blocks, LANES), F32),
            pltpu.VMEM((blocks + 1, SPAN_Z * SUB, LANES), F32),
            pltpu.VMEM(((depth + 2) * SUB, LANES), F32),
            pltpu.VMEM((SUB, LANES), jnp.int32),
            pltpu.SMEM((SUB, LANES), jnp.int32),
            pltpu.VMEM((halves * padded_nodes * SUB, LANES), F32),
            pltpu.VMEM((halves * padded_nodes, LANES), jnp.int32),
            pltpu.VMEM((halves * 6, LANES, LANES), F32),
            pltpu.VMEM((8, halves * own_y, LANES), jnp.int32),
            pltpu.VMEM((8, halves * own_y, LANES), jnp.int32),
            pltpu.VMEM((tiles[1] + 1, TILE_Z * SUB, LANES), F32),
            pltpu.VMEM((blocks, LANES, 3 * LANES), BF16),
            pltpu.VMEM((blocks, LANES, 3 * LANES), BF16),
        ]
        + faces
        + faces
        + [dma((6,)), dma((6,)), dma((8,)), dma((8,)), dma((8,)), dma(())],
        compiler_params=pltpu.CompilerParams(collective_id=0, has_side_effects=True),
        name="nodes_step",
    )(slot_tile_number, block_count, *operands)
    shapes = [jax.ShapeDtypeStruct((n, blocks, LANES), F32) for n in (3, 9, 9, 6)]
    return pl.pallas_call(
        particle_kernel,
        out_shape=tuple(shapes),
        in_specs=[smem] + [hbm] * 3,
        out_specs=(hbm,) * 4,
        scratch_shapes=[
            pltpu.VMEM(result_shape.shape, F32),
            pltpu.VMEM(deform.shape, F32),
            pltpu.VMEM(body_id.shape, jnp.int32),
        ]
        + [pltpu.VMEM(a.shape, F32) for a in shapes]
        + [dma((3,)), dma((4,))],
        name="particles_step",
    )(block_count, result, deform, body_id)


def solution(mesh):
    particle = P(None, ("gx", "gy"), None)
    flat = P(("gx", "gy"), None)
    placed = (
        particle,
        flat,
        particle,
        particle,
        particle,
        flat,
        flat,
        P(("gx", "gy")),
        P("gx", "gy"),
        P("gx", "gy", None),
    )
    return jax.shard_map(
        per_device,
        mesh=mesh,
        in_specs=placed,
        out_specs=(particle,) * 4,
        check_vma=False,
    )
```

```python
import functools

import jax
import jax.numpy as jnp
from jax import lax
from jax.experimental import pallas as pl
from jax.experimental.pallas import tpu as pltpu
from jax.sharding import PartitionSpec as P

DT = 0.1
MU = 2.0
LAM = 3.0
GRAVITY = -2.0
FLOOR = 0.25
LANES = 128
SUB = 8
TILE_X, TILE_Y, TILE_Z = 4, 4, 8
SPAN_Z = TILE_Z + 2
MESH = pl.DeviceIdType.MESH
F32 = jnp.float32
BF16 = jnp.bfloat16
SIDES = [(-1, 0), (1, 0), (0, -1), (0, 1)]
DIRECTIONS = [(-1, 0), (1, 0), (0, -1), (0, 1), (-1, -1), (-1, 1), (1, -1), (1, 1)]


def spline_weights(fraction):
    return [
        0.5 * (1.5 - fraction) * (1.5 - fraction),
        0.75 - (fraction - 1.0) * (fraction - 1.0),
        0.5 * (fraction - 0.5) * (fraction - 0.5),
    ]


def determinant(m):
    return (
        m[0] * (m[4] * m[8] - m[5] * m[7])
        - m[1] * (m[3] * m[8] - m[5] * m[6])
        + m[2] * (m[3] * m[7] - m[4] * m[6])
    )


def kirchhoff(m):
    ratio = determinant(m)
    pressure = 0.5 * LAM * (ratio * ratio - 1.0)

    def dot(r, c):
        return m[3 * r] * m[3 * c] + m[3 * r + 1] * m[3 * c + 1] + m[3 * r + 2] * m[3 * c + 2]

    return [MU * (dot(r, r) - 1.0) + pressure for r in range(3)] + [
        MU * dot(0, 1),
        MU * dot(0, 2),
        MU * dot(1, 2),
    ]


SYMMETRIC = [0, 3, 4, 3, 1, 5, 4, 5, 2]


def split(value):
    high = value.astype(BF16)
    return high, (value - high.astype(F32)).astype(BF16)


def store_rows(rows_ref, blocks, offset_ref, cell_ref):
    cell = cell_ref[...]
    cells = [cell // (TILE_Y * TILE_Z), cell // TILE_Z % TILE_Y, cell % TILE_Z]
    rows = []
    for axis in range(2):
        fraction = offset_ref[axis]
        weights = spline_weights(fraction)
        rows.append(cells[axis].astype(F32))
        rows.extend(weights)
        rows.extend(weights[step] * (step - fraction) for step in range(3))
    fraction = offset_ref[2]
    weights = spline_weights(fraction)
    moments = [weights[step] * (step - fraction) for step in range(3)]
    for values in (weights, moments):
        for k in range(SPAN_Z):
            total = jnp.zeros_like(fraction)
            for step in range(3):
                total = jnp.where(cells[2] == k - step, values[step], total)
            rows.append(total)
    for index, row in enumerate(rows):
        rows_ref[pl.ds(index * blocks, blocks), :] = row


N_ROWS = 14 + 2 * SPAN_Z


def node_coordinates(n_x, padded_nodes):
    node = lax.broadcasted_iota(jnp.int32, (padded_nodes, LANES), 0)
    return (node % n_x).astype(F32), (node // n_x).astype(F32)


def plane_weights(rows_ref, blocks, block, tile, tiles, coordinates):
    tiles_y, tiles_z = tiles
    tile_x = (tile // (tiles_y * tiles_z) * TILE_X).astype(F32)
    tile_y = (tile // tiles_z % tiles_y * TILE_Y).astype(F32)

    def row(index):
        return rows_ref[pl.ds(index * blocks + block, 1), :]

    parts = []
    for axis, corner in enumerate((tile_x, tile_y)):
        first = 7 * axis
        step = coordinates[axis] - (row(first) + corner)
        hits = [step == float(s) for s in range(3)]
        for shift in (1, 4):
            total = jnp.zeros_like(step)
            for s in range(3):
                total = jnp.where(hits[s], row(first + shift + s), total)
            parts.append(total)
    weight_x, moment_x, weight_y, moment_y = parts
    out = [weight_x * weight_y, moment_x * weight_y, weight_x * moment_y]
    pad = jnp.zeros((LANES - coordinates[0].shape[0], LANES), F32)
    return [jnp.concatenate([p, pad], 0) for p in out]


def face_runs(kind, side, n_x, n_y):
    if kind == "x":
        first = 0 if side < 0 else n_x - 2
        return [(y * n_x + first, 2) for y in range(n_y)]
    layers = (0, 1) if side < 0 else (n_y - 2, n_y - 1)
    if kind == "inner":
        return [(y * n_x + 2, n_x - 4) for y in layers]
    return [(y * n_x + first, 2) for y in layers for first in (0, n_x - 2)]


FACES = [("x", -1), ("x", 1), ("inner", -1), ("inner", 1), ("outer", -1), ("outer", 1)]


def nodes_kernel(
    shape,
    tile_ref,
    count_ref,
    offset_hbm,
    mass_hbm,
    velocity_hbm,
    affine_hbm,
    deform_hbm,
    cell_hbm,
    body_hbm,
    code_hbm,
    result_ref,
    *scratch,
):
    n_x, n_y, padded_nodes, halves, tiles, unroll = shape
    inputs = scratch[:8]
    offset_ref, mass_ref, velocity_ref, affine_ref, deform_ref = inputs[:5]
    cell_ref, body_ref, code_ref = inputs[5:]
    (
        source_ref,
        rows_ref,
        chain_ref,
        grid_ref,
        table_ref,
        links,
        node_ref,
        codes_ref,
        planes_ref,
        send_code,
        recv_code,
        speed_ref,
        high_ref,
        low_ref,
    ) = scratch[8:22]
    sends = scratch[22:28]
    recvs = scratch[28:34]
    send_sem, recv_sem, code_send_sem, code_recv_sem, in_sem, table_sem = scratch[34:]
    blocks = mass_ref.shape[0]
    size_x, size_y = lax.axis_size("gx"), lax.axis_size("gy")
    me_x, me_y = lax.axis_index("gx"), lax.axis_index("gy")
    own_x, own_y = n_x - 2, n_y - 2

    hbm = (
        offset_hbm,
        mass_hbm,
        velocity_hbm,
        affine_hbm,
        deform_hbm,
        cell_hbm,
        body_hbm,
        code_hbm,
    )
    loads = [
        pltpu.make_async_copy(source, target, in_sem.at[i])
        for i, (source, target) in enumerate(zip(hbm, inputs))
    ]
    for load in loads:
        load.start()

    valid = []
    for dx, dy in DIRECTIONS:
        ok = None
        for d, me, size in ((dx, me_x, size_x), (dy, me_y, size_y)):
            if d == 0:
                continue
            one = me > 0 if d < 0 else me < size - 1
            ok = one if ok is None else jnp.logical_and(ok, one)
        valid.append(ok)
    barrier = pltpu.get_barrier_semaphore()

    def target(index):
        dx, dy = DIRECTIONS[index]
        return {"gx": me_x + dx, "gy": me_y + dy}

    for index in range(8):

        @pl.when(valid[index])
        def _(index=index):
            pl.semaphore_signal(
                barrier, inc=1, device_id=target(index), device_id_type=MESH
            )

    opposite = [DIRECTIONS.index((-dx, -dy)) for dx, dy in DIRECTIONS]
    plane = padded_nodes * SUB

    lane = lax.broadcasted_iota(jnp.int32, (SUB, LANES), 1)
    heights = [tile_ref[s] % tiles[1] for s in range(blocks)]
    height = jnp.full((SUB, LANES), -1, jnp.int32)
    for s in range(blocks):
        height = jnp.where(lane == s, heights[s], height)
    before = jnp.zeros((SUB, LANES), jnp.int32)
    last = jnp.zeros((SUB, LANES), jnp.int32)
    for s in range(blocks):
        before = jnp.where((height == heights[s]) & (lane > s), s + 1, before)
        last = jnp.where(lane == heights[s], s + 1, last)
    sublane = lax.broadcasted_iota(jnp.int32, (SUB, LANES), 0)
    table_ref[...] = jnp.where(sublane == 0, before, last)
    table_copy = pltpu.make_async_copy(table_ref, links, table_sem)
    table_copy.start()

    for load in loads[:7]:
        load.wait()
    slot = lax.broadcasted_iota(jnp.int32, mass_ref.shape, 0)
    mass = jnp.where(slot < count_ref[0, 0], mass_ref[...], 0.0)
    even = body_ref[...] % 2 == 0
    masses = [jnp.where(even, mass, 0.0), jnp.where(even, 0.0, mass)]
    tau = kirchhoff([deform_ref[i] for i in range(9)])
    force = [affine_ref[i] - 4.0 * DT * tau[SYMMETRIC[i]] for i in range(9)]
    zero = jnp.zeros_like(mass)

    def put(group, channel, value):
        source_ref[pl.ds(group * blocks * SUB + channel, blocks, stride=SUB), :] = value

    for field in range(2):
        put(0, 4 * field, masses[field])
        for r in range(3):
            put(0, 4 * field + 1 + r, masses[field] * velocity_ref[r])
        for c in range(3):
            put(1 + c, 4 * field, zero)
            for r in range(3):
                put(1 + c, 4 * field + 1 + r, masses[field] * force[3 * r + c])
    store_rows(rows_ref, blocks, offset_ref, cell_ref)
    coordinates = node_coordinates(n_x, padded_nodes)
    span = SPAN_Z * SUB
    chain_ref[0] = jnp.zeros((span, LANES), F32)
    table_copy.wait()

    def block_sums(block):
        tile = tile_ref[block]
        planes = plane_weights(rows_ref, blocks, block, tile, tiles, coordinates)
        groups = [
            source_ref[
                pl.ds(pl.multiple_of(g * blocks * SUB + block * SUB, SUB), SUB), :
            ]
            for g in range(4)
        ]
        left = [[], [], []]
        for k in range(SPAN_Z):
            weight = rows_ref[pl.ds((14 + k) * blocks + block, 1), :]
            moment = rows_ref[pl.ds((14 + SPAN_Z + k) * blocks + block, 1), :]
            left[0].append(groups[0] * weight + groups[3] * moment)
            left[1].append(groups[1] * weight)
            left[2].append(groups[2] * weight)
        left = jnp.concatenate([jnp.concatenate(part, 0) for part in left], 1)
        right = jnp.concatenate(planes, 1)
        left_high, left_low = split(left)
        right_high, right_low = split(right)
        high_ref[block] = right_high
        low_ref[block] = right_low
        product = lax.dot_general(
            jnp.concatenate([left_high, left_low], 0),
            jnp.concatenate([right_high, right_low], 0),
            (((1,), (1,)), ((), ())),
            preferred_element_type=F32,
        )
        return product[:span, :LANES] + (product[:span, LANES:] + product[span:, :LANES])

    def step(index, carry):
        members = [index * unroll + u for u in range(unroll)]
        sums = [block_sums(block) for block in members]
        for block, patch in zip(members, sums):
            chain_ref[block + 1] = chain_ref[links[0, block]] + patch
        return carry

    lax.fori_loop(0, blocks // unroll, step, 0)

    loads[7].wait()
    for half in range(halves):
        lanes = pl.ds(half * LANES, LANES)
        rows = pl.ds(half * own_y, own_y)
        for index, (dx, dy) in enumerate(DIRECTIONS):
            x = 0 if dx < 0 else own_x - 1
            y = 0 if dy < 0 else own_y - 1
            if dy == 0:
                send_code[index, rows, :] = code_ref[x, :, lanes]
            elif dx == 0:
                for i in range(own_x):
                    send_code[index, pl.ds(half * own_y + i, 1), :] = code_ref[
                        i, pl.ds(y, 1), lanes
                    ]
            else:
                send_code[index, rows, :] = jnp.broadcast_to(
                    code_ref[x, pl.ds(y, 1), lanes], (own_y, LANES)
                )

    def code_copy(index):
        return pltpu.make_async_remote_copy(
            src_ref=send_code.at[index],
            dst_ref=recv_code.at[opposite[index]],
            send_sem=code_send_sem.at[index],
            recv_sem=code_recv_sem.at[opposite[index]],
            device_id=target(index),
            device_id_type=MESH,
        )

    def face_copy(face):
        return pltpu.make_async_remote_copy(
            src_ref=sends[face],
            dst_ref=recvs[face ^ 1],
            send_sem=send_sem.at[face],
            recv_sem=recv_sem.at[face ^ 1],
            device_id=target(min(face, 2 + face % 2)),
            device_id_type=MESH,
        )

    def face_valid(face):
        return valid[min(face, 2 + face % 2)]

    arrivals = sum(ok.astype(jnp.int32) for ok in valid)
    pl.semaphore_wait(barrier, arrivals)
    for index in range(8):

        @pl.when(valid[index])
        def _(index=index):
            code_copy(index).start()

        @pl.when(jnp.logical_not(valid[index]))
        def _(index=index):
            recv_code[index] = jnp.zeros(recv_code.shape[1:], jnp.int32)

    body_rows = TILE_Z * SUB
    over = span - body_rows

    def assemble(j, carry):
        patch = chain_ref[links[1, j]]
        rows = pl.multiple_of(j * body_rows, SUB)
        grid_ref[pl.ds(rows, over), :] = patch[:over] + carry
        grid_ref[pl.ds(rows + over, body_rows - over), :] = patch[over:body_rows]
        return patch[body_rows:]

    tail = lax.fori_loop(0, tiles[1], assemble, jnp.zeros((over, LANES), F32), unroll=4)
    grid_ref[pl.ds(tiles[1] * body_rows, over), :] = tail

    for half in range(halves):
        for c in range(SUB):
            part = grid_ref[pl.ds((1 + half * LANES) * SUB + c, LANES, stride=SUB), :]
            node_ref[pl.ds(half * plane + c, padded_nodes, stride=SUB), :] = part.T[
                :padded_nodes
            ]

    def each_run(face):
        offset = 0
        for half in range(halves):
            for first, count in face_runs(*FACES[face], n_x, n_y):
                yield (
                    pl.ds(half * plane + first * SUB, count * SUB),
                    pl.ds(offset, count * SUB),
                )
                offset += count * SUB

    def send_face(face):
        for nodes, run in each_run(face):
            sends[face][run, :] = node_ref[nodes, :]

        @pl.when(face_valid(face))
        def _():
            face_copy(face).start()

        @pl.when(jnp.logical_not(face_valid(face)))
        def _():
            recvs[face][...] = jnp.zeros_like(recvs[face])

    def take_face(face):
        @pl.when(face_valid(face))
        def _():
            face_copy(face ^ 1).wait_recv()

        for nodes, run in each_run(face):
            node_ref[nodes, :] = node_ref[nodes, :] + recvs[face][run, :]

    for face in (0, 1, 2, 3):
        send_face(face)

    codes_ref[...] = jnp.zeros_like(codes_ref)
    for half in range(halves):
        lanes = pl.ds(half * LANES, LANES)
        for x in range(own_x):
            codes_ref[
                pl.ds(half * padded_nodes + n_x + x + 1, own_y, stride=n_x), :
            ] = code_ref[x, :, lanes]
    planes_ref[:, pl.ds(padded_nodes, LANES - padded_nodes), :] = jnp.zeros(
        (planes_ref.shape[0], LANES - padded_nodes, LANES), F32
    )
    for index, (dx, dy) in enumerate(DIRECTIONS):

        @pl.when(valid[index])
        def _(index=index):
            code_copy(opposite[index]).wait_recv()

        x = 0 if dx < 0 else n_x - 1
        y = 0 if dy < 0 else n_y - 1
        for half in range(halves):
            base = half * padded_nodes
            rows = pl.ds(half * own_y, own_y)
            if dy == 0:
                codes_ref[pl.ds(base + n_x + x, own_y, stride=n_x), :] = recv_code[
                    index, rows, :
                ]
            elif dx == 0:
                codes_ref[pl.ds(base + y * n_x + 1, own_x), :] = recv_code[
                    index, pl.ds(half * own_y, own_x), :
                ]
            else:
                codes_ref[pl.ds(base + y * n_x + x, 1), :] = recv_code[
                    index, pl.ds(half * own_y, 1), :
                ]

    take_face(0)
    take_face(1)
    send_face(4)
    send_face(5)

    groups = padded_nodes // SUB

    def update(half, group):
        base = half * plane + group * (SUB * SUB)
        channels = [
            node_ref[pl.ds(base + c, SUB, stride=SUB), :] for c in range(SUB)
        ]
        row = half * padded_nodes + group * SUB
        code = codes_ref[pl.ds(pl.multiple_of(row, SUB), SUB), :]
        shifted = code + (code >= 13).astype(jnp.int32)
        normal = [shifted // 9 - 1, shifted // 3 % 3 - 1, shifted % 3 - 1]
        normal = [n.astype(F32) for n in normal]
        length = jnp.sqrt(
            normal[0] * normal[0] + normal[1] * normal[1] + normal[2] * normal[2]
        )
        normal = [n / length for n in normal]
        masses = [channels[0], channels[4]]
        momenta = [channels[1:4], channels[5:8]]
        gravity = [0.0, 0.0, DT * GRAVITY]
        speeds = [
            [p / jnp.maximum(masses[f], FLOOR) + gravity[r] for r, p in enumerate(momenta[f])]
            for f in range(2)
        ]
        both = jnp.maximum(masses[0] + masses[1], FLOOR)
        center = [
            (momenta[0][r] + momenta[1][r]) / both + gravity[r] for r in range(3)
        ]
        share = jnp.minimum(1.0, jnp.minimum(masses[0], masses[1]) / FLOOR)
        closing = [
            share
            * jnp.maximum(
                sum((speeds[0][r] - center[r]) * normal[r] for r in range(3)), 0.0
            ),
            share
            * jnp.maximum(
                sum((center[r] - speeds[1][r]) * normal[r] for r in range(3)), 0.0
            ),
        ]
        node = group * SUB + lax.broadcasted_iota(jnp.int32, (SUB, LANES), 0)
        x = me_x * own_x + node % n_x
        y = me_y * own_y + node // n_x
        inside = (x >= 1) & (x <= size_x * own_x) & (y >= 1) & (y <= size_y * own_y)
        rows = pl.ds(pl.multiple_of(group * SUB, SUB), SUB)
        for f, sign in ((0, -1.0), (1, 1.0)):
            for r in range(3):
                speed = speeds[f][r] + sign * closing[f] * normal[r]
                planes_ref[half * 6 + 3 * f + r, rows, :] = jnp.where(inside, speed, 0.0)

    def update_groups(first, count):
        def body(step, carry):
            update(step // count, first + step % count)
            return carry

        lax.fori_loop(0, halves * count, body, 0)

    early = -(-2 * n_x // SUB)
    late = (n_y - 2) * n_x // SUB
    update_groups(early, late - early)
    for face in (2, 3, 4, 5):
        take_face(face)
    update_groups(0, early)
    update_groups(late, groups - late)
    edge = jnp.zeros((SUB, LANES), F32)
    depth = halves * LANES
    grid_ref[pl.ds(0, SUB), :] = edge
    grid_ref[pl.ds((depth + 1) * SUB, SUB), :] = edge
    for half in range(halves):
        for c in range(6):
            channel = c // 3 * 4 + c % 3
            grid_ref[
                pl.ds((1 + half * LANES) * SUB + channel, LANES, stride=SUB), :
            ] = planes_ref[half * 6 + c].T
    for j in range(tiles[1]):
        speed_ref[j] = grid_ref[pl.ds(j * body_rows, body_rows), :]
    speed_ref[tiles[1], pl.ds(0, over), :] = grid_ref[pl.ds(tiles[1] * body_rows, over), :]

    def block_speeds(block):
        at = tile_ref[block] % tiles[1]
        speeds = jnp.concatenate([speed_ref[at], speed_ref[at + 1][:over]], 0)
        left_high, left_low = split(speeds)
        right_high, right_low = high_ref[block], low_ref[block]
        product = jnp.dot(
            jnp.concatenate([left_high, left_low, left_high], 1),
            jnp.concatenate([right_high, right_high, right_low], 0),
            preferred_element_type=F32,
        )
        sums = [jnp.zeros((SUB, LANES), F32) for _ in range(4)]
        for k in range(SPAN_Z):
            weight = rows_ref[pl.ds((14 + k) * blocks + block, 1), :]
            moment = rows_ref[pl.ds((14 + SPAN_Z + k) * blocks + block, 1), :]
            rows = [product[k * SUB : (k + 1) * SUB, v * LANES : (v + 1) * LANES] for v in range(3)]
            sums[0] = sums[0] + rows[0] * weight
            sums[1] = sums[1] + rows[1] * weight
            sums[2] = sums[2] + rows[2] * weight
            sums[3] = sums[3] + rows[0] * moment
        return sums

    def gather_step(index, carry):
        members = [index * unroll + u for u in range(unroll)]
        results = [block_speeds(block) for block in members]
        for block, sums in zip(members, results):
            for v in range(4):
                start = pl.multiple_of(v * blocks * SUB + block * SUB, SUB)
                result_ref[pl.ds(start, SUB), :] = sums[v]
        return carry

    lax.fori_loop(0, blocks // unroll, gather_step, 0)

    for index in range(8):

        @pl.when(valid[index])
        def _(index=index):
            code_copy(index).wait_send()

    for face in range(6):

        @pl.when(face_valid(face))
        def _(face=face):
            face_copy(face).wait_send()


def particle_kernel(
    count_ref,
    result_hbm,
    deform_hbm,
    body_hbm,
    new_velocity_hbm,
    new_affine_hbm,
    new_deform_hbm,
    new_stress_hbm,
    result_ref,
    deform_ref,
    body_ref,
    new_velocity_ref,
    new_affine_ref,
    new_deform_ref,
    new_stress_ref,
    in_sem,
    out_sem,
):
    pairs = ((result_hbm, result_ref), (deform_hbm, deform_ref), (body_hbm, body_ref))
    loads = [
        pltpu.make_async_copy(source, target, in_sem.at[i])
        for i, (source, target) in enumerate(pairs)
    ]
    for load in loads:
        load.start()
    pairs = (
        (new_velocity_ref, new_velocity_hbm),
        (new_affine_ref, new_affine_hbm),
        (new_deform_ref, new_deform_hbm),
        (new_stress_ref, new_stress_hbm),
    )
    stores = [
        pltpu.make_async_copy(source, target, out_sem.at[i])
        for i, (source, target) in enumerate(pairs)
    ]
    for load in loads:
        load.wait()
    blocks = body_ref.shape[0]
    slot = lax.broadcasted_iota(jnp.int32, body_ref.shape, 0)
    live = slot < count_ref[0, 0]
    even = body_ref[...] % 2 == 0

    def take(v, r):
        fields = [
            result_ref[pl.ds(v * blocks * SUB + 4 * f + r, blocks, stride=SUB), :]
            for f in range(2)
        ]
        return jnp.where(live, jnp.where(even, fields[0], fields[1]), 0.0)

    for r in range(3):
        new_velocity_ref[r] = take(0, r)
    stores[0].start()
    affine = [4.0 * take(1 + c, r) for r in range(3) for c in range(3)]
    deform = [deform_ref[i] for i in range(9)]
    moved = []
    for r in range(3):
        for c in range(3):
            entry = deform[3 * r + c]
            for i in range(3):
                entry = entry + DT * affine[3 * r + i] * deform[3 * i + c]
            moved.append(jnp.where(live, entry, 0.0))
    for i in range(9):
        new_affine_ref[i] = affine[i]
    stores[1].start()
    for i in range(9):
        new_deform_ref[i] = moved[i]
    stores[2].start()
    for i, entry in enumerate(kirchhoff(moved)):
        new_stress_ref[i] = jnp.where(live, entry, 0.0)
    stores[3].start()
    for store in stores:
        store.wait()


def per_device(
    offset,
    particle_mass,
    velocity,
    affine,
    deform,
    particle_cell,
    body_id,
    slot_tile_number,
    block_count,
    normal_code,
):
    blocks, particles = particle_mass.shape
    own_x, own_y, depth = normal_code.shape
    tiles = (own_y // TILE_Y, depth // TILE_Z)
    n_x, n_y = own_x + 2, own_y + 2
    padded_nodes = -(-n_x * n_y // SUB) * SUB
    halves = depth // LANES
    assert particles == LANES and padded_nodes <= LANES and depth % LANES == 0
    unroll = next(u for u in (8, 4, 2, 1) if blocks % u == 0)
    assert own_x == own_y and max(blocks, tiles[1]) <= LANES
    vmem = pl.BlockSpec(memory_space=pltpu.VMEM)
    smem = pl.BlockSpec(memory_space=pltpu.SMEM)
    hbm = pl.BlockSpec(memory_space=pltpu.HBM)
    result_shape = jax.ShapeDtypeStruct((4 * blocks * SUB, LANES), F32)
    operands = (offset, particle_mass, velocity, affine, deform, particle_cell, body_id)
    operands = operands + (normal_code,)
    faces = [
        pltpu.VMEM(
            (halves * SUB * sum(count for _, count in face_runs(*face, n_x, n_y)), LANES), F32
        )
        for face in FACES
    ]
    dma = pltpu.SemaphoreType.DMA
    result = pl.pallas_call(
        functools.partial(
            nodes_kernel, (n_x, n_y, padded_nodes, halves, tiles, unroll)
        ),
        out_shape=result_shape,
        in_specs=[smem, smem] + [hbm] * 8,
        out_specs=vmem,
        scratch_shapes=[pltpu.VMEM(a.shape, a.dtype) for a in operands]
        + [
            pltpu.VMEM((4 * blocks * SUB, LANES), F32),
            pltpu.VMEM((N_ROWS * blocks, LANES), F32),
            pltpu.VMEM((blocks + 1, SPAN_Z * SUB, LANES), F32),
            pltpu.VMEM(((depth + 2) * SUB, LANES), F32),
            pltpu.VMEM((SUB, LANES), jnp.int32),
            pltpu.SMEM((SUB, LANES), jnp.int32),
            pltpu.VMEM((halves * padded_nodes * SUB, LANES), F32),
            pltpu.VMEM((halves * padded_nodes, LANES), jnp.int32),
            pltpu.VMEM((halves * 6, LANES, LANES), F32),
            pltpu.VMEM((8, halves * own_y, LANES), jnp.int32),
            pltpu.VMEM((8, halves * own_y, LANES), jnp.int32),
            pltpu.VMEM((tiles[1] + 1, TILE_Z * SUB, LANES), F32),
            pltpu.VMEM((blocks, LANES, 3 * LANES), BF16),
            pltpu.VMEM((blocks, LANES, 3 * LANES), BF16),
        ]
        + faces
        + faces
        + [dma((6,)), dma((6,)), dma((8,)), dma((8,)), dma((8,)), dma(())],
        compiler_params=pltpu.CompilerParams(collective_id=0, has_side_effects=True),
        name="nodes_step",
    )(slot_tile_number, block_count, *operands)
    shapes = [jax.ShapeDtypeStruct((n, blocks, LANES), F32) for n in (3, 9, 9, 6)]
    return pl.pallas_call(
        particle_kernel,
        out_shape=tuple(shapes),
        in_specs=[smem] + [hbm] * 3,
        out_specs=(hbm,) * 4,
        scratch_shapes=[
            pltpu.VMEM(result_shape.shape, F32),
            pltpu.VMEM(deform.shape, F32),
            pltpu.VMEM(body_id.shape, jnp.int32),
        ]
        + [pltpu.VMEM(a.shape, F32) for a in shapes]
        + [dma((3,)), dma((4,))],
        name="particles_step",
    )(block_count, result, deform, body_id)


def solution(mesh):
    particle = P(None, ("gx", "gy"), None)
    flat = P(("gx", "gy"), None)
    placed = (
        particle,
        flat,
        particle,
        particle,
        particle,
        flat,
        flat,
        P(("gx", "gy")),
        P("gx", "gy"),
        P("gx", "gy", None),
    )
    return jax.shard_map(
        per_device,
        mesh=mesh,
        in_specs=placed,
        out_specs=(particle,) * 4,
        check_vma=False,
    )
```

```python
import functools

import jax
import jax.numpy as jnp
from jax import lax
from jax.experimental import pallas as pl
from jax.experimental.pallas import tpu as pltpu
from jax.sharding import PartitionSpec as P

DT = 0.1
MU = 2.0
LAM = 3.0
GRAVITY = -2.0
FLOOR = 0.25
LANES = 128
SUB = 8
TILE_X, TILE_Y, TILE_Z = 4, 4, 8
SPAN_Z = TILE_Z + 2
MESH = pl.DeviceIdType.MESH
F32 = jnp.float32
BF16 = jnp.bfloat16
SIDES = [(-1, 0), (1, 0), (0, -1), (0, 1)]
DIRECTIONS = [(-1, 0), (1, 0), (0, -1), (0, 1), (-1, -1), (-1, 1), (1, -1), (1, 1)]


def spline_weights(fraction):
    return [
        0.5 * (1.5 - fraction) * (1.5 - fraction),
        0.75 - (fraction - 1.0) * (fraction - 1.0),
        0.5 * (fraction - 0.5) * (fraction - 0.5),
    ]


def determinant(m):
    return (
        m[0] * (m[4] * m[8] - m[5] * m[7])
        - m[1] * (m[3] * m[8] - m[5] * m[6])
        + m[2] * (m[3] * m[7] - m[4] * m[6])
    )


def kirchhoff(m):
    ratio = determinant(m)
    pressure = 0.5 * LAM * (ratio * ratio - 1.0)

    def dot(r, c):
        return m[3 * r] * m[3 * c] + m[3 * r + 1] * m[3 * c + 1] + m[3 * r + 2] * m[3 * c + 2]

    return [MU * (dot(r, r) - 1.0) + pressure for r in range(3)] + [
        MU * dot(0, 1),
        MU * dot(0, 2),
        MU * dot(1, 2),
    ]


SYMMETRIC = [0, 3, 4, 3, 1, 5, 4, 5, 2]


def split(value):
    high = value.astype(BF16)
    return high, (value - high.astype(F32)).astype(BF16)


def store_rows(rows_ref, blocks, offset_ref, cell_ref):
    cell = cell_ref[...]
    cells = [cell // (TILE_Y * TILE_Z), cell // TILE_Z % TILE_Y, cell % TILE_Z]
    rows = []
    for axis in range(2):
        fraction = offset_ref[axis]
        weights = spline_weights(fraction)
        rows.append(cells[axis].astype(F32))
        rows.extend(weights)
        rows.extend(weights[step] * (step - fraction) for step in range(3))
    fraction = offset_ref[2]
    weights = spline_weights(fraction)
    moments = [weights[step] * (step - fraction) for step in range(3)]
    for values in (weights, moments):
        for k in range(SPAN_Z):
            total = jnp.zeros_like(fraction)
            for step in range(3):
                total = jnp.where(cells[2] == k - step, values[step], total)
            rows.append(total)
    for index, row in enumerate(rows):
        rows_ref[pl.ds(index * blocks, blocks), :] = row


N_ROWS = 14 + 2 * SPAN_Z


def plane_groups(n_x, n_y):
    groups = [(n_x + x, n_x) for x in range(n_x)]
    groups += [(0, 1), ((n_y - 1) * n_x, 1)]
    corners = [(SUB, 0), (SUB + 1, 0), (SUB, n_y - 1), (SUB + 1, n_y - 1)]
    return groups, [y * n_x + x for x, y in corners]


def axis_weights(rows_ref, blocks, block, axis, corner, coordinates):
    def row(index):
        return rows_ref[pl.ds((7 * axis + index) * blocks + block, 1), :]

    base = row(0) + corner
    weights = [row(1 + s) for s in range(3)]
    moments = [row(4 + s) for s in range(3)]
    out = []
    for coordinate in coordinates:
        step = coordinate - base
        hits = [step == float(s) for s in range(3)]
        for rows in (weights, moments):
            total = jnp.zeros_like(step)
            for s in range(3):
                total = jnp.where(hits[s], rows[s], total)
            out.append(total)
    return out


def plane_weights(rows_ref, blocks, block, tile, tiles, n_x, n_y):
    tiles_y, tiles_z = tiles
    tile_x = (tile // (tiles_y * tiles_z) * TILE_X).astype(F32)
    tile_y = (tile // tiles_z % tiles_y * TILE_Y).astype(F32)
    lines = lax.broadcasted_iota(jnp.int32, (SUB, LANES), 0)
    low_x = lines.astype(F32)
    high_x = (lines % 2 + SUB).astype(F32)
    inner_y = low_x + 1.0
    outer_y = jnp.where(lines % 4 < 2, 0, n_y - 1).astype(F32)
    wx, mx, wx_high, mx_high = axis_weights(
        rows_ref, blocks, block, 0, tile_x, (low_x, high_x)
    )
    wy, my, wy_outer, my_outer = axis_weights(
        rows_ref, blocks, block, 1, tile_y, (inner_y, outer_y)
    )

    def line(low, high, x):
        value = low[x : x + 1] if x < SUB else high[x - SUB : x - SUB + 1]
        return jnp.broadcast_to(value, (SUB, LANES))

    weight_x = [line(wx, wx_high, x) for x in range(n_x)]
    moment_x = [line(mx, mx_high, x) for x in range(n_x)]
    first = [jnp.broadcast_to(v[0:1], (SUB, LANES)) for v in (wy_outer, my_outer)]
    last = [jnp.broadcast_to(v[2:3], (SUB, LANES)) for v in (wy_outer, my_outer)]
    corner = lines < 4
    wx_high = jnp.where(corner, wx_high, 0.0)
    mx_high = jnp.where(corner, mx_high, 0.0)
    pairs = [(weight_x[x], moment_x[x], wy, my) for x in range(n_x)]
    pairs += [(wx, mx, *first), (wx, mx, *last), (wx_high, mx_high, wy_outer, my_outer)]
    pad = [jnp.zeros((LANES - SUB * len(pairs), LANES), F32)]
    return [
        jnp.concatenate([w * v for w, _, v, _ in pairs] + pad, 0),
        jnp.concatenate([m * v for _, m, v, _ in pairs] + pad, 0),
        jnp.concatenate([w * n for w, _, _, n in pairs] + pad, 0),
    ]


def face_runs(kind, side, n_x, n_y):
    if kind == "x":
        first = 0 if side < 0 else n_x - 2
        return [(y * n_x + first, 2) for y in range(n_y)]
    layers = (0, 1) if side < 0 else (n_y - 2, n_y - 1)
    if kind == "inner":
        return [(y * n_x + 2, n_x - 4) for y in layers]
    return [(y * n_x + first, 2) for y in layers for first in (0, n_x - 2)]


FACES = [("x", -1), ("x", 1), ("inner", -1), ("inner", 1), ("outer", -1), ("outer", 1)]


def nodes_kernel(
    shape,
    tile_ref,
    count_ref,
    offset_hbm,
    mass_hbm,
    velocity_hbm,
    affine_hbm,
    deform_hbm,
    cell_hbm,
    body_hbm,
    code_hbm,
    result_ref,
    *scratch,
):
    n_x, n_y, padded_nodes, halves, tiles, unroll = shape
    inputs = scratch[:8]
    offset_ref, mass_ref, velocity_ref, affine_ref, deform_ref = inputs[:5]
    cell_ref, body_ref, code_ref = inputs[5:]
    (
        source_ref,
        rows_ref,
        chain_ref,
        grid_ref,
        table_ref,
        links,
        node_ref,
        codes_ref,
        planes_ref,
        send_code,
        recv_code,
        speed_ref,
        high_ref,
        low_ref,
    ) = scratch[8:22]
    sends = scratch[22:28]
    recvs = scratch[28:34]
    send_sem, recv_sem, code_send_sem, code_recv_sem, in_sem, table_sem = scratch[34:]
    blocks = mass_ref.shape[0]
    size_x, size_y = lax.axis_size("gx"), lax.axis_size("gy")
    me_x, me_y = lax.axis_index("gx"), lax.axis_index("gy")
    own_x, own_y = n_x - 2, n_y - 2

    hbm = (
        offset_hbm,
        mass_hbm,
        velocity_hbm,
        affine_hbm,
        deform_hbm,
        cell_hbm,
        body_hbm,
        code_hbm,
    )
    loads = [
        pltpu.make_async_copy(source, target, in_sem.at[i])
        for i, (source, target) in enumerate(zip(hbm, inputs))
    ]
    for load in loads:
        load.start()

    valid = []
    for dx, dy in DIRECTIONS:
        ok = None
        for d, me, size in ((dx, me_x, size_x), (dy, me_y, size_y)):
            if d == 0:
                continue
            one = me > 0 if d < 0 else me < size - 1
            ok = one if ok is None else jnp.logical_and(ok, one)
        valid.append(ok)
    barrier = pltpu.get_barrier_semaphore()

    def target(index):
        dx, dy = DIRECTIONS[index]
        return {"gx": me_x + dx, "gy": me_y + dy}

    for index in range(8):

        @pl.when(valid[index])
        def _(index=index):
            pl.semaphore_signal(
                barrier, inc=1, device_id=target(index), device_id_type=MESH
            )

    opposite = [DIRECTIONS.index((-dx, -dy)) for dx, dy in DIRECTIONS]
    plane = padded_nodes * SUB

    lane = lax.broadcasted_iota(jnp.int32, (SUB, LANES), 1)
    heights = [tile_ref[s] % tiles[1] for s in range(blocks)]
    height = jnp.full((SUB, LANES), -1, jnp.int32)
    for s in range(blocks):
        height = jnp.where(lane == s, heights[s], height)
    before = jnp.zeros((SUB, LANES), jnp.int32)
    last = jnp.zeros((SUB, LANES), jnp.int32)
    for s in range(blocks):
        before = jnp.where((height == heights[s]) & (lane > s), s + 1, before)
        last = jnp.where(lane == heights[s], s + 1, last)
    sublane = lax.broadcasted_iota(jnp.int32, (SUB, LANES), 0)
    table_ref[...] = jnp.where(sublane == 0, before, last)
    table_copy = pltpu.make_async_copy(table_ref, links, table_sem)
    table_copy.start()

    for load in loads[:7]:
        load.wait()
    slot = lax.broadcasted_iota(jnp.int32, mass_ref.shape, 0)
    mass = jnp.where(slot < count_ref[0, 0], mass_ref[...], 0.0)
    even = body_ref[...] % 2 == 0
    masses = [jnp.where(even, mass, 0.0), jnp.where(even, 0.0, mass)]
    tau = kirchhoff([deform_ref[i] for i in range(9)])
    force = [affine_ref[i] - 4.0 * DT * tau[SYMMETRIC[i]] for i in range(9)]
    zero = jnp.zeros_like(mass)

    def put(group, channel, value):
        source_ref[pl.ds(group * blocks * SUB + channel, blocks, stride=SUB), :] = value

    for field in range(2):
        put(0, 4 * field, masses[field])
        for r in range(3):
            put(0, 4 * field + 1 + r, masses[field] * velocity_ref[r])
        for c in range(3):
            put(1 + c, 4 * field, zero)
            for r in range(3):
                put(1 + c, 4 * field + 1 + r, masses[field] * force[3 * r + c])
    store_rows(rows_ref, blocks, offset_ref, cell_ref)
    span = SPAN_Z * SUB
    chain_ref[0] = jnp.zeros((span, LANES), F32)
    table_copy.wait()

    def block_sums(block):
        tile = tile_ref[block]
        planes = plane_weights(rows_ref, blocks, block, tile, tiles, n_x, n_y)
        groups = [
            source_ref[
                pl.ds(pl.multiple_of(g * blocks * SUB + block * SUB, SUB), SUB), :
            ]
            for g in range(4)
        ]
        left = [[], [], []]
        for k in range(SPAN_Z):
            weight = rows_ref[pl.ds((14 + k) * blocks + block, 1), :]
            moment = rows_ref[pl.ds((14 + SPAN_Z + k) * blocks + block, 1), :]
            left[0].append(groups[0] * weight + groups[3] * moment)
            left[1].append(groups[1] * weight)
            left[2].append(groups[2] * weight)
        left = jnp.concatenate([jnp.concatenate(part, 0) for part in left], 1)
        right = jnp.concatenate(planes, 1)
        left_high, left_low = split(left)
        right_high, right_low = split(right)
        high_ref[block] = right_high
        low_ref[block] = right_low
        product = lax.dot_general(
            jnp.concatenate([left_high, left_low], 0),
            jnp.concatenate([right_high, right_low], 0),
            (((1,), (1,)), ((), ())),
            preferred_element_type=F32,
        )
        return product[:span, :LANES] + (product[:span, LANES:] + product[span:, :LANES])

    def step(index, carry):
        members = [index * unroll + u for u in range(unroll)]
        sums = [block_sums(block) for block in members]
        for block, patch in zip(members, sums):
            chain_ref[block + 1] = chain_ref[links[0, block]] + patch
        return carry

    lax.fori_loop(0, blocks // unroll, step, 0)

    loads[7].wait()
    for half in range(halves):
        lanes = pl.ds(half * LANES, LANES)
        rows = pl.ds(half * own_y, own_y)
        for index, (dx, dy) in enumerate(DIRECTIONS):
            x = 0 if dx < 0 else own_x - 1
            y = 0 if dy < 0 else own_y - 1
            if dy == 0:
                send_code[index, rows, :] = code_ref[x, :, lanes]
            elif dx == 0:
                for i in range(own_x):
                    send_code[index, pl.ds(half * own_y + i, 1), :] = code_ref[
                        i, pl.ds(y, 1), lanes
                    ]
            else:
                send_code[index, rows, :] = jnp.broadcast_to(
                    code_ref[x, pl.ds(y, 1), lanes], (own_y, LANES)
                )

    def code_copy(index):
        return pltpu.make_async_remote_copy(
            src_ref=send_code.at[index],
            dst_ref=recv_code.at[opposite[index]],
            send_sem=code_send_sem.at[index],
            recv_sem=code_recv_sem.at[opposite[index]],
            device_id=target(index),
            device_id_type=MESH,
        )

    def face_copy(face):
        return pltpu.make_async_remote_copy(
            src_ref=sends[face],
            dst_ref=recvs[face ^ 1],
            send_sem=send_sem.at[face],
            recv_sem=recv_sem.at[face ^ 1],
            device_id=target(min(face, 2 + face % 2)),
            device_id_type=MESH,
        )

    def face_valid(face):
        return valid[min(face, 2 + face % 2)]

    arrivals = sum(ok.astype(jnp.int32) for ok in valid)
    pl.semaphore_wait(barrier, arrivals)
    for index in range(8):

        @pl.when(valid[index])
        def _(index=index):
            code_copy(index).start()

        @pl.when(jnp.logical_not(valid[index]))
        def _(index=index):
            recv_code[index] = jnp.zeros(recv_code.shape[1:], jnp.int32)

    body_rows = TILE_Z * SUB
    over = span - body_rows

    def assemble(j, carry):
        patch = chain_ref[links[1, j]]
        rows = pl.multiple_of(j * body_rows, SUB)
        grid_ref[pl.ds(rows, over), :] = patch[:over] + carry
        grid_ref[pl.ds(rows + over, body_rows - over), :] = patch[over:body_rows]
        return patch[body_rows:]

    tail = lax.fori_loop(0, tiles[1], assemble, jnp.zeros((over, LANES), F32), unroll=4)
    grid_ref[pl.ds(tiles[1] * body_rows, over), :] = tail

    lane_groups, lane_corners = plane_groups(n_x, n_y)
    nodes = n_x * n_y

    for half in range(halves):
        for c in range(SUB):
            part = grid_ref[pl.ds((1 + half * LANES) * SUB + c, LANES, stride=SUB), :]
            part = part.T
            for i, (first, hop) in enumerate(lane_groups):
                node_ref[
                    pl.ds(half * plane + first * SUB + c, SUB, stride=hop * SUB), :
                ] = part[i * SUB : (i + 1) * SUB]
            at = len(lane_groups) * SUB
            for i, first in enumerate(lane_corners):
                node_ref[pl.ds(half * plane + first * SUB + c, 1), :] = part[
                    at + i : at + i + 1
                ]
            node_ref[
                pl.ds(half * plane + nodes * SUB + c, padded_nodes - nodes, stride=SUB), :
            ] = jnp.zeros((padded_nodes - nodes, LANES), F32)

    def each_run(face):
        offset = 0
        for half in range(halves):
            for first, count in face_runs(*FACES[face], n_x, n_y):
                yield (
                    pl.ds(half * plane + first * SUB, count * SUB),
                    pl.ds(offset, count * SUB),
                )
                offset += count * SUB

    def send_face(face):
        for nodes, run in each_run(face):
            sends[face][run, :] = node_ref[nodes, :]

        @pl.when(face_valid(face))
        def _():
            face_copy(face).start()

        @pl.when(jnp.logical_not(face_valid(face)))
        def _():
            recvs[face][...] = jnp.zeros_like(recvs[face])

    def take_face(face):
        @pl.when(face_valid(face))
        def _():
            face_copy(face ^ 1).wait_recv()

        for nodes, run in each_run(face):
            node_ref[nodes, :] = node_ref[nodes, :] + recvs[face][run, :]

    for face in (0, 1, 2, 3):
        send_face(face)

    codes_ref[...] = jnp.zeros_like(codes_ref)
    for half in range(halves):
        lanes = pl.ds(half * LANES, LANES)
        for x in range(own_x):
            codes_ref[
                pl.ds(half * padded_nodes + n_x + x + 1, own_y, stride=n_x), :
            ] = code_ref[x, :, lanes]
    for index, (dx, dy) in enumerate(DIRECTIONS):

        @pl.when(valid[index])
        def _(index=index):
            code_copy(opposite[index]).wait_recv()

        x = 0 if dx < 0 else n_x - 1
        y = 0 if dy < 0 else n_y - 1
        for half in range(halves):
            base = half * padded_nodes
            rows = pl.ds(half * own_y, own_y)
            if dy == 0:
                codes_ref[pl.ds(base + n_x + x, own_y, stride=n_x), :] = recv_code[
                    index, rows, :
                ]
            elif dx == 0:
                codes_ref[pl.ds(base + y * n_x + 1, own_x), :] = recv_code[
                    index, pl.ds(half * own_y, own_x), :
                ]
            else:
                codes_ref[pl.ds(base + y * n_x + x, 1), :] = recv_code[
                    index, pl.ds(half * own_y, 1), :
                ]

    take_face(0)
    take_face(1)
    send_face(4)
    send_face(5)

    groups = padded_nodes // SUB

    def update(half, group):
        base = half * plane + group * (SUB * SUB)
        channels = [
            node_ref[pl.ds(base + c, SUB, stride=SUB), :] for c in range(SUB)
        ]
        row = half * padded_nodes + group * SUB
        code = codes_ref[pl.ds(pl.multiple_of(row, SUB), SUB), :]
        shifted = code + (code >= 13).astype(jnp.int32)
        normal = [shifted // 9 - 1, shifted // 3 % 3 - 1, shifted % 3 - 1]
        normal = [n.astype(F32) for n in normal]
        length = jnp.sqrt(
            normal[0] * normal[0] + normal[1] * normal[1] + normal[2] * normal[2]
        )
        normal = [n / length for n in normal]
        masses = [channels[0], channels[4]]
        momenta = [channels[1:4], channels[5:8]]
        gravity = [0.0, 0.0, DT * GRAVITY]
        speeds = [
            [p / jnp.maximum(masses[f], FLOOR) + gravity[r] for r, p in enumerate(momenta[f])]
            for f in range(2)
        ]
        both = jnp.maximum(masses[0] + masses[1], FLOOR)
        center = [
            (momenta[0][r] + momenta[1][r]) / both + gravity[r] for r in range(3)
        ]
        share = jnp.minimum(1.0, jnp.minimum(masses[0], masses[1]) / FLOOR)
        closing = [
            share
            * jnp.maximum(
                sum((speeds[0][r] - center[r]) * normal[r] for r in range(3)), 0.0
            ),
            share
            * jnp.maximum(
                sum((center[r] - speeds[1][r]) * normal[r] for r in range(3)), 0.0
            ),
        ]
        node = group * SUB + lax.broadcasted_iota(jnp.int32, (SUB, LANES), 0)
        x = me_x * own_x + node % n_x
        y = me_y * own_y + node // n_x
        inside = (x >= 1) & (x <= size_x * own_x) & (y >= 1) & (y <= size_y * own_y)
        for f, sign in ((0, -1.0), (1, 1.0)):
            for r in range(3):
                speed = speeds[f][r] + sign * closing[f] * normal[r]
                at = (half * 6 + 3 * f + r) * LANES + pl.multiple_of(group * SUB, SUB)
                planes_ref[pl.ds(at, SUB), :] = jnp.where(inside, speed, 0.0)

    def update_groups(first, count):
        def body(step, carry):
            update(step // count, first + step % count)
            return carry

        lax.fori_loop(0, halves * count, body, 0)

    early = -(-2 * n_x // SUB)
    late = (n_y - 2) * n_x // SUB
    update_groups(early, late - early)
    for face in (2, 3, 4, 5):
        take_face(face)
    update_groups(0, early)
    update_groups(late, groups - late)
    edge = jnp.zeros((SUB, LANES), F32)
    depth = halves * LANES
    grid_ref[pl.ds(0, SUB), :] = edge
    grid_ref[pl.ds((depth + 1) * SUB, SUB), :] = edge
    for half in range(halves):
        for c in range(6):
            channel = c // 3 * 4 + c % 3
            at = (half * 6 + c) * LANES
            part = [
                planes_ref[pl.ds(at + first, SUB, stride=hop), :]
                for first, hop in lane_groups
            ]
            part += [planes_ref[pl.ds(at + first, 1), :] for first in lane_corners]
            rest = LANES - len(lane_groups) * SUB - len(lane_corners)
            part.append(jnp.zeros((rest, LANES), F32))
            grid_ref[
                pl.ds((1 + half * LANES) * SUB + channel, LANES, stride=SUB), :
            ] = jnp.concatenate(part, 0).T
    for j in range(tiles[1]):
        speed_ref[j] = grid_ref[pl.ds(j * body_rows, body_rows), :]
    speed_ref[tiles[1], pl.ds(0, over), :] = grid_ref[pl.ds(tiles[1] * body_rows, over), :]

    def block_speeds(block):
        at = tile_ref[block] % tiles[1]
        speeds = jnp.concatenate([speed_ref[at], speed_ref[at + 1][:over]], 0)
        left_high, left_low = split(speeds)
        right_high, right_low = high_ref[block], low_ref[block]
        product = jnp.dot(
            jnp.concatenate([left_high, left_low, left_high], 1),
            jnp.concatenate([right_high, right_high, right_low], 0),
            preferred_element_type=F32,
        )
        sums = [jnp.zeros((SUB, LANES), F32) for _ in range(4)]
        for k in range(SPAN_Z):
            weight = rows_ref[pl.ds((14 + k) * blocks + block, 1), :]
            moment = rows_ref[pl.ds((14 + SPAN_Z + k) * blocks + block, 1), :]
            rows = [product[k * SUB : (k + 1) * SUB, v * LANES : (v + 1) * LANES] for v in range(3)]
            sums[0] = sums[0] + rows[0] * weight
            sums[1] = sums[1] + rows[1] * weight
            sums[2] = sums[2] + rows[2] * weight
            sums[3] = sums[3] + rows[0] * moment
        return sums

    def gather_step(index, carry):
        members = [index * unroll + u for u in range(unroll)]
        results = [block_speeds(block) for block in members]
        for block, sums in zip(members, results):
            for v in range(4):
                start = pl.multiple_of(v * blocks * SUB + block * SUB, SUB)
                result_ref[pl.ds(start, SUB), :] = sums[v]
        return carry

    lax.fori_loop(0, blocks // unroll, gather_step, 0)

    for index in range(8):

        @pl.when(valid[index])
        def _(index=index):
            code_copy(index).wait_send()

    for face in range(6):

        @pl.when(face_valid(face))
        def _(face=face):
            face_copy(face).wait_send()


def particle_kernel(
    count_ref,
    result_hbm,
    deform_hbm,
    body_hbm,
    new_velocity_hbm,
    new_affine_hbm,
    new_deform_hbm,
    new_stress_hbm,
    result_ref,
    deform_ref,
    body_ref,
    new_velocity_ref,
    new_affine_ref,
    new_deform_ref,
    new_stress_ref,
    in_sem,
    out_sem,
):
    pairs = ((result_hbm, result_ref), (deform_hbm, deform_ref), (body_hbm, body_ref))
    loads = [
        pltpu.make_async_copy(source, target, in_sem.at[i])
        for i, (source, target) in enumerate(pairs)
    ]
    for load in loads:
        load.start()
    pairs = (
        (new_velocity_ref, new_velocity_hbm),
        (new_affine_ref, new_affine_hbm),
        (new_deform_ref, new_deform_hbm),
        (new_stress_ref, new_stress_hbm),
    )
    stores = [
        pltpu.make_async_copy(source, target, out_sem.at[i])
        for i, (source, target) in enumerate(pairs)
    ]
    for load in loads:
        load.wait()
    blocks = body_ref.shape[0]
    slot = lax.broadcasted_iota(jnp.int32, body_ref.shape, 0)
    live = slot < count_ref[0, 0]
    even = body_ref[...] % 2 == 0

    def take(v, r):
        fields = [
            result_ref[pl.ds(v * blocks * SUB + 4 * f + r, blocks, stride=SUB), :]
            for f in range(2)
        ]
        return jnp.where(live, jnp.where(even, fields[0], fields[1]), 0.0)

    for r in range(3):
        new_velocity_ref[r] = take(0, r)
    stores[0].start()
    affine = [4.0 * take(1 + c, r) for r in range(3) for c in range(3)]
    deform = [deform_ref[i] for i in range(9)]
    moved = []
    for r in range(3):
        for c in range(3):
            entry = deform[3 * r + c]
            for i in range(3):
                entry = entry + DT * affine[3 * r + i] * deform[3 * i + c]
            moved.append(jnp.where(live, entry, 0.0))
    for i in range(9):
        new_affine_ref[i] = affine[i]
    stores[1].start()
    for i in range(9):
        new_deform_ref[i] = moved[i]
    stores[2].start()
    for i, entry in enumerate(kirchhoff(moved)):
        new_stress_ref[i] = jnp.where(live, entry, 0.0)
    stores[3].start()
    for store in stores:
        store.wait()


def per_device(
    offset,
    particle_mass,
    velocity,
    affine,
    deform,
    particle_cell,
    body_id,
    slot_tile_number,
    block_count,
    normal_code,
):
    blocks, particles = particle_mass.shape
    own_x, own_y, depth = normal_code.shape
    tiles = (own_y // TILE_Y, depth // TILE_Z)
    n_x, n_y = own_x + 2, own_y + 2
    padded_nodes = -(-n_x * n_y // SUB) * SUB
    halves = depth // LANES
    assert particles == LANES and padded_nodes <= LANES and depth % LANES == 0
    unroll = next(u for u in (24, 8, 4, 2, 1) if blocks % u == 0)
    assert own_x == own_y == SUB and max(blocks, tiles[1]) <= LANES
    vmem = pl.BlockSpec(memory_space=pltpu.VMEM)
    smem = pl.BlockSpec(memory_space=pltpu.SMEM)
    hbm = pl.BlockSpec(memory_space=pltpu.HBM)
    result_shape = jax.ShapeDtypeStruct((4 * blocks * SUB, LANES), F32)
    operands = (offset, particle_mass, velocity, affine, deform, particle_cell, body_id)
    operands = operands + (normal_code,)
    faces = [
        pltpu.VMEM(
            (halves * SUB * sum(count for _, count in face_runs(*face, n_x, n_y)), LANES), F32
        )
        for face in FACES
    ]
    dma = pltpu.SemaphoreType.DMA
    result = pl.pallas_call(
        functools.partial(
            nodes_kernel, (n_x, n_y, padded_nodes, halves, tiles, unroll)
        ),
        out_shape=result_shape,
        in_specs=[smem, smem] + [hbm] * 8,
        out_specs=vmem,
        scratch_shapes=[pltpu.VMEM(a.shape, a.dtype) for a in operands]
        + [
            pltpu.VMEM((4 * blocks * SUB, LANES), F32),
            pltpu.VMEM((N_ROWS * blocks, LANES), F32),
            pltpu.VMEM((blocks + 1, SPAN_Z * SUB, LANES), F32),
            pltpu.VMEM(((depth + 2) * SUB, LANES), F32),
            pltpu.VMEM((SUB, LANES), jnp.int32),
            pltpu.SMEM((SUB, LANES), jnp.int32),
            pltpu.VMEM((halves * padded_nodes * SUB, LANES), F32),
            pltpu.VMEM((halves * padded_nodes, LANES), jnp.int32),
            pltpu.VMEM((halves * 6 * LANES, LANES), F32),
            pltpu.VMEM((8, halves * own_y, LANES), jnp.int32),
            pltpu.VMEM((8, halves * own_y, LANES), jnp.int32),
            pltpu.VMEM((tiles[1] + 1, TILE_Z * SUB, LANES), F32),
            pltpu.VMEM((blocks, LANES, 3 * LANES), BF16),
            pltpu.VMEM((blocks, LANES, 3 * LANES), BF16),
        ]
        + faces
        + faces
        + [dma((6,)), dma((6,)), dma((8,)), dma((8,)), dma((8,)), dma(())],
        compiler_params=pltpu.CompilerParams(collective_id=0, has_side_effects=True),
        name="nodes_step",
    )(slot_tile_number, block_count, *operands)
    shapes = [jax.ShapeDtypeStruct((n, blocks, LANES), F32) for n in (3, 9, 9, 6)]
    return pl.pallas_call(
        particle_kernel,
        out_shape=tuple(shapes),
        in_specs=[smem] + [hbm] * 3,
        out_specs=(hbm,) * 4,
        scratch_shapes=[
            pltpu.VMEM(result_shape.shape, F32),
            pltpu.VMEM(deform.shape, F32),
            pltpu.VMEM(body_id.shape, jnp.int32),
        ]
        + [pltpu.VMEM(a.shape, F32) for a in shapes]
        + [dma((3,)), dma((4,))],
        name="particles_step",
    )(block_count, result, deform, body_id)


def solution(mesh):
    particle = P(None, ("gx", "gy"), None)
    flat = P(("gx", "gy"), None)
    placed = (
        particle,
        flat,
        particle,
        particle,
        particle,
        flat,
        flat,
        P(("gx", "gy")),
        P("gx", "gy"),
        P("gx", "gy", None),
    )
    return jax.shard_map(
        per_device,
        mesh=mesh,
        in_specs=placed,
        out_specs=(particle,) * 4,
        check_vma=False,
    )
```

```python
import functools

import jax
import jax.numpy as jnp
from jax import lax
from jax.experimental import pallas as pl
from jax.experimental.pallas import tpu as pltpu
from jax.sharding import PartitionSpec as P

DT = 0.1
MU = 2.0
LAM = 3.0
GRAVITY = -2.0
FLOOR = 0.25
LANES = 128
SUB = 8
TILE_X, TILE_Y, TILE_Z = 4, 4, 8
SPAN_Z = TILE_Z + 2
MESH = pl.DeviceIdType.MESH
F32 = jnp.float32
BF16 = jnp.bfloat16
SIDES = [(-1, 0), (1, 0), (0, -1), (0, 1)]
DIRECTIONS = [(-1, 0), (1, 0), (0, -1), (0, 1), (-1, -1), (-1, 1), (1, -1), (1, 1)]


def spline_weights(fraction):
    return [
        0.5 * (1.5 - fraction) * (1.5 - fraction),
        0.75 - (fraction - 1.0) * (fraction - 1.0),
        0.5 * (fraction - 0.5) * (fraction - 0.5),
    ]


def determinant(m):
    return (
        m[0] * (m[4] * m[8] - m[5] * m[7])
        - m[1] * (m[3] * m[8] - m[5] * m[6])
        + m[2] * (m[3] * m[7] - m[4] * m[6])
    )


def kirchhoff(m):
    ratio = determinant(m)
    pressure = 0.5 * LAM * (ratio * ratio - 1.0)

    def dot(r, c):
        return m[3 * r] * m[3 * c] + m[3 * r + 1] * m[3 * c + 1] + m[3 * r + 2] * m[3 * c + 2]

    return [MU * (dot(r, r) - 1.0) + pressure for r in range(3)] + [
        MU * dot(0, 1),
        MU * dot(0, 2),
        MU * dot(1, 2),
    ]


SYMMETRIC = [0, 3, 4, 3, 1, 5, 4, 5, 2]


def split(value):
    high = value.astype(BF16)
    return high, (value - high.astype(F32)).astype(BF16)


def store_rows(rows_ref, blocks, offset_ref, cell_ref):
    cell = cell_ref[...]
    cells = [cell // (TILE_Y * TILE_Z), cell // TILE_Z % TILE_Y, cell % TILE_Z]
    rows = []
    for axis in range(2):
        fraction = offset_ref[axis]
        weights = spline_weights(fraction)
        rows.append(cells[axis].astype(F32))
        rows.extend(weights)
        rows.extend(weights[step] * (step - fraction) for step in range(3))
    fraction = offset_ref[2]
    weights = spline_weights(fraction)
    moments = [weights[step] * (step - fraction) for step in range(3)]
    for values in (weights, moments):
        for k in range(SPAN_Z):
            total = jnp.zeros_like(fraction)
            for step in range(3):
                total = jnp.where(cells[2] == k - step, values[step], total)
            rows.append(total)
    for index, row in enumerate(rows):
        rows_ref[pl.ds(index * blocks, blocks), :] = row


N_ROWS = 14 + 2 * SPAN_Z


def plane_groups(n_x, n_y):
    groups = [(n_x + x, n_x) for x in range(n_x)]
    groups += [(0, 1), ((n_y - 1) * n_x, 1)]
    corners = [(SUB, 0), (SUB + 1, 0), (SUB, n_y - 1), (SUB + 1, n_y - 1)]
    return groups, [y * n_x + x for x, y in corners]


def axis_weights(rows_ref, blocks, block, axis, corner, coordinates):
    def row(index):
        return rows_ref[pl.ds((7 * axis + index) * blocks + block, 1), :]

    base = row(0) + corner
    weights = [row(1 + s) for s in range(3)]
    moments = [row(4 + s) for s in range(3)]
    out = []
    for coordinate in coordinates:
        step = coordinate - base
        hits = [step == float(s) for s in range(3)]
        for rows in (weights, moments):
            total = jnp.zeros_like(step)
            for s in range(3):
                total = jnp.where(hits[s], rows[s], total)
            out.append(total)
    return out


def plane_weights(rows_ref, blocks, block, tile, tiles, n_x, n_y):
    tiles_y, tiles_z = tiles
    tile_x = (tile // (tiles_y * tiles_z) * TILE_X).astype(F32)
    tile_y = (tile // tiles_z % tiles_y * TILE_Y).astype(F32)
    lines = lax.broadcasted_iota(jnp.int32, (SUB, LANES), 0)
    low_x = lines.astype(F32)
    high_x = (lines % 2 + SUB).astype(F32)
    inner_y = low_x + 1.0
    outer_y = jnp.where(lines % 4 < 2, 0, n_y - 1).astype(F32)
    wx, mx, wx_high, mx_high = axis_weights(
        rows_ref, blocks, block, 0, tile_x, (low_x, high_x)
    )
    wy, my, wy_outer, my_outer = axis_weights(
        rows_ref, blocks, block, 1, tile_y, (inner_y, outer_y)
    )

    def line(low, high, x):
        value = low[x : x + 1] if x < SUB else high[x - SUB : x - SUB + 1]
        return jnp.broadcast_to(value, (SUB, LANES))

    weight_x = [line(wx, wx_high, x) for x in range(n_x)]
    moment_x = [line(mx, mx_high, x) for x in range(n_x)]
    first = [jnp.broadcast_to(v[0:1], (SUB, LANES)) for v in (wy_outer, my_outer)]
    last = [jnp.broadcast_to(v[2:3], (SUB, LANES)) for v in (wy_outer, my_outer)]
    corner = lines < 4
    wx_high = jnp.where(corner, wx_high, 0.0)
    mx_high = jnp.where(corner, mx_high, 0.0)
    pairs = [(weight_x[x], moment_x[x], wy, my) for x in range(n_x)]
    pairs += [(wx, mx, *first), (wx, mx, *last), (wx_high, mx_high, wy_outer, my_outer)]
    pad = [jnp.zeros((LANES - SUB * len(pairs), LANES), F32)]
    return [
        jnp.concatenate([w * v for w, _, v, _ in pairs] + pad, 0),
        jnp.concatenate([m * v for _, m, v, _ in pairs] + pad, 0),
        jnp.concatenate([w * n for w, _, _, n in pairs] + pad, 0),
    ]


def face_runs(kind, side, n_x, n_y):
    if kind == "x":
        first = 0 if side < 0 else n_x - 2
        return [(y * n_x + first, 2) for y in range(n_y)]
    layers = (0, 1) if side < 0 else (n_y - 2, n_y - 1)
    if kind == "inner":
        return [(y * n_x + 2, n_x - 4) for y in layers]
    return [(y * n_x + first, 2) for y in layers for first in (0, n_x - 2)]


FACES = [("x", -1), ("x", 1), ("inner", -1), ("inner", 1), ("outer", -1), ("outer", 1)]


def nodes_kernel(
    shape,
    tile_ref,
    count_ref,
    offset_hbm,
    mass_hbm,
    velocity_hbm,
    affine_hbm,
    deform_hbm,
    cell_hbm,
    body_hbm,
    code_hbm,
    result_ref,
    *scratch,
):
    n_x, n_y, padded_nodes, halves, tiles, unroll = shape
    inputs = scratch[:8]
    offset_ref, mass_ref, velocity_ref, affine_ref, deform_ref = inputs[:5]
    cell_ref, body_ref, code_ref = inputs[5:]
    (
        source_ref,
        rows_ref,
        chain_ref,
        grid_ref,
        table_ref,
        links,
        node_ref,
        codes_ref,
        planes_ref,
        send_code,
        recv_code,
        speed_ref,
        high_ref,
        low_ref,
    ) = scratch[8:22]
    sends = scratch[22:28]
    recvs = scratch[28:34]
    send_sem, recv_sem, code_send_sem, code_recv_sem, in_sem, table_sem = scratch[34:40]
    relays = scratch[40:42]
    relay_send_sem, relay_recv_sem, pass_send_sem, pass_recv_sem = scratch[42:]
    blocks = mass_ref.shape[0]
    size_x, size_y = lax.axis_size("gx"), lax.axis_size("gy")
    me_x, me_y = lax.axis_index("gx"), lax.axis_index("gy")
    own_x, own_y = n_x - 2, n_y - 2

    hbm = (
        offset_hbm,
        mass_hbm,
        velocity_hbm,
        affine_hbm,
        deform_hbm,
        cell_hbm,
        body_hbm,
        code_hbm,
    )
    loads = [
        pltpu.make_async_copy(source, target, in_sem.at[i])
        for i, (source, target) in enumerate(zip(hbm, inputs))
    ]
    for load in loads:
        load.start()

    valid = []
    for dx, dy in DIRECTIONS:
        ok = None
        for d, me, size in ((dx, me_x, size_x), (dy, me_y, size_y)):
            if d == 0:
                continue
            one = me > 0 if d < 0 else me < size - 1
            ok = one if ok is None else jnp.logical_and(ok, one)
        valid.append(ok)
    barrier = pltpu.get_barrier_semaphore()

    def target(index):
        dx, dy = DIRECTIONS[index]
        return {"gx": me_x + dx, "gy": me_y + dy}

    for index in range(8):

        @pl.when(valid[index])
        def _(index=index):
            pl.semaphore_signal(
                barrier, inc=1, device_id=target(index), device_id_type=MESH
            )

    relayed = size_y == 4
    if relayed:
        pl.semaphore_signal(
            barrier,
            inc=1,
            device_id={"gx": me_x, "gy": (me_y + 2) % 4},
            device_id_type=MESH,
        )

    opposite = [DIRECTIONS.index((-dx, -dy)) for dx, dy in DIRECTIONS]
    plane = padded_nodes * SUB

    lane = lax.broadcasted_iota(jnp.int32, (SUB, LANES), 1)
    heights = [tile_ref[s] % tiles[1] for s in range(blocks)]
    height = jnp.full((SUB, LANES), -1, jnp.int32)
    for s in range(blocks):
        height = jnp.where(lane == s, heights[s], height)
    before = jnp.zeros((SUB, LANES), jnp.int32)
    last = jnp.zeros((SUB, LANES), jnp.int32)
    for s in range(blocks):
        before = jnp.where((height == heights[s]) & (lane > s), s + 1, before)
        last = jnp.where(lane == heights[s], s + 1, last)
    sublane = lax.broadcasted_iota(jnp.int32, (SUB, LANES), 0)
    table_ref[...] = jnp.where(sublane == 0, before, last)
    table_copy = pltpu.make_async_copy(table_ref, links, table_sem)
    table_copy.start()

    for load in loads[:7]:
        load.wait()
    slot = lax.broadcasted_iota(jnp.int32, mass_ref.shape, 0)
    mass = jnp.where(slot < count_ref[0, 0], mass_ref[...], 0.0)
    even = body_ref[...] % 2 == 0
    masses = [jnp.where(even, mass, 0.0), jnp.where(even, 0.0, mass)]
    tau = kirchhoff([deform_ref[i] for i in range(9)])
    force = [affine_ref[i] - 4.0 * DT * tau[SYMMETRIC[i]] for i in range(9)]
    zero = jnp.zeros_like(mass)

    def put(group, channel, value):
        source_ref[pl.ds(group * blocks * SUB + channel, blocks, stride=SUB), :] = value

    for field in range(2):
        put(0, 4 * field, masses[field])
        for r in range(3):
            put(0, 4 * field + 1 + r, masses[field] * velocity_ref[r])
        for c in range(3):
            put(1 + c, 4 * field, zero)
            for r in range(3):
                put(1 + c, 4 * field + 1 + r, masses[field] * force[3 * r + c])
    store_rows(rows_ref, blocks, offset_ref, cell_ref)
    span = SPAN_Z * SUB
    chain_ref[0] = jnp.zeros((span, LANES), F32)
    table_copy.wait()

    def block_sums(block):
        tile = tile_ref[block]
        planes = plane_weights(rows_ref, blocks, block, tile, tiles, n_x, n_y)
        groups = [
            source_ref[
                pl.ds(pl.multiple_of(g * blocks * SUB + block * SUB, SUB), SUB), :
            ]
            for g in range(4)
        ]
        left = [[], [], []]
        for k in range(SPAN_Z):
            weight = rows_ref[pl.ds((14 + k) * blocks + block, 1), :]
            moment = rows_ref[pl.ds((14 + SPAN_Z + k) * blocks + block, 1), :]
            left[0].append(groups[0] * weight + groups[3] * moment)
            left[1].append(groups[1] * weight)
            left[2].append(groups[2] * weight)
        left = jnp.concatenate([jnp.concatenate(part, 0) for part in left], 1)
        right = jnp.concatenate(planes, 1)
        left_high, left_low = split(left)
        right_high, right_low = split(right)
        high_ref[block] = right_high
        low_ref[block] = right_low
        product = lax.dot_general(
            jnp.concatenate([left_high, left_low], 0),
            jnp.concatenate([right_high, right_low], 0),
            (((1,), (1,)), ((), ())),
            preferred_element_type=F32,
        )
        return product[:span, :LANES] + (product[:span, LANES:] + product[span:, :LANES])

    def step(index, carry):
        members = [index * unroll + u for u in range(unroll)]
        sums = [block_sums(block) for block in members]
        for block, patch in zip(members, sums):
            chain_ref[block + 1] = chain_ref[links[0, block]] + patch
        return carry

    lax.fori_loop(0, blocks // unroll, step, 0)

    loads[7].wait()
    for half in range(halves):
        lanes = pl.ds(half * LANES, LANES)
        rows = pl.ds(half * own_y, own_y)
        for index, (dx, dy) in enumerate(DIRECTIONS):
            x = 0 if dx < 0 else own_x - 1
            y = 0 if dy < 0 else own_y - 1
            if dy == 0:
                send_code[index, rows, :] = code_ref[x, :, lanes]
            elif dx == 0:
                for i in range(own_x):
                    send_code[index, pl.ds(half * own_y + i, 1), :] = code_ref[
                        i, pl.ds(y, 1), lanes
                    ]
            else:
                send_code[index, rows, :] = jnp.broadcast_to(
                    code_ref[x, pl.ds(y, 1), lanes], (own_y, LANES)
                )

    def code_copy(index):
        return pltpu.make_async_remote_copy(
            src_ref=send_code.at[index],
            dst_ref=recv_code.at[opposite[index]],
            send_sem=code_send_sem.at[index],
            recv_sem=code_recv_sem.at[opposite[index]],
            device_id=target(index),
            device_id_type=MESH,
        )

    def face_copy(face):
        return pltpu.make_async_remote_copy(
            src_ref=sends[face],
            dst_ref=recvs[face ^ 1],
            send_sem=send_sem.at[face],
            recv_sem=recv_sem.at[face ^ 1],
            device_id=target(min(face, 2 + face % 2)),
            device_id_type=MESH,
        )

    def face_valid(face):
        return valid[min(face, 2 + face % 2)]

    def is_relayed(face):
        return me_y == (1 if FACES[face][1] > 0 else 2)

    def is_direct(face):
        if relayed and face >= 2:
            return jnp.logical_and(face_valid(face), jnp.logical_not(is_relayed(face)))
        return face_valid(face)

    def half_rows(ref, half):
        count = ref.shape[0] // 2
        return ref.at[pl.ds(half * count, count)]

    def relay_copy(face, half):
        part, slot = face // 2 - 1, 1 - face % 2
        return pltpu.make_async_remote_copy(
            src_ref=half_rows(sends[face], half),
            dst_ref=relays[part].at[slot],
            send_sem=relay_send_sem.at[2 * part + half],
            recv_sem=relay_recv_sem.at[2 * part + slot],
            device_id={"gx": me_x, "gy": 3 * half},
            device_id_type=MESH,
        )

    def pass_copy(part, slot, half):
        return pltpu.make_async_remote_copy(
            src_ref=relays[part].at[slot],
            dst_ref=half_rows(recvs[2 * part + 2 + slot], half),
            send_sem=pass_send_sem.at[2 * part + slot],
            recv_sem=pass_recv_sem.at[2 * part + half],
            device_id={"gx": me_x, "gy": 2 - slot},
            device_id_type=MESH,
        )

    def pass_on(part):
        for half in range(2):

            @pl.when(me_y == 3 * half)
            def _(half=half):
                for slot in range(2):
                    relay_copy(2 * part + 3 - slot, half).wait_recv()
                    pass_copy(part, slot, half).start()

    arrivals = sum(ok.astype(jnp.int32) for ok in valid) + int(relayed)
    pl.semaphore_wait(barrier, arrivals)
    for index in range(8):

        @pl.when(valid[index])
        def _(index=index):
            code_copy(index).start()

        @pl.when(jnp.logical_not(valid[index]))
        def _(index=index):
            recv_code[index] = jnp.zeros(recv_code.shape[1:], jnp.int32)

    body_rows = TILE_Z * SUB
    over = span - body_rows

    def assemble(j, carry):
        patch = chain_ref[links[1, j]]
        rows = pl.multiple_of(j * body_rows, SUB)
        grid_ref[pl.ds(rows, over), :] = patch[:over] + carry
        grid_ref[pl.ds(rows + over, body_rows - over), :] = patch[over:body_rows]
        return patch[body_rows:]

    tail = lax.fori_loop(0, tiles[1], assemble, jnp.zeros((over, LANES), F32), unroll=4)
    grid_ref[pl.ds(tiles[1] * body_rows, over), :] = tail

    lane_groups, lane_corners = plane_groups(n_x, n_y)
    nodes = n_x * n_y

    for half in range(halves):
        for c in range(SUB):
            part = grid_ref[pl.ds((1 + half * LANES) * SUB + c, LANES, stride=SUB), :]
            part = part.T
            for i, (first, hop) in enumerate(lane_groups):
                node_ref[
                    pl.ds(half * plane + first * SUB + c, SUB, stride=hop * SUB), :
                ] = part[i * SUB : (i + 1) * SUB]
            at = len(lane_groups) * SUB
            for i, first in enumerate(lane_corners):
                node_ref[pl.ds(half * plane + first * SUB + c, 1), :] = part[
                    at + i : at + i + 1
                ]
            node_ref[
                pl.ds(half * plane + nodes * SUB + c, padded_nodes - nodes, stride=SUB), :
            ] = jnp.zeros((padded_nodes - nodes, LANES), F32)

    def each_run(face):
        offset = 0
        for half in range(halves):
            for first, count in face_runs(*FACES[face], n_x, n_y):
                yield (
                    pl.ds(half * plane + first * SUB, count * SUB),
                    pl.ds(offset, count * SUB),
                )
                offset += count * SUB

    def send_far(face):
        for rows, run in each_run(face):
            sends[face][run, :] = node_ref[rows, :]
        if relayed:

            @pl.when(is_relayed(face))
            def _():
                for half in range(2):
                    relay_copy(face, half).start()

    def send_face(face):
        if face < 2:
            for rows, run in each_run(face):
                sends[face][run, :] = node_ref[rows, :]

        @pl.when(is_direct(face))
        def _():
            face_copy(face).start()

        @pl.when(jnp.logical_not(face_valid(face)))
        def _():
            recvs[face][...] = jnp.zeros_like(recvs[face])

    def take_face(face):
        @pl.when(is_direct(face))
        def _():
            face_copy(face ^ 1).wait_recv()

        if relayed and face >= 2:

            @pl.when(is_relayed(face))
            def _():
                for half in range(2):
                    pass_copy(face // 2 - 1, face % 2, half).wait_recv()

        for rows, run in each_run(face):
            node_ref[rows, :] = node_ref[rows, :] + recvs[face][run, :]

    send_far(2)
    send_far(3)
    for face in (2, 3, 0, 1):
        send_face(face)

    codes_ref[...] = jnp.zeros_like(codes_ref)
    for half in range(halves):
        lanes = pl.ds(half * LANES, LANES)
        for x in range(own_x):
            codes_ref[
                pl.ds(half * padded_nodes + n_x + x + 1, own_y, stride=n_x), :
            ] = code_ref[x, :, lanes]
    for index, (dx, dy) in enumerate(DIRECTIONS):

        @pl.when(valid[index])
        def _(index=index):
            code_copy(opposite[index]).wait_recv()

        x = 0 if dx < 0 else n_x - 1
        y = 0 if dy < 0 else n_y - 1
        for half in range(halves):
            base = half * padded_nodes
            rows = pl.ds(half * own_y, own_y)
            if dy == 0:
                codes_ref[pl.ds(base + n_x + x, own_y, stride=n_x), :] = recv_code[
                    index, rows, :
                ]
            elif dx == 0:
                codes_ref[pl.ds(base + y * n_x + 1, own_x), :] = recv_code[
                    index, pl.ds(half * own_y, own_x), :
                ]
            else:
                codes_ref[pl.ds(base + y * n_x + x, 1), :] = recv_code[
                    index, pl.ds(half * own_y, 1), :
                ]

    if relayed:
        pass_on(0)
    take_face(0)
    take_face(1)
    send_far(4)
    send_far(5)
    send_face(4)
    send_face(5)

    groups = padded_nodes // SUB

    def update(half, group):
        base = half * plane + group * (SUB * SUB)
        channels = [
            node_ref[pl.ds(base + c, SUB, stride=SUB), :] for c in range(SUB)
        ]
        row = half * padded_nodes + group * SUB
        code = codes_ref[pl.ds(pl.multiple_of(row, SUB), SUB), :]
        shifted = code + (code >= 13).astype(jnp.int32)
        normal = [shifted // 9 - 1, shifted // 3 % 3 - 1, shifted % 3 - 1]
        normal = [n.astype(F32) for n in normal]
        length = jnp.sqrt(
            normal[0] * normal[0] + normal[1] * normal[1] + normal[2] * normal[2]
        )
        normal = [n / length for n in normal]
        masses = [channels[0], channels[4]]
        momenta = [channels[1:4], channels[5:8]]
        gravity = [0.0, 0.0, DT * GRAVITY]
        speeds = [
            [p / jnp.maximum(masses[f], FLOOR) + gravity[r] for r, p in enumerate(momenta[f])]
            for f in range(2)
        ]
        both = jnp.maximum(masses[0] + masses[1], FLOOR)
        center = [
            (momenta[0][r] + momenta[1][r]) / both + gravity[r] for r in range(3)
        ]
        share = jnp.minimum(1.0, jnp.minimum(masses[0], masses[1]) / FLOOR)
        closing = [
            share
            * jnp.maximum(
                sum((speeds[0][r] - center[r]) * normal[r] for r in range(3)), 0.0
            ),
            share
            * jnp.maximum(
                sum((center[r] - speeds[1][r]) * normal[r] for r in range(3)), 0.0
            ),
        ]
        node = group * SUB + lax.broadcasted_iota(jnp.int32, (SUB, LANES), 0)
        x = me_x * own_x + node % n_x
        y = me_y * own_y + node // n_x
        inside = (x >= 1) & (x <= size_x * own_x) & (y >= 1) & (y <= size_y * own_y)
        for f, sign in ((0, -1.0), (1, 1.0)):
            for r in range(3):
                speed = speeds[f][r] + sign * closing[f] * normal[r]
                at = (half * 6 + 3 * f + r) * LANES + pl.multiple_of(group * SUB, SUB)
                planes_ref[pl.ds(at, SUB), :] = jnp.where(inside, speed, 0.0)

    def update_groups(first, count):
        def body(step, carry):
            update(step // count, first + step % count)
            return carry

        lax.fori_loop(0, halves * count, body, 0)

    early = -(-2 * n_x // SUB)
    late = (n_y - 2) * n_x // SUB
    update_groups(early, late - early)
    if relayed:
        pass_on(1)
    for face in (2, 3, 4, 5):
        take_face(face)
    update_groups(0, early)
    update_groups(late, groups - late)
    edge = jnp.zeros((SUB, LANES), F32)
    depth = halves * LANES
    grid_ref[pl.ds(0, SUB), :] = edge
    grid_ref[pl.ds((depth + 1) * SUB, SUB), :] = edge
    for half in range(halves):
        for c in range(6):
            channel = c // 3 * 4 + c % 3
            at = (half * 6 + c) * LANES
            part = [
                planes_ref[pl.ds(at + first, SUB, stride=hop), :]
                for first, hop in lane_groups
            ]
            part += [planes_ref[pl.ds(at + first, 1), :] for first in lane_corners]
            rest = LANES - len(lane_groups) * SUB - len(lane_corners)
            part.append(jnp.zeros((rest, LANES), F32))
            grid_ref[
                pl.ds((1 + half * LANES) * SUB + channel, LANES, stride=SUB), :
            ] = jnp.concatenate(part, 0).T
    for j in range(tiles[1]):
        speed_ref[j] = grid_ref[pl.ds(j * body_rows, body_rows), :]
    speed_ref[tiles[1], pl.ds(0, over), :] = grid_ref[pl.ds(tiles[1] * body_rows, over), :]

    def block_speeds(block):
        at = tile_ref[block] % tiles[1]
        speeds = jnp.concatenate([speed_ref[at], speed_ref[at + 1][:over]], 0)
        left_high, left_low = split(speeds)
        right_high, right_low = high_ref[block], low_ref[block]
        product = jnp.dot(
            jnp.concatenate([left_high, left_low, left_high], 1),
            jnp.concatenate([right_high, right_high, right_low], 0),
            preferred_element_type=F32,
        )
        sums = [jnp.zeros((SUB, LANES), F32) for _ in range(4)]
        for k in range(SPAN_Z):
            weight = rows_ref[pl.ds((14 + k) * blocks + block, 1), :]
            moment = rows_ref[pl.ds((14 + SPAN_Z + k) * blocks + block, 1), :]
            rows = [product[k * SUB : (k + 1) * SUB, v * LANES : (v + 1) * LANES] for v in range(3)]
            sums[0] = sums[0] + rows[0] * weight
            sums[1] = sums[1] + rows[1] * weight
            sums[2] = sums[2] + rows[2] * weight
            sums[3] = sums[3] + rows[0] * moment
        return sums

    def gather_step(index, carry):
        members = [index * unroll + u for u in range(unroll)]
        results = [block_speeds(block) for block in members]
        for block, sums in zip(members, results):
            for v in range(4):
                start = pl.multiple_of(v * blocks * SUB + block * SUB, SUB)
                result_ref[pl.ds(start, SUB), :] = sums[v]
        return carry

    lax.fori_loop(0, blocks // unroll, gather_step, 0)

    for index in range(8):

        @pl.when(valid[index])
        def _(index=index):
            code_copy(index).wait_send()

    for face in range(6):

        @pl.when(is_direct(face))
        def _(face=face):
            face_copy(face).wait_send()

        if relayed and face >= 2:

            @pl.when(is_relayed(face))
            def _(face=face):
                for half in range(2):
                    relay_copy(face, half).wait_send()

    if relayed:
        for half in range(2):

            @pl.when(me_y == 3 * half)
            def _(half=half):
                for part in range(2):
                    for slot in range(2):
                        pass_copy(part, slot, half).wait_send()


def particle_kernel(
    count_ref,
    result_hbm,
    deform_hbm,
    body_hbm,
    new_velocity_hbm,
    new_affine_hbm,
    new_deform_hbm,
    new_stress_hbm,
    result_ref,
    deform_ref,
    body_ref,
    new_velocity_ref,
    new_affine_ref,
    new_deform_ref,
    new_stress_ref,
    in_sem,
    out_sem,
):
    pairs = ((result_hbm, result_ref), (deform_hbm, deform_ref), (body_hbm, body_ref))
    loads = [
        pltpu.make_async_copy(source, target, in_sem.at[i])
        for i, (source, target) in enumerate(pairs)
    ]
    for load in loads:
        load.start()
    pairs = (
        (new_velocity_ref, new_velocity_hbm),
        (new_affine_ref, new_affine_hbm),
        (new_deform_ref, new_deform_hbm),
        (new_stress_ref, new_stress_hbm),
    )
    stores = [
        pltpu.make_async_copy(source, target, out_sem.at[i])
        for i, (source, target) in enumerate(pairs)
    ]
    for load in loads:
        load.wait()
    blocks = body_ref.shape[0]
    slot = lax.broadcasted_iota(jnp.int32, body_ref.shape, 0)
    live = slot < count_ref[0, 0]
    even = body_ref[...] % 2 == 0

    def take(v, r):
        fields = [
            result_ref[pl.ds(v * blocks * SUB + 4 * f + r, blocks, stride=SUB), :]
            for f in range(2)
        ]
        return jnp.where(live, jnp.where(even, fields[0], fields[1]), 0.0)

    for r in range(3):
        new_velocity_ref[r] = take(0, r)
    stores[0].start()
    affine = [4.0 * take(1 + c, r) for r in range(3) for c in range(3)]
    deform = [deform_ref[i] for i in range(9)]
    moved = []
    for r in range(3):
        for c in range(3):
            entry = deform[3 * r + c]
            for i in range(3):
                entry = entry + DT * affine[3 * r + i] * deform[3 * i + c]
            moved.append(jnp.where(live, entry, 0.0))
    for i in range(9):
        new_affine_ref[i] = affine[i]
    stores[1].start()
    for i in range(9):
        new_deform_ref[i] = moved[i]
    stores[2].start()
    for i, entry in enumerate(kirchhoff(moved)):
        new_stress_ref[i] = jnp.where(live, entry, 0.0)
    stores[3].start()
    for store in stores:
        store.wait()


def per_device(
    offset,
    particle_mass,
    velocity,
    affine,
    deform,
    particle_cell,
    body_id,
    slot_tile_number,
    block_count,
    normal_code,
):
    blocks, particles = particle_mass.shape
    own_x, own_y, depth = normal_code.shape
    tiles = (own_y // TILE_Y, depth // TILE_Z)
    n_x, n_y = own_x + 2, own_y + 2
    padded_nodes = -(-n_x * n_y // SUB) * SUB
    halves = depth // LANES
    assert particles == LANES and padded_nodes <= LANES and depth % LANES == 0
    unroll = next(u for u in (24, 8, 4, 2, 1) if blocks % u == 0)
    assert own_x == own_y == SUB and max(blocks, tiles[1]) <= LANES
    vmem = pl.BlockSpec(memory_space=pltpu.VMEM)
    smem = pl.BlockSpec(memory_space=pltpu.SMEM)
    hbm = pl.BlockSpec(memory_space=pltpu.HBM)
    result_shape = jax.ShapeDtypeStruct((4 * blocks * SUB, LANES), F32)
    operands = (offset, particle_mass, velocity, affine, deform, particle_cell, body_id)
    operands = operands + (normal_code,)
    faces = [
        pltpu.VMEM(
            (halves * SUB * sum(count for _, count in face_runs(*face, n_x, n_y)), LANES), F32
        )
        for face in FACES
    ]
    dma = pltpu.SemaphoreType.DMA
    result = pl.pallas_call(
        functools.partial(
            nodes_kernel, (n_x, n_y, padded_nodes, halves, tiles, unroll)
        ),
        out_shape=result_shape,
        in_specs=[smem, smem] + [hbm] * 8,
        out_specs=vmem,
        scratch_shapes=[pltpu.VMEM(a.shape, a.dtype) for a in operands]
        + [
            pltpu.VMEM((4 * blocks * SUB, LANES), F32),
            pltpu.VMEM((N_ROWS * blocks, LANES), F32),
            pltpu.VMEM((blocks + 1, SPAN_Z * SUB, LANES), F32),
            pltpu.VMEM(((depth + 2) * SUB, LANES), F32),
            pltpu.VMEM((SUB, LANES), jnp.int32),
            pltpu.SMEM((SUB, LANES), jnp.int32),
            pltpu.VMEM((halves * padded_nodes * SUB, LANES), F32),
            pltpu.VMEM((halves * padded_nodes, LANES), jnp.int32),
            pltpu.VMEM((halves * 6 * LANES, LANES), F32),
            pltpu.VMEM((8, halves * own_y, LANES), jnp.int32),
            pltpu.VMEM((8, halves * own_y, LANES), jnp.int32),
            pltpu.VMEM((tiles[1] + 1, TILE_Z * SUB, LANES), F32),
            pltpu.VMEM((blocks, LANES, 3 * LANES), BF16),
            pltpu.VMEM((blocks, LANES, 3 * LANES), BF16),
        ]
        + faces
        + faces
        + [dma((6,)), dma((6,)), dma((8,)), dma((8,)), dma((8,)), dma(())]
        + [pltpu.VMEM((2, face.shape[0] // 2, LANES), F32) for face in faces[2::2]]
        + [dma((4,))] * 4,
        compiler_params=pltpu.CompilerParams(collective_id=0, has_side_effects=True),
        name="nodes_step",
    )(slot_tile_number, block_count, *operands)
    shapes = [jax.ShapeDtypeStruct((n, blocks, LANES), F32) for n in (3, 9, 9, 6)]
    return pl.pallas_call(
        particle_kernel,
        out_shape=tuple(shapes),
        in_specs=[smem] + [hbm] * 3,
        out_specs=(hbm,) * 4,
        scratch_shapes=[
            pltpu.VMEM(result_shape.shape, F32),
            pltpu.VMEM(deform.shape, F32),
            pltpu.VMEM(body_id.shape, jnp.int32),
        ]
        + [pltpu.VMEM(a.shape, F32) for a in shapes]
        + [dma((3,)), dma((4,))],
        name="particles_step",
    )(block_count, result, deform, body_id)


def solution(mesh):
    particle = P(None, ("gx", "gy"), None)
    flat = P(("gx", "gy"), None)
    placed = (
        particle,
        flat,
        particle,
        particle,
        particle,
        flat,
        flat,
        P(("gx", "gy")),
        P("gx", "gy"),
        P("gx", "gy", None),
    )
    return jax.shard_map(
        per_device,
        mesh=mesh,
        in_specs=placed,
        out_specs=(particle,) * 4,
        check_vma=False,
    )
```

```python
import functools

import jax
import jax.numpy as jnp
from jax import lax
from jax.experimental import pallas as pl
from jax.experimental.pallas import tpu as pltpu
from jax.sharding import PartitionSpec as P

DT = 0.1
MU = 2.0
LAM = 3.0
GRAVITY = -2.0
FLOOR = 0.25
LANES = 128
SUB = 8
TILE_X, TILE_Y, TILE_Z = 4, 4, 8
SPAN_Z = TILE_Z + 2
MESH = pl.DeviceIdType.MESH
F32 = jnp.float32
BF16 = jnp.bfloat16
SIDES = [(-1, 0), (1, 0), (0, -1), (0, 1)]
DIRECTIONS = [(-1, 0), (1, 0), (0, -1), (0, 1), (-1, -1), (-1, 1), (1, -1), (1, 1)]


def spline_weights(fraction):
    return [
        0.5 * (1.5 - fraction) * (1.5 - fraction),
        0.75 - (fraction - 1.0) * (fraction - 1.0),
        0.5 * (fraction - 0.5) * (fraction - 0.5),
    ]


def determinant(m):
    return (
        m[0] * (m[4] * m[8] - m[5] * m[7])
        - m[1] * (m[3] * m[8] - m[5] * m[6])
        + m[2] * (m[3] * m[7] - m[4] * m[6])
    )


def kirchhoff(m):
    ratio = determinant(m)
    pressure = 0.5 * LAM * (ratio * ratio - 1.0)

    def dot(r, c):
        return m[3 * r] * m[3 * c] + m[3 * r + 1] * m[3 * c + 1] + m[3 * r + 2] * m[3 * c + 2]

    return [MU * (dot(r, r) - 1.0) + pressure for r in range(3)] + [
        MU * dot(0, 1),
        MU * dot(0, 2),
        MU * dot(1, 2),
    ]


SYMMETRIC = [0, 3, 4, 3, 1, 5, 4, 5, 2]


def split(value):
    high = value.astype(BF16)
    return high, (value - high.astype(F32)).astype(BF16)


def store_rows(rows_ref, blocks, offset_ref, cell_ref):
    cell = cell_ref[...]
    cells = [cell // (TILE_Y * TILE_Z), cell // TILE_Z % TILE_Y, cell % TILE_Z]
    rows = []
    for axis in range(2):
        fraction = offset_ref[axis]
        weights = spline_weights(fraction)
        rows.append(cells[axis].astype(F32))
        rows.extend(weights)
        rows.extend(weights[step] * (step - fraction) for step in range(3))
    fraction = offset_ref[2]
    weights = spline_weights(fraction)
    moments = [weights[step] * (step - fraction) for step in range(3)]
    for values in (weights, moments):
        for k in range(SPAN_Z):
            total = jnp.zeros_like(fraction)
            for step in range(3):
                total = jnp.where(cells[2] == k - step, values[step], total)
            rows.append(total)
    for index, row in enumerate(rows):
        rows_ref[pl.ds(index * blocks, blocks), :] = row


N_ROWS = 14 + 2 * SPAN_Z


def plane_groups(n_x, n_y):
    groups = [(n_x + x, n_x) for x in range(n_x)]
    groups += [(0, 1), ((n_y - 1) * n_x, 1)]
    corners = [(SUB, 0), (SUB + 1, 0), (SUB, n_y - 1), (SUB + 1, n_y - 1)]
    return groups, [y * n_x + x for x, y in corners]


def axis_weights(rows_ref, blocks, block, axis, corner, coordinates):
    def row(index):
        return rows_ref[pl.ds((7 * axis + index) * blocks + block, 1), :]

    base = row(0) + corner
    weights = [row(1 + s) for s in range(3)]
    moments = [row(4 + s) for s in range(3)]
    out = []
    for coordinate in coordinates:
        step = coordinate - base
        hits = [step == float(s) for s in range(3)]
        for rows in (weights, moments):
            total = jnp.zeros_like(step)
            for s in range(3):
                total = jnp.where(hits[s], rows[s], total)
            out.append(total)
    return out


def plane_weights(rows_ref, blocks, block, tile, tiles, n_x, n_y):
    tiles_y, tiles_z = tiles
    tile_x = (tile // (tiles_y * tiles_z) * TILE_X).astype(F32)
    tile_y = (tile // tiles_z % tiles_y * TILE_Y).astype(F32)
    lines = lax.broadcasted_iota(jnp.int32, (SUB, LANES), 0)
    low_x = lines.astype(F32)
    high_x = (lines % 2 + SUB).astype(F32)
    inner_y = low_x + 1.0
    outer_y = jnp.where(lines % 4 < 2, 0, n_y - 1).astype(F32)
    wx, mx, wx_high, mx_high = axis_weights(
        rows_ref, blocks, block, 0, tile_x, (low_x, high_x)
    )
    wy, my, wy_outer, my_outer = axis_weights(
        rows_ref, blocks, block, 1, tile_y, (inner_y, outer_y)
    )

    def line(low, high, x):
        value = low[x : x + 1] if x < SUB else high[x - SUB : x - SUB + 1]
        return jnp.broadcast_to(value, (SUB, LANES))

    weight_x = [line(wx, wx_high, x) for x in range(n_x)]
    moment_x = [line(mx, mx_high, x) for x in range(n_x)]
    first = [jnp.broadcast_to(v[0:1], (SUB, LANES)) for v in (wy_outer, my_outer)]
    last = [jnp.broadcast_to(v[2:3], (SUB, LANES)) for v in (wy_outer, my_outer)]
    corner = lines < 4
    wx_high = jnp.where(corner, wx_high, 0.0)
    mx_high = jnp.where(corner, mx_high, 0.0)
    pairs = [(weight_x[x], moment_x[x], wy, my) for x in range(n_x)]
    pairs += [(wx, mx, *first), (wx, mx, *last), (wx_high, mx_high, wy_outer, my_outer)]
    pad = [jnp.zeros((LANES - SUB * len(pairs), LANES), F32)]
    return [
        jnp.concatenate([w * v for w, _, v, _ in pairs] + pad, 0),
        jnp.concatenate([m * v for _, m, v, _ in pairs] + pad, 0),
        jnp.concatenate([w * n for w, _, _, n in pairs] + pad, 0),
    ]


def face_runs(kind, side, n_x, n_y):
    if kind == "x":
        first = 0 if side < 0 else n_x - 2
        return [(y * n_x + first, 2) for y in range(n_y)]
    layers = (0, 1) if side < 0 else (n_y - 2, n_y - 1)
    if kind == "inner":
        return [(y * n_x + 2, n_x - 4) for y in layers]
    return [(y * n_x + first, 2) for y in layers for first in (0, n_x - 2)]


FACES = [("x", -1), ("x", 1), ("inner", -1), ("inner", 1), ("outer", -1), ("outer", 1)]


def nodes_kernel(
    shape,
    tile_ref,
    count_ref,
    offset_hbm,
    mass_hbm,
    velocity_hbm,
    affine_hbm,
    deform_hbm,
    cell_hbm,
    body_hbm,
    code_hbm,
    chosen_ref,
    *scratch,
):
    n_x, n_y, padded_nodes, halves, tiles, unroll = shape
    inputs = scratch[:8]
    offset_ref, mass_ref, velocity_ref, affine_ref, deform_ref = inputs[:5]
    cell_ref, body_ref, code_ref = inputs[5:]
    (
        source_ref,
        rows_ref,
        chain_ref,
        grid_ref,
        table_ref,
        links,
        node_ref,
        codes_ref,
        planes_ref,
        send_code,
        recv_code,
        speed_ref,
        high_ref,
        low_ref,
        result_ref,
    ) = scratch[8:23]
    sends = scratch[23:29]
    recvs = scratch[29:35]
    send_sem, recv_sem, code_send_sem, code_recv_sem, in_sem, table_sem = scratch[35:41]
    relays = scratch[41:43]
    relay_send_sem, relay_recv_sem, pass_send_sem, pass_recv_sem = scratch[43:]
    blocks = mass_ref.shape[0]
    size_x, size_y = lax.axis_size("gx"), lax.axis_size("gy")
    me_x, me_y = lax.axis_index("gx"), lax.axis_index("gy")
    own_x, own_y = n_x - 2, n_y - 2

    hbm = (
        offset_hbm,
        mass_hbm,
        velocity_hbm,
        affine_hbm,
        deform_hbm,
        cell_hbm,
        body_hbm,
        code_hbm,
    )
    loads = [
        pltpu.make_async_copy(source, target, in_sem.at[i])
        for i, (source, target) in enumerate(zip(hbm, inputs))
    ]
    for load in loads:
        load.start()

    valid = []
    for dx, dy in DIRECTIONS:
        ok = None
        for d, me, size in ((dx, me_x, size_x), (dy, me_y, size_y)):
            if d == 0:
                continue
            one = me > 0 if d < 0 else me < size - 1
            ok = one if ok is None else jnp.logical_and(ok, one)
        valid.append(ok)
    barrier = pltpu.get_barrier_semaphore()

    def target(index):
        dx, dy = DIRECTIONS[index]
        return {"gx": me_x + dx, "gy": me_y + dy}

    for index in range(8):

        @pl.when(valid[index])
        def _(index=index):
            pl.semaphore_signal(
                barrier, inc=1, device_id=target(index), device_id_type=MESH
            )

    relayed = size_y == 4
    if relayed:
        pl.semaphore_signal(
            barrier,
            inc=1,
            device_id={"gx": me_x, "gy": (me_y + 2) % 4},
            device_id_type=MESH,
        )

    opposite = [DIRECTIONS.index((-dx, -dy)) for dx, dy in DIRECTIONS]
    plane = padded_nodes * SUB

    lane = lax.broadcasted_iota(jnp.int32, (SUB, LANES), 1)
    heights = [tile_ref[s] % tiles[1] for s in range(blocks)]
    height = jnp.full((SUB, LANES), -1, jnp.int32)
    for s in range(blocks):
        height = jnp.where(lane == s, heights[s], height)
    before = jnp.zeros((SUB, LANES), jnp.int32)
    last = jnp.zeros((SUB, LANES), jnp.int32)
    for s in range(blocks):
        before = jnp.where((height == heights[s]) & (lane > s), s + 1, before)
        last = jnp.where(lane == heights[s], s + 1, last)
    sublane = lax.broadcasted_iota(jnp.int32, (SUB, LANES), 0)
    table_ref[...] = jnp.where(sublane == 0, before, last)
    table_copy = pltpu.make_async_copy(table_ref, links, table_sem)
    table_copy.start()

    for load in loads[:7]:
        load.wait()
    slot = lax.broadcasted_iota(jnp.int32, mass_ref.shape, 0)
    mass = jnp.where(slot < count_ref[0, 0], mass_ref[...], 0.0)
    even = body_ref[...] % 2 == 0
    masses = [jnp.where(even, mass, 0.0), jnp.where(even, 0.0, mass)]
    tau = kirchhoff([deform_ref[i] for i in range(9)])
    force = [affine_ref[i] - 4.0 * DT * tau[SYMMETRIC[i]] for i in range(9)]
    zero = jnp.zeros_like(mass)

    def put(group, channel, value):
        source_ref[pl.ds(group * blocks * SUB + channel, blocks, stride=SUB), :] = value

    for field in range(2):
        put(0, 4 * field, masses[field])
        for r in range(3):
            put(0, 4 * field + 1 + r, masses[field] * velocity_ref[r])
        for c in range(3):
            put(1 + c, 4 * field, zero)
            for r in range(3):
                put(1 + c, 4 * field + 1 + r, masses[field] * force[3 * r + c])
    store_rows(rows_ref, blocks, offset_ref, cell_ref)
    span = SPAN_Z * SUB
    chain_ref[0] = jnp.zeros((span, LANES), F32)
    table_copy.wait()

    def block_sums(block):
        tile = tile_ref[block]
        planes = plane_weights(rows_ref, blocks, block, tile, tiles, n_x, n_y)
        groups = [
            source_ref[
                pl.ds(pl.multiple_of(g * blocks * SUB + block * SUB, SUB), SUB), :
            ]
            for g in range(4)
        ]
        left = [[], [], []]
        for k in range(SPAN_Z):
            weight = rows_ref[pl.ds((14 + k) * blocks + block, 1), :]
            moment = rows_ref[pl.ds((14 + SPAN_Z + k) * blocks + block, 1), :]
            left[0].append(groups[0] * weight + groups[3] * moment)
            left[1].append(groups[1] * weight)
            left[2].append(groups[2] * weight)
        left = jnp.concatenate([jnp.concatenate(part, 0) for part in left], 1)
        right = jnp.concatenate(planes, 1)
        left_high, left_low = split(left)
        right_high, right_low = split(right)
        high_ref[block] = right_high
        low_ref[block] = right_low
        product = lax.dot_general(
            jnp.concatenate([left_high, left_low], 0),
            jnp.concatenate([right_high, right_low], 0),
            (((1,), (1,)), ((), ())),
            preferred_element_type=F32,
        )
        return product[:span, :LANES] + (product[:span, LANES:] + product[span:, :LANES])

    def step(index, carry):
        members = [index * unroll + u for u in range(unroll)]
        sums = [block_sums(block) for block in members]
        for block, patch in zip(members, sums):
            chain_ref[block + 1] = chain_ref[links[0, block]] + patch
        return carry

    lax.fori_loop(0, blocks // unroll, step, 0)

    loads[7].wait()
    for half in range(halves):
        lanes = pl.ds(half * LANES, LANES)
        rows = pl.ds(half * own_y, own_y)
        for index, (dx, dy) in enumerate(DIRECTIONS):
            x = 0 if dx < 0 else own_x - 1
            y = 0 if dy < 0 else own_y - 1
            if dy == 0:
                send_code[index, rows, :] = code_ref[x, :, lanes]
            elif dx == 0:
                for i in range(own_x):
                    send_code[index, pl.ds(half * own_y + i, 1), :] = code_ref[
                        i, pl.ds(y, 1), lanes
                    ]
            else:
                send_code[index, rows, :] = jnp.broadcast_to(
                    code_ref[x, pl.ds(y, 1), lanes], (own_y, LANES)
                )

    def code_copy(index):
        return pltpu.make_async_remote_copy(
            src_ref=send_code.at[index],
            dst_ref=recv_code.at[opposite[index]],
            send_sem=code_send_sem.at[index],
            recv_sem=code_recv_sem.at[opposite[index]],
            device_id=target(index),
            device_id_type=MESH,
        )

    def face_copy(face):
        return pltpu.make_async_remote_copy(
            src_ref=sends[face],
            dst_ref=recvs[face ^ 1],
            send_sem=send_sem.at[face],
            recv_sem=recv_sem.at[face ^ 1],
            device_id=target(min(face, 2 + face % 2)),
            device_id_type=MESH,
        )

    def face_valid(face):
        return valid[min(face, 2 + face % 2)]

    def is_relayed(face):
        return me_y == (1 if FACES[face][1] > 0 else 2)

    def is_direct(face):
        if relayed and face >= 2:
            return jnp.logical_and(face_valid(face), jnp.logical_not(is_relayed(face)))
        return face_valid(face)

    def half_rows(ref, half):
        count = ref.shape[0] // 2
        return ref.at[pl.ds(half * count, count)]

    def relay_copy(face, half):
        part, slot = face // 2 - 1, 1 - face % 2
        return pltpu.make_async_remote_copy(
            src_ref=half_rows(sends[face], half),
            dst_ref=relays[part].at[slot],
            send_sem=relay_send_sem.at[2 * part + half],
            recv_sem=relay_recv_sem.at[2 * part + slot],
            device_id={"gx": me_x, "gy": 3 * half},
            device_id_type=MESH,
        )

    def pass_copy(part, slot, half):
        return pltpu.make_async_remote_copy(
            src_ref=relays[part].at[slot],
            dst_ref=half_rows(recvs[2 * part + 2 + slot], half),
            send_sem=pass_send_sem.at[2 * part + slot],
            recv_sem=pass_recv_sem.at[2 * part + half],
            device_id={"gx": me_x, "gy": 2 - slot},
            device_id_type=MESH,
        )

    def pass_on(part):
        for half in range(2):

            @pl.when(me_y == 3 * half)
            def _(half=half):
                for slot in range(2):
                    relay_copy(2 * part + 3 - slot, half).wait_recv()
                    pass_copy(part, slot, half).start()

    arrivals = sum(ok.astype(jnp.int32) for ok in valid) + int(relayed)
    pl.semaphore_wait(barrier, arrivals)
    for index in range(8):

        @pl.when(valid[index])
        def _(index=index):
            code_copy(index).start()

        @pl.when(jnp.logical_not(valid[index]))
        def _(index=index):
            recv_code[index] = jnp.zeros(recv_code.shape[1:], jnp.int32)

    body_rows = TILE_Z * SUB
    over = span - body_rows

    def assemble(j, carry):
        patch = chain_ref[links[1, j]]
        rows = pl.multiple_of(j * body_rows, SUB)
        grid_ref[pl.ds(rows, over), :] = patch[:over] + carry
        grid_ref[pl.ds(rows + over, body_rows - over), :] = patch[over:body_rows]
        return patch[body_rows:]

    tail = lax.fori_loop(0, tiles[1], assemble, jnp.zeros((over, LANES), F32), unroll=4)
    grid_ref[pl.ds(tiles[1] * body_rows, over), :] = tail

    lane_groups, lane_corners = plane_groups(n_x, n_y)
    nodes = n_x * n_y

    for half in range(halves):
        for c in range(SUB):
            part = grid_ref[pl.ds((1 + half * LANES) * SUB + c, LANES, stride=SUB), :]
            part = part.T
            for i, (first, hop) in enumerate(lane_groups):
                node_ref[
                    pl.ds(half * plane + first * SUB + c, SUB, stride=hop * SUB), :
                ] = part[i * SUB : (i + 1) * SUB]
            at = len(lane_groups) * SUB
            for i, first in enumerate(lane_corners):
                node_ref[pl.ds(half * plane + first * SUB + c, 1), :] = part[
                    at + i : at + i + 1
                ]
            node_ref[
                pl.ds(half * plane + nodes * SUB + c, padded_nodes - nodes, stride=SUB), :
            ] = jnp.zeros((padded_nodes - nodes, LANES), F32)

    def each_run(face):
        offset = 0
        for half in range(halves):
            for first, count in face_runs(*FACES[face], n_x, n_y):
                yield (
                    pl.ds(half * plane + first * SUB, count * SUB),
                    pl.ds(offset, count * SUB),
                )
                offset += count * SUB

    def send_far(face):
        for rows, run in each_run(face):
            sends[face][run, :] = node_ref[rows, :]
        if relayed:

            @pl.when(is_relayed(face))
            def _():
                for half in range(2):
                    relay_copy(face, half).start()

    def send_face(face):
        if face < 2:
            for rows, run in each_run(face):
                sends[face][run, :] = node_ref[rows, :]

        @pl.when(is_direct(face))
        def _():
            face_copy(face).start()

        @pl.when(jnp.logical_not(face_valid(face)))
        def _():
            recvs[face][...] = jnp.zeros_like(recvs[face])

    def take_face(face):
        @pl.when(is_direct(face))
        def _():
            face_copy(face ^ 1).wait_recv()

        if relayed and face >= 2:

            @pl.when(is_relayed(face))
            def _():
                for half in range(2):
                    pass_copy(face // 2 - 1, face % 2, half).wait_recv()

        for rows, run in each_run(face):
            node_ref[rows, :] = node_ref[rows, :] + recvs[face][run, :]

    send_far(2)
    send_far(3)
    for face in (2, 3, 0, 1):
        send_face(face)

    codes_ref[...] = jnp.zeros_like(codes_ref)
    for half in range(halves):
        lanes = pl.ds(half * LANES, LANES)
        for x in range(own_x):
            codes_ref[
                pl.ds(half * padded_nodes + n_x + x + 1, own_y, stride=n_x), :
            ] = code_ref[x, :, lanes]
    for index, (dx, dy) in enumerate(DIRECTIONS):

        @pl.when(valid[index])
        def _(index=index):
            code_copy(opposite[index]).wait_recv()

        x = 0 if dx < 0 else n_x - 1
        y = 0 if dy < 0 else n_y - 1
        for half in range(halves):
            base = half * padded_nodes
            rows = pl.ds(half * own_y, own_y)
            if dy == 0:
                codes_ref[pl.ds(base + n_x + x, own_y, stride=n_x), :] = recv_code[
                    index, rows, :
                ]
            elif dx == 0:
                codes_ref[pl.ds(base + y * n_x + 1, own_x), :] = recv_code[
                    index, pl.ds(half * own_y, own_x), :
                ]
            else:
                codes_ref[pl.ds(base + y * n_x + x, 1), :] = recv_code[
                    index, pl.ds(half * own_y, 1), :
                ]

    if relayed:
        pass_on(0)
    take_face(0)
    take_face(1)
    send_far(4)
    send_far(5)
    send_face(4)
    send_face(5)

    groups = padded_nodes // SUB

    def update(half, group):
        base = half * plane + group * (SUB * SUB)
        channels = [
            node_ref[pl.ds(base + c, SUB, stride=SUB), :] for c in range(SUB)
        ]
        row = half * padded_nodes + group * SUB
        code = codes_ref[pl.ds(pl.multiple_of(row, SUB), SUB), :]
        shifted = jnp.where(code >= 13, code + 1, code).astype(F32)
        nines = jnp.floor(shifted * (1.0 / 9.0) + 0.01)
        rest = shifted - 9.0 * nines
        threes = jnp.floor(rest * (1.0 / 3.0) + 0.01)
        normal = [nines - 1.0, threes - 1.0, rest - 3.0 * threes - 1.0]
        scale = lax.rsqrt(
            normal[0] * normal[0] + normal[1] * normal[1] + normal[2] * normal[2]
        )
        normal = [n * scale for n in normal]
        masses = [channels[0], channels[4]]
        momenta = [channels[1:4], channels[5:8]]
        gravity = [0.0, 0.0, DT * GRAVITY]
        inverse = [1.0 / jnp.maximum(masses[f], FLOOR) for f in range(2)]
        speeds = [
            [p * inverse[f] + gravity[r] for r, p in enumerate(momenta[f])]
            for f in range(2)
        ]
        both = 1.0 / jnp.maximum(masses[0] + masses[1], FLOOR)
        center = [
            (momenta[0][r] + momenta[1][r]) * both + gravity[r] for r in range(3)
        ]
        share = jnp.minimum(1.0, jnp.minimum(masses[0], masses[1]) * (1.0 / FLOOR))
        closing = [
            share
            * jnp.maximum(
                sum((speeds[0][r] - center[r]) * normal[r] for r in range(3)), 0.0
            ),
            share
            * jnp.maximum(
                sum((center[r] - speeds[1][r]) * normal[r] for r in range(3)), 0.0
            ),
        ]
        node = group * SUB + lax.broadcasted_iota(jnp.int32, (SUB, LANES), 0)
        layer = jnp.floor((node.astype(F32) + 0.5) * (1.0 / n_x)).astype(jnp.int32)
        x = me_x * own_x + node - layer * n_x
        y = me_y * own_y + layer
        inside = (x >= 1) & (x <= size_x * own_x) & (y >= 1) & (y <= size_y * own_y)
        for f, sign in ((0, -1.0), (1, 1.0)):
            for r in range(3):
                speed = speeds[f][r] + sign * closing[f] * normal[r]
                at = (half * 6 + 3 * f + r) * LANES + pl.multiple_of(group * SUB, SUB)
                planes_ref[pl.ds(at, SUB), :] = jnp.where(inside, speed, 0.0)

    def update_groups(first, count):
        def body(step, carry):
            update(step // count, first + step % count)
            return carry

        lax.fori_loop(0, halves * count, body, 0)

    early = -(-2 * n_x // SUB)
    late = (n_y - 2) * n_x // SUB
    update_groups(early, late - early)
    if relayed:
        pass_on(1)
    for face in (2, 3, 4, 5):
        take_face(face)
    update_groups(0, early)
    update_groups(late, groups - late)
    edge = jnp.zeros((SUB, LANES), F32)
    depth = halves * LANES
    grid_ref[pl.ds(0, SUB), :] = edge
    grid_ref[pl.ds((depth + 1) * SUB, SUB), :] = edge
    for half in range(halves):
        for c in range(6):
            channel = c // 3 * 4 + c % 3
            at = (half * 6 + c) * LANES
            part = [
                planes_ref[pl.ds(at + first, SUB, stride=hop), :]
                for first, hop in lane_groups
            ]
            part += [planes_ref[pl.ds(at + first, 1), :] for first in lane_corners]
            rest = LANES - len(lane_groups) * SUB - len(lane_corners)
            part.append(jnp.zeros((rest, LANES), F32))
            grid_ref[
                pl.ds((1 + half * LANES) * SUB + channel, LANES, stride=SUB), :
            ] = jnp.concatenate(part, 0).T
    for j in range(tiles[1]):
        speed_ref[j] = grid_ref[pl.ds(j * body_rows, body_rows), :]
    speed_ref[tiles[1], pl.ds(0, over), :] = grid_ref[pl.ds(tiles[1] * body_rows, over), :]

    def block_speeds(block):
        at = tile_ref[block] % tiles[1]
        speeds = jnp.concatenate([speed_ref[at], speed_ref[at + 1][:over]], 0)
        left_high, left_low = split(speeds)
        right_high, right_low = high_ref[block], low_ref[block]
        product = jnp.dot(
            jnp.concatenate([left_high, left_low, left_high], 1),
            jnp.concatenate([right_high, right_high, right_low], 0),
            preferred_element_type=F32,
        )
        sums = [jnp.zeros((SUB, LANES), F32) for _ in range(4)]
        for k in range(SPAN_Z):
            weight = rows_ref[pl.ds((14 + k) * blocks + block, 1), :]
            moment = rows_ref[pl.ds((14 + SPAN_Z + k) * blocks + block, 1), :]
            rows = [product[k * SUB : (k + 1) * SUB, v * LANES : (v + 1) * LANES] for v in range(3)]
            sums[0] = sums[0] + rows[0] * weight
            sums[1] = sums[1] + rows[1] * weight
            sums[2] = sums[2] + rows[2] * weight
            sums[3] = sums[3] + rows[0] * moment
        return sums

    def gather_step(index, carry):
        members = [index * unroll + u for u in range(unroll)]
        results = [block_speeds(block) for block in members]
        for block, sums in zip(members, results):
            for v in range(4):
                start = pl.multiple_of(v * blocks * SUB + block * SUB, SUB)
                result_ref[pl.ds(start, SUB), :] = sums[v]
        return carry

    lax.fori_loop(0, blocks // unroll, gather_step, 0)
    live = slot < count_ref[0, 0]
    even = body_ref[...] % 2 == 0
    for v in range(4):
        for r in range(3):
            fields = [
                result_ref[pl.ds(v * blocks * SUB + 4 * f + r, blocks, stride=SUB), :]
                for f in range(2)
            ]
            value = jnp.where(live, jnp.where(even, fields[0], fields[1]), 0.0)
            chosen_ref[3 * v + r] = value if v == 0 else 4.0 * value

    for index in range(8):

        @pl.when(valid[index])
        def _(index=index):
            code_copy(index).wait_send()

    for face in range(6):

        @pl.when(is_direct(face))
        def _(face=face):
            face_copy(face).wait_send()

        if relayed and face >= 2:

            @pl.when(is_relayed(face))
            def _(face=face):
                for half in range(2):
                    relay_copy(face, half).wait_send()

    if relayed:
        for half in range(2):

            @pl.when(me_y == 3 * half)
            def _(half=half):
                for part in range(2):
                    for slot in range(2):
                        pass_copy(part, slot, half).wait_send()


def particle_kernel(
    count_ref,
    result_hbm,
    deform_hbm,
    new_velocity_hbm,
    new_affine_hbm,
    new_deform_hbm,
    new_stress_hbm,
    result_ref,
    deform_ref,
    new_velocity_ref,
    new_affine_ref,
    new_deform_ref,
    new_stress_ref,
    in_sem,
    out_sem,
):
    pairs = ((result_hbm, result_ref), (deform_hbm, deform_ref))
    loads = [
        pltpu.make_async_copy(source, target, in_sem.at[i])
        for i, (source, target) in enumerate(pairs)
    ]
    for load in loads:
        load.start()
    pairs = (
        (new_velocity_ref, new_velocity_hbm),
        (new_affine_ref, new_affine_hbm),
        (new_deform_ref, new_deform_hbm),
        (new_stress_ref, new_stress_hbm),
    )
    stores = [
        pltpu.make_async_copy(source, target, out_sem.at[i])
        for i, (source, target) in enumerate(pairs)
    ]
    for load in loads:
        load.wait()
    slot = lax.broadcasted_iota(jnp.int32, result_ref.shape[1:], 0)
    live = slot < count_ref[0, 0]
    for r in range(3):
        new_velocity_ref[r] = result_ref[r]
    stores[0].start()
    affine = [result_ref[3 + 3 * c + r] for r in range(3) for c in range(3)]
    deform = [deform_ref[i] for i in range(9)]
    moved = []
    for r in range(3):
        for c in range(3):
            entry = deform[3 * r + c]
            for i in range(3):
                entry = entry + DT * affine[3 * r + i] * deform[3 * i + c]
            moved.append(jnp.where(live, entry, 0.0))
    for i in range(9):
        new_affine_ref[i] = affine[i]
    stores[1].start()
    for i in range(9):
        new_deform_ref[i] = moved[i]
    stores[2].start()
    for i, entry in enumerate(kirchhoff(moved)):
        new_stress_ref[i] = jnp.where(live, entry, 0.0)
    stores[3].start()
    for store in stores:
        store.wait()


def per_device(
    offset,
    particle_mass,
    velocity,
    affine,
    deform,
    particle_cell,
    body_id,
    slot_tile_number,
    block_count,
    normal_code,
):
    blocks, particles = particle_mass.shape
    own_x, own_y, depth = normal_code.shape
    tiles = (own_y // TILE_Y, depth // TILE_Z)
    n_x, n_y = own_x + 2, own_y + 2
    padded_nodes = -(-n_x * n_y // SUB) * SUB
    halves = depth // LANES
    assert particles == LANES and padded_nodes <= LANES and depth % LANES == 0
    unroll = next(u for u in (24, 8, 4, 2, 1) if blocks % u == 0)
    assert own_x == own_y == SUB and max(blocks, tiles[1]) <= LANES
    vmem = pl.BlockSpec(memory_space=pltpu.VMEM)
    smem = pl.BlockSpec(memory_space=pltpu.SMEM)
    hbm = pl.BlockSpec(memory_space=pltpu.HBM)
    result_shape = jax.ShapeDtypeStruct((12, blocks, LANES), F32)
    operands = (offset, particle_mass, velocity, affine, deform, particle_cell, body_id)
    operands = operands + (normal_code,)
    faces = [
        pltpu.VMEM(
            (halves * SUB * sum(count for _, count in face_runs(*face, n_x, n_y)), LANES), F32
        )
        for face in FACES
    ]
    dma = pltpu.SemaphoreType.DMA
    result = pl.pallas_call(
        functools.partial(
            nodes_kernel, (n_x, n_y, padded_nodes, halves, tiles, unroll)
        ),
        out_shape=result_shape,
        in_specs=[smem, smem] + [hbm] * 8,
        out_specs=vmem,
        scratch_shapes=[pltpu.VMEM(a.shape, a.dtype) for a in operands]
        + [
            pltpu.VMEM((4 * blocks * SUB, LANES), F32),
            pltpu.VMEM((N_ROWS * blocks, LANES), F32),
            pltpu.VMEM((blocks + 1, SPAN_Z * SUB, LANES), F32),
            pltpu.VMEM(((depth + 2) * SUB, LANES), F32),
            pltpu.VMEM((SUB, LANES), jnp.int32),
            pltpu.SMEM((SUB, LANES), jnp.int32),
            pltpu.VMEM((halves * padded_nodes * SUB, LANES), F32),
            pltpu.VMEM((halves * padded_nodes, LANES), jnp.int32),
            pltpu.VMEM((halves * 6 * LANES, LANES), F32),
            pltpu.VMEM((8, halves * own_y, LANES), jnp.int32),
            pltpu.VMEM((8, halves * own_y, LANES), jnp.int32),
            pltpu.VMEM((tiles[1] + 1, TILE_Z * SUB, LANES), F32),
            pltpu.VMEM((blocks, LANES, 3 * LANES), BF16),
            pltpu.VMEM((blocks, LANES, 3 * LANES), BF16),
            pltpu.VMEM((4 * blocks * SUB, LANES), F32),
        ]
        + faces
        + faces
        + [dma((6,)), dma((6,)), dma((8,)), dma((8,)), dma((8,)), dma(())]
        + [pltpu.VMEM((2, face.shape[0] // 2, LANES), F32) for face in faces[2::2]]
        + [dma((4,))] * 4,
        compiler_params=pltpu.CompilerParams(collective_id=0, has_side_effects=True),
        name="nodes_step",
    )(slot_tile_number, block_count, *operands)
    shapes = [jax.ShapeDtypeStruct((n, blocks, LANES), F32) for n in (3, 9, 9, 6)]
    return pl.pallas_call(
        particle_kernel,
        out_shape=tuple(shapes),
        in_specs=[smem] + [hbm] * 2,
        out_specs=(hbm,) * 4,
        scratch_shapes=[
            pltpu.VMEM(result_shape.shape, F32),
            pltpu.VMEM(deform.shape, F32),
        ]
        + [pltpu.VMEM(a.shape, F32) for a in shapes]
        + [dma((2,)), dma((4,))],
        name="particles_step",
    )(block_count, result, deform)


def solution(mesh):
    particle = P(None, ("gx", "gy"), None)
    flat = P(("gx", "gy"), None)
    placed = (
        particle,
        flat,
        particle,
        particle,
        particle,
        flat,
        flat,
        P(("gx", "gy")),
        P("gx", "gy"),
        P("gx", "gy", None),
    )
    return jax.shard_map(
        per_device,
        mesh=mesh,
        in_specs=placed,
        out_specs=(particle,) * 4,
        check_vma=False,
    )
```
